256 devices in a mesh: seq: 32 (over z, y_hi, core), dp: 8 (over x, y_lo).
Axes of the slice: x: 4, y: 4 (y_hi: 2, y_lo: 2; y = y_hi * 2 + y_lo), z: 8, core: 2. Of those that a mesh axis runs over, the one named last changes fastest.
Arguments:
- video: bfloat16 [8, 32, 256, 1152], P('dp', 'seq'), may hold values from -6 to 6
- spatial_in: bfloat16 [1152, 1728], replicated, may hold values from -0.1875 to 0.1875
- spatial_out: bfloat16 [576, 1152], replicated, may hold values from -1 to 1
- temporal_in: bfloat16 [1152, 1728], replicated, may hold values from -0.1875 to 0.1875
- temporal_out: bfloat16 [576, 1152], replicated, may hold values from -1 to 1
- cotangent: bfloat16 [8, 32, 256, 1152], P('dp', 'seq'), may hold values from -6 to 6
Outputs:
- blocks_out: bfloat16 [8, 32, 256, 1152], P('dp', 'seq')
- grad_video: bfloat16 [8, 32, 256, 1152], P('dp', 'seq')
- grad_in: float32 [1152, 1728], P('seq', 'dp')
- grad_out: float32 [576, 1152], P('seq', 'dp')
The draws below stay inside these ranges and needn't reach their ends.
All inputs are finite; a program needn't handle non-finite values.
Results may differ from the reference program's by a relative error of at most 0.034.
Values may be sent and summed in bfloat16 or wider, within the bound.
A program may use at most 128 MiB of HBM per device.

```python
import jax
import jax.numpy as jnp
from jax import lax

D = 1152
HEADS = 8
HEAD = 72
S = 256
HD = 576
F = 32
VIDEOS = 8


def block_scale(stream_key, extent, split, least, largest):
    def one(axis_at, shards_of):
        heights = jax.random.uniform(jax.random.fold_in(jax.random.fold_in(stream_key, 6), axis_at), (shards_of,), jnp.float32, least / len(split), largest / len(split))
        return jnp.repeat(jnp.exp(heights), extent[axis_at] // shards_of).reshape((-1,) + (1,) * (len(extent) - axis_at - 1))

    loudness = one(*split[0])
    for cut in split[1:]:
        loudness = loudness * one(*cut)
    return loudness


def scatter_about(key, extent, width, limit, pieces=(), dtype=jnp.bfloat16):
    array = width * jax.random.normal(key, extent, jnp.float32)
    if pieces:
        array = array * block_scale(key, extent, pieces, -0.22, 0.18)
    return jnp.clip(array, -limit, limit).astype(dtype)


def setup_inputs(seed: int = 0) -> dict:
    key_list = jax.random.split(jax.random.key(seed), 7)
    video = scatter_about(key_list[0], (VIDEOS, F, S, D), 1.0, 6.0, ((0, 8), (1, 32)))
    spatial_in = scatter_about(key_list[1], (D, 3 * HD), D ** -0.5, 0.1875)
    spatial_out = scatter_about(key_list[2], (HD, D), (HD // 16) ** -0.5, 1.0)
    temporal_in = scatter_about(key_list[3], (D, 3 * HD), D ** -0.5, 0.1875)
    temporal_out = scatter_about(key_list[4], (HD, D), (HD // 16) ** -0.5, 1.0)
    cotangent = scatter_about(key_list[5], (VIDEOS, F, S, D), 1.0, 6.0, ((0, 8), (1, 32)))
    return dict(video=video, spatial_in=spatial_in, spatial_out=spatial_out, temporal_in=temporal_in, temporal_out=temporal_out, cotangent=cotangent)


def norm_forward(inputs):
    center = inputs - lax.optimization_barrier(jnp.mean(inputs, -1, keepdims=True))
    inverse = lax.rsqrt(lax.optimization_barrier(jnp.mean(center * center, -1, keepdims=True)) + 1e-06)
    return (center * inverse, inverse)

def norm_backward(normed, inverse, incoming):
    return inverse * (incoming - lax.optimization_barrier(jnp.mean(incoming, -1, keepdims=True)) - normed * lax.optimization_barrier(jnp.mean(incoming * normed, -1, keepdims=True)))

def attend(queries, key_rows, val_rows, factor):
    scores = jnp.einsum('glhd,gmhd->ghlm', queries.astype(jnp.float32), key_rows.astype(jnp.float32)) * factor
    exponent = jnp.exp(scores)
    shares = exponent / lax.optimization_barrier(jnp.sum(exponent, -1, keepdims=True))
    weights = shares.astype(jnp.bfloat16)
    attended = jnp.einsum('ghlm,gmhd->glhd', weights.astype(jnp.float32), val_rows.astype(jnp.float32)).astype(jnp.bfloat16)
    return (attended, shares, weights)

def attend_back(queries, key_rows, val_rows, shares, weights, incoming, factor):
    grad_val = jnp.einsum('ghlm,glhd->gmhd', weights.astype(jnp.float32), incoming.astype(jnp.float32)).astype(jnp.bfloat16)
    grad_weights = jnp.einsum('glhd,gmhd->ghlm', incoming.astype(jnp.float32), val_rows.astype(jnp.float32))
    grad_score = shares * (grad_weights - lax.optimization_barrier(jnp.sum(grad_weights * shares, -1, keepdims=True))) * factor
    grad_query = jnp.einsum('ghlm,gmhd->glhd', grad_score, key_rows.astype(jnp.float32), precision=lax.Precision.HIGHEST).astype(jnp.bfloat16)
    grad_key = jnp.einsum('ghlm,glhd->gmhd', grad_score, queries.astype(jnp.float32), precision=lax.Precision.HIGHEST).astype(jnp.bfloat16)
    return (grad_query, grad_key, grad_val)

def one_video(video_one, cotangent_one, spatial_in, spatial_out, temporal_in, temporal_out):
    factor = HEAD ** (-0.5)
    count_rows = F * S
    video_wide = video_one.astype(jnp.float32)
    spatial_normed, spatial_inverse = norm_forward(video_wide)
    spatial_h = spatial_normed.astype(jnp.bfloat16).reshape(count_rows, D)
    spatial_qkv = jnp.dot(spatial_h, spatial_in, preferred_element_type=jnp.float32).astype(jnp.bfloat16).reshape(F, S, 3, HEADS, HEAD)
    spatial_att, spatial_shares, spatial_weights = attend(spatial_qkv[:, :, 0], spatial_qkv[:, :, 1], spatial_qkv[:, :, 2], factor)
    residual = (video_wide + jnp.dot(spatial_att.reshape(count_rows, HD), spatial_out, preferred_element_type=jnp.float32).reshape(F, S, D)).astype(jnp.bfloat16)
    temporal_normed, temporal_inverse = norm_forward(residual.astype(jnp.float32))
    temporal_h = temporal_normed.astype(jnp.bfloat16).reshape(count_rows, D)
    temporal_qkv = jnp.dot(temporal_h, temporal_in, preferred_element_type=jnp.float32).astype(jnp.bfloat16).reshape(F, S, 3, HEADS, HEAD)
    swapped = jnp.swapaxes(temporal_qkv, 0, 1)
    temporal_att, temporal_shares, temporal_weights = attend(swapped[:, :, 0], swapped[:, :, 1], swapped[:, :, 2], factor)
    frame_rows = jnp.swapaxes(temporal_att, 0, 1).reshape(count_rows, HD)
    blocks_out = (residual.astype(jnp.float32) + jnp.dot(frame_rows, temporal_out, preferred_element_type=jnp.float32).reshape(F, S, D)).astype(jnp.bfloat16)
    incoming = cotangent_one.reshape(count_rows, D)
    grad_out = jnp.dot(frame_rows.T, incoming, preferred_element_type=jnp.float32)
    grad_frames = jnp.dot(incoming, temporal_out.T, preferred_element_type=jnp.float32).astype(jnp.bfloat16).reshape(F, S, HEADS, HEAD)
    grad_att = jnp.swapaxes(grad_frames, 0, 1)
    temporal_grads = attend_back(swapped[:, :, 0], swapped[:, :, 1], swapped[:, :, 2], temporal_shares, temporal_weights, grad_att, factor)
    grad_qkv = jnp.swapaxes(jnp.stack(temporal_grads, 2), 0, 1).reshape(count_rows, 3 * HD)
    grad_in = jnp.dot(temporal_h.T, grad_qkv, preferred_element_type=jnp.float32)
    grad_norm_t = jnp.dot(grad_qkv, temporal_in.T, preferred_element_type=jnp.float32).reshape(F, S, D)
    grad_residual = (cotangent_one.astype(jnp.float32) + norm_backward(temporal_normed, temporal_inverse, grad_norm_t)).astype(jnp.bfloat16)
    grad_spatial = jnp.dot(grad_residual.reshape(count_rows, D), spatial_out.T, preferred_element_type=jnp.float32).astype(jnp.bfloat16).reshape(F, S, HEADS, HEAD)
    spatial_grads = attend_back(spatial_qkv[:, :, 0], spatial_qkv[:, :, 1], spatial_qkv[:, :, 2], spatial_shares, spatial_weights, grad_spatial, factor)
    grad_sqkv = jnp.stack(spatial_grads, 2).reshape(count_rows, 3 * HD)
    grad_norm_s = jnp.dot(grad_sqkv, spatial_in.T, preferred_element_type=jnp.float32).reshape(F, S, D)
    grad_video = (grad_residual.astype(jnp.float32) + norm_backward(spatial_normed, spatial_inverse, grad_norm_s)).astype(jnp.bfloat16)
    return (blocks_out, grad_video, grad_in, grad_out)

def reference(video, spatial_in, spatial_out, temporal_in, temporal_out, cotangent):

    def per_video(pair):
        return one_video(pair[0], pair[1], spatial_in, spatial_out, temporal_in, temporal_out)
    blocks_out, grad_video, grad_in, grad_out = lax.map(per_video, (video, cotangent))
    return (blocks_out, grad_video, lax.optimization_barrier(jnp.sum(grad_in, 0)), lax.optimization_barrier(jnp.sum(grad_out, 0)))
```

```python
import jax
import jax.numpy as jnp
from jax import lax
from jax.sharding import PartitionSpec as P

HEADS = 8
HEAD = 72
F32 = jnp.float32
BF16 = jnp.bfloat16


def norm_forward(inputs):
    center = inputs - jnp.mean(inputs, -1, keepdims=True)
    inverse = lax.rsqrt(jnp.mean(center * center, -1, keepdims=True) + 1e-06)
    return (center * inverse, inverse)


def norm_backward(normed, inverse, incoming):
    return inverse * (
        incoming
        - jnp.mean(incoming, -1, keepdims=True)
        - normed * jnp.mean(incoming * normed, -1, keepdims=True)
    )


def dot(a, b):
    return jnp.dot(a, b, preferred_element_type=F32)


def dot_t(a, b):
    return lax.dot_general(a, b, (((1,), (1,)), ((), ())), preferred_element_type=F32)


def t_dot(a, b):
    return lax.dot_general(a, b, (((0,), (0,)), ((), ())), preferred_element_type=F32)


def forward_heads(qkv, mask, factor):
    rows = qkv.shape[0]
    q, k, v = [t.reshape(rows, HEADS, HEAD) for t in jnp.split(qkv, 3, axis=1)]
    scores = jnp.einsum("lhd,mhd->hlm", q, k, preferred_element_type=F32) * factor
    exponent = jnp.exp(scores)
    if mask is not None:
        exponent = jnp.where(mask, exponent, 0.0)
    shares = exponent / jnp.sum(exponent, -1, keepdims=True)
    weights = shares.astype(BF16)
    att = jnp.einsum("hlm,mhd->lhd", weights, v, preferred_element_type=F32).astype(BF16)
    return att.reshape(rows, HEADS * HEAD), shares, weights


def backward_heads(qkv, shares, weights, incoming, factor):
    rows = qkv.shape[0]
    q, k, v = [t.reshape(rows, HEADS, HEAD) for t in jnp.split(qkv, 3, axis=1)]
    g = incoming.reshape(rows, HEADS, HEAD)
    gv = jnp.einsum("hlm,lhd->mhd", weights, g, preferred_element_type=F32)
    e = jnp.einsum("lhd,mhd->hlm", g, v, preferred_element_type=F32)
    r = shares * (e - jnp.sum(e * shares, -1, keepdims=True)) * factor
    r = r.astype(BF16)
    gq = jnp.einsum("hlm,mhd->lhd", r, k, preferred_element_type=F32)
    gk = jnp.einsum("hlm,lhd->mhd", r, q, preferred_element_type=F32)
    return jnp.stack([gq.astype(BF16), gk.astype(BF16), gv.astype(BF16)], 1).reshape(rows, -1)


def scatter_sum(grad, groups_seq):
    rows, cols = grad.shape
    n_dp = lax.axis_size("dp")
    n_seq = lax.axis_size("seq")
    pairs = [(2 * i, 2 * i + 1) for i in range(n_seq // 2)]
    same = [tuple(range(c, n_seq, 2)) for c in range(2)]
    piece_r, piece_c = rows // n_seq, cols // n_dp
    x = grad.astype(BF16).reshape(n_seq // 2, 2, piece_r, cols)
    x = jnp.swapaxes(x, 0, 1)
    x = lax.all_to_all(x, "seq", 0, 0, axis_index_groups=pairs, tiled=True)
    x = jnp.sum(x.astype(F32), 0).astype(BF16)
    x = x.reshape(n_seq // 2 * piece_r, n_dp, piece_c)
    x = jnp.swapaxes(x, 0, 1)
    x = lax.all_to_all(x, "dp", 0, 0, tiled=True)
    x = jnp.sum(x.astype(F32), 0).astype(BF16)
    x = x.reshape(n_seq // 2, piece_r, piece_c)
    x = lax.all_to_all(x, "seq", 0, 0, axis_index_groups=same, tiled=True)
    return jnp.sum(x.astype(F32), 0)


def local(video, spatial_in, spatial_out, temporal_in, temporal_out, cotangent):
    width = video.shape[-1]
    places = video.shape[2]
    rows = places
    groups = lax.axis_size("seq")
    spread = places // groups
    factor = HEAD ** (-0.5)
    cot = cotangent.reshape(rows, width)
    vid = video.reshape(rows, width).astype(F32)

    def swap(x):
        y = lax.all_to_all(x.reshape(groups, spread, x.shape[-1]), "seq", 0, 0, tiled=True)
        return y.reshape(rows, x.shape[-1])

    grad_att = swap(dot_t(cot, temporal_out).astype(BF16))
    s_norm, s_inv = norm_forward(vid)
    s_qkv = dot(s_norm.astype(BF16), spatial_in).astype(BF16)
    s_att, s_shares, s_weights = forward_heads(s_qkv, None, factor)
    residual = (vid + dot(s_att, spatial_out)).astype(BF16)
    t_norm, t_inv = norm_forward(residual.astype(F32))
    h = swap(t_norm.astype(BF16))
    qkv = dot(h, temporal_in).astype(BF16)
    place = lax.broadcasted_iota(jnp.int32, (rows, rows), 0) % spread
    other = lax.broadcasted_iota(jnp.int32, (rows, rows), 1) % spread
    mask = (place == other)[None]
    att, shares, weights = forward_heads(qkv, mask, factor)
    frame_att = swap(att)
    g_qkv = backward_heads(qkv, shares, weights, grad_att, factor)
    grad_in = scatter_sum(t_dot(h, g_qkv), groups)
    g_h = swap(dot_t(g_qkv, temporal_in).astype(BF16)).astype(F32)
    grad_out = scatter_sum(t_dot(frame_att, cot), groups)
    blocks_out = (residual.astype(F32) + dot(frame_att, temporal_out)).astype(BF16)
    grad_res = (cot.astype(F32) + norm_backward(t_norm, t_inv, g_h)).astype(BF16)
    g_spatial = dot_t(grad_res, spatial_out).astype(BF16)
    g_sqkv = backward_heads(s_qkv, s_shares, s_weights, g_spatial, factor)
    g_sh = dot_t(g_sqkv, spatial_in)
    grad_video = (grad_res.astype(F32) + norm_backward(s_norm, s_inv, g_sh)).astype(BF16)
    return (blocks_out.reshape(video.shape), grad_video.reshape(video.shape), grad_in, grad_out)


def solution(mesh):
    in_specs = (P("dp", "seq", None, None), P(), P(), P(), P(), P("dp", "seq", None, None))
    out_specs = (
        P("dp", "seq", None, None),
        P("dp", "seq", None, None),
        P("seq", "dp"),
        P("seq", "dp"),
    )
    return jax.shard_map(local, mesh=mesh, in_specs=in_specs, out_specs=out_specs, check_vma=False)
```

```python
import jax
import jax.numpy as jnp
from jax import lax
from jax.experimental import pallas as pl
from jax.experimental.pallas import tpu as pltpu
from jax.sharding import PartitionSpec as P

HEADS = 8
HEAD = 72
D = 1152
HD = 576
N = 256
PAD = 640
FACTOR = HEAD ** (-0.5)
F32 = jnp.float32
BF16 = jnp.bfloat16
MESH = pl.DeviceIdType.MESH
CHUNK = 32
ROWS = 216
ZROWS = 64


def dot(a, b):
    return jnp.dot(a, b, preferred_element_type=F32)


def dot_nt(a, b):
    return lax.dot_general(a, b, (((1,), (1,)), ((), ())), preferred_element_type=F32)


def dot_tn(a, b):
    return lax.dot_general(a, b, (((0,), (0,)), ((), ())), preferred_element_type=F32)


def window(head):
    start = head * HEAD
    low = start // 128 * 128
    wide = 128 if start + HEAD <= low + 128 else 256
    return start - low, slice(low, low + wide), wide


def head_mask(offset, wide):
    lane = lax.broadcasted_iota(jnp.int32, (N, wide), 1)
    return (lane >= offset) & (lane < offset + HEAD)


def scratch_shapes():
    slab = (2, ROWS, 128)
    vm = lambda *shape: pltpu.VMEM(shape, BF16)
    vf = lambda *shape: pltpu.VMEM(shape, F32)
    dma = pltpu.SemaphoreType.DMA
    return dict(
        vid=vm(N, D), cot=vm(N, D), wsi=vm(D, 3 * HD), wso=vm(HD, D), wti=vm(D, 3 * HD), wto=vm(HD, D),
        ga_send=vm(32, 8, HD), ga_recv=vm(32, 8, HD), h_send=vm(32, 8, D), h_recv=vm(32, 8, D),
        at_send=vm(32, 8, HD), at_recv=vm(32, 8, HD), gh_send=vm(32, 8, D), gh_recv=vm(32, 8, D),
        sh=vm(N, D), sq=vm(N, PAD), sk=vm(N, PAD), sv=vm(N, PAD), sw=vm(HEADS, N, N),
        th=vm(N, D), tq=vm(N, PAD), tk=vm(N, PAD), tv=vm(N, PAD), tw=vm(HEADS, N, N),
        acc=vf(N, PAD), accq=vf(N, PAD), acck=vf(N, PAD), accv=vf(N, PAD),
        small=vm(N, PAD), nat=vm(N, 1792), big=vf(N, D),
        res=vm(N, D), s_mean=vf(N, 128), s_inv=vf(N, 128), t_mean=vf(N, 128), t_inv=vf(N, 128),
        turn=vf(D, N), h_t=vm(D, N), att_t=vm(HD, N),
        gpad=vm(8, N, 256), cpad=vm(8, N, 256),
        part=vm(2, 2, 4, 4, *slab), c_recv=vm(2, 4, 4, *slab),
        one_recv=vm(2, 2, 2, *slab), two_recv=vm(2, 2, 4, *slab),
        mid=vm(2, 4, *slab), three_recv=vm(2, 2, ROWS, 128), four_recv=vm(2, 2, *slab),
        zsum=vf(2, *slab), z_send=vm(8, 2, ZROWS, 128), z_recv=vm(8, 2, ZROWS, 128),
        load=dma((6,)), a_send=dma((4,)), a_recv=dma((4,)), c_ssem=dma((2, 4)), c_rsem=dma((2, 4)),
        one_ssem=dma((2, 2)), one_rsem=dma((2, 2)), two_ssem=dma((2, 2, 2)), two_rsem=dma((2, 2, 2)),
        three_ssem=dma((2, 2)), three_rsem=dma((2, 2)), four_ssem=dma((2, 2, 2)), four_rsem=dma((2, 2, 2)),
        z_ssem=dma, z_rsem=dma,
    )


def rows_of(step, size=CHUNK):
    return pl.ds(pl.multiple_of(step * size, size), size)


def slabs_of(step, size=CHUNK // 8):
    return pl.ds(step * size, size)


def mean_of(x):
    return jnp.sum(x, -1, keepdims=True) * (1.0 / D)


def normalize(x):
    center = x - mean_of(x)
    inverse = lax.rsqrt(mean_of(center * center) + 1e-06)
    return center, inverse


def project(src, w, q, k, v):
    x = src[...]
    q[...] = dot(x, w[:, 0:PAD]).astype(BF16)
    k[...] = pltpu.roll(dot(x, w[:, 512:D]), PAD - 64, 1).astype(BF16)
    v[:, 512:PAD] = jnp.zeros((N, 128), BF16)
    v[:, 0:HD] = dot(x, w[:, D : 3 * HD]).astype(BF16)


def forward_heads(q, k, v, weights, acc, keep):
    for head in range(HEADS):
        offset, cut, wide = window(head)
        mine = head_mask(offset, wide)
        queries = jnp.where(mine, q[:, cut].astype(F32), 0.0).astype(BF16)
        p = jnp.exp(dot_nt(queries, k[:, cut]) * FACTOR)
        if keep is not None:
            p = jnp.where(keep, p, 0.0)
        w = (p * (1.0 / jnp.sum(p, -1, keepdims=True))).astype(BF16)
        weights[head] = w
        out = dot(w, v[:, cut])
        acc[:, cut] = out if head == 0 else jnp.where(mine, out, acc[:, cut])


def backward_heads(q, k, v, weights, grad, accq, acck, accv):
    for head in range(HEADS):
        offset, cut, wide = window(head)
        mine = head_mask(offset, wide)
        g = grad[:, cut]
        w = weights[head]
        e = dot_nt(jnp.where(mine, g.astype(F32), 0.0).astype(BF16), v[:, cut])
        p = w.astype(F32)
        r = (p * (e - jnp.sum(e * p, -1, keepdims=True)) * FACTOR).astype(BF16)
        for acc, out in ((accv, dot_tn(w, g)), (accq, dot(r, k[:, cut])), (acck, dot_tn(r, q[:, cut]))):
            acc[:, cut] = out if head == 0 else jnp.where(mine, out, acc[:, cut])


def join(nat, accq, acck, accv):
    lane = lax.broadcasted_iota(jnp.int32, (N, 128), 1)
    moved = pltpu.roll(acck[...], 64, 1)
    nat[:, 0:512] = accq[:, 0:512].astype(BF16)
    nat[:, 512:640] = jnp.where(lane < 64, accq[:, 512:640], moved[:, 0:128]).astype(BF16)
    nat[:, 640:1152] = moved[:, 128:640].astype(BF16)
    nat[:, 1152:1664] = accv[:, 0:512].astype(BF16)
    nat[:, 1664:1792] = jnp.where(lane < 64, accv[:, 512:640], 0.0).astype(BF16)


def kernel(vid_hbm, wsi_hbm, wso_hbm, wti_hbm, wto_hbm, cot_hbm, o_out, o_gv, o_gi, o_go, names, *refs):
    r = dict(zip(names, refs))
    seq = lax.axis_index("seq")
    dp = lax.axis_index("dp")
    z, y_hi, core = seq // 4, seq // 2 % 2, seq % 2
    x, y_lo = dp // 2, dp % 2
    y = y_hi * 2 + y_lo

    def at_seq(s):
        return {"seq": s, "dp": dp}

    def at_x(to):
        return {"seq": seq, "dp": to * 2 + y_lo}

    def at_y(to):
        return {"seq": z * 4 + to // 2 * 2 + core, "dp": x * 2 + to % 2}

    loads = []
    for i, (src, dst) in enumerate(
        ((cot_hbm, "cot"), (wto_hbm, "wto"), (vid_hbm, "vid"), (wsi_hbm, "wsi"), (wso_hbm, "wso"), (wti_hbm, "wti"))
    ):
        copy = pltpu.make_async_copy(src, r[dst], r["load"].at[i])
        copy.start()
        loads.append(copy)

    barrier = pltpu.get_barrier_semaphore()

    def greet(k, carry):
        pl.semaphore_signal(barrier, inc=1, device_id=at_seq(lax.rem(seq + k, 32)), device_id_type=MESH)
        return carry

    lax.fori_loop(1, 32, greet, 0)
    for step in (1, 3):
        pl.semaphore_signal(barrier, inc=1, device_id=at_x((x + step) % 4), device_id_type=MESH)
        pl.semaphore_signal(barrier, inc=1, device_id=at_y((y + step) % 4), device_id_type=MESH)

    def exchange(which, send, recv):
        def one(i, carry):
            k = 16 + (i + 1) // 2 * (1 - 2 * (i % 2))
            to = lax.rem(seq + k, 32)
            pltpu.make_async_remote_copy(
                src_ref=send.at[to],
                dst_ref=recv.at[seq],
                send_sem=r["a_send"].at[which],
                recv_sem=r["a_recv"].at[which],
                device_id=at_seq(to),
                device_id_type=MESH,
            ).start()
            return carry

        lax.fori_loop(0, 31, one, 0)
        recv[seq] = send[seq]

    def wait_exchange(which, recv):
        some = recv.at[pl.ds(0, 31)]
        pltpu.make_async_copy(some, some, r["a_recv"].at[which]).wait()

    def wait_sent(which, send):
        some = send.at[pl.ds(0, 31)]
        pltpu.make_async_copy(some, some, r["a_send"].at[which]).wait()

    loads[0].wait()
    loads[1].wait()
    ga = dot_nt(r["cot"][...], r["wto"][...])
    r["ga_send"][...] = ga.reshape(32, 8, HD).astype(BF16)
    pl.semaphore_wait(barrier, 35)
    exchange(0, r["ga_send"], r["ga_recv"])

    loads[2].wait()

    def norm_video(i, carry):
        rows = rows_of(i)
        v = r["vid"][rows, :].astype(F32)
        mean = mean_of(v)
        center = v - mean
        inverse = lax.rsqrt(mean_of(center * center) + 1e-06)
        r["s_mean"][rows, :] = jnp.broadcast_to(mean, (CHUNK, 128))
        r["s_inv"][rows, :] = jnp.broadcast_to(inverse, (CHUNK, 128))
        r["sh"][rows, :] = (center * inverse).astype(BF16)
        return carry

    lax.fori_loop(0, N // CHUNK, norm_video, 0)
    loads[3].wait()
    project(r["sh"], r["wsi"], r["sq"], r["sk"], r["sv"])
    forward_heads(r["sq"], r["sk"], r["sv"], r["sw"], r["acc"], None)
    r["small"][...] = r["acc"][...].astype(BF16)
    loads[4].wait()
    for n in range(0, D, 384):
        r["big"][:, n : n + 384] = dot(r["small"][:, 0:HD], r["wso"][:, n : n + 384])

    def norm_residual(i, carry):
        rows = rows_of(i)
        v = (r["vid"][rows, :].astype(F32) + r["big"][rows, :]).astype(BF16)
        r["res"][rows, :] = v
        v = v.astype(F32)
        mean = mean_of(v)
        center = v - mean
        inverse = lax.rsqrt(mean_of(center * center) + 1e-06)
        r["t_mean"][rows, :] = jnp.broadcast_to(mean, (CHUNK, 128))
        r["t_inv"][rows, :] = jnp.broadcast_to(inverse, (CHUNK, 128))
        r["h_send"][slabs_of(i)] = (center * inverse).reshape(CHUNK // 8, 8, D).astype(BF16)
        return carry

    lax.fori_loop(0, N // CHUNK, norm_residual, 0)
    exchange(1, r["h_send"], r["h_recv"])

    for b in range(8):
        part = r["cot"][:, 128 * b : 128 * b + 256].astype(F32)
        if b:
            part = pltpu.roll(part, 256 - 16 * b, 1)
        r["cpad"][b] = part.astype(BF16)
    loads[5].wait()

    wait_exchange(0, r["ga_recv"])
    r["small"][:, 512:PAD] = jnp.zeros((N, 128), BF16)
    r["small"][:, 0:HD] = r["ga_recv"][...].astype(F32).reshape(N, HD).astype(BF16)
    wait_exchange(1, r["h_recv"])

    def take_h(i, carry):
        v = r["h_recv"][slabs_of(i)].astype(F32).reshape(CHUNK, D)
        r["th"][rows_of(i), :] = v.astype(BF16)
        return carry

    lax.fori_loop(0, N // CHUNK, take_h, 0)
    project(r["th"], r["wti"], r["tq"], r["tk"], r["tv"])
    place = lax.broadcasted_iota(jnp.int32, (N, N), 0) % 8
    other = lax.broadcasted_iota(jnp.int32, (N, N), 1) % 8
    forward_heads(r["tq"], r["tk"], r["tv"], r["tw"], r["acc"], place == other)
    r["at_send"][...] = r["acc"][:, 0:HD].reshape(32, 8, HD).astype(BF16)
    exchange(2, r["at_send"], r["at_recv"])

    backward_heads(r["tq"], r["tk"], r["tv"], r["tw"], r["small"], r["accq"], r["acck"], r["accv"])
    join(r["nat"], r["accq"], r["acck"], r["accv"])
    for n in range(0, D, 384):
        r["big"][:, n : n + 384] = dot_nt(r["nat"][:, 0 : 3 * HD], r["wti"][n : n + 384, :])

    def give_gh(i, carry):
        r["gh_send"][slabs_of(i)] = r["big"][rows_of(i), :].reshape(CHUNK // 8, 8, D).astype(BF16)
        return carry

    lax.fori_loop(0, N // CHUNK, give_gh, 0)
    exchange(3, r["gh_send"], r["gh_recv"])

    r["turn"][...] = r["th"][...].astype(F32).T
    for c in range(2):
        for hi in range(2):
            for quad in range(2):
                pieces = []
                for zz in range(4 * quad, 4 * quad + 4):
                    first = zz * 144 + hi * 72 + c * 36
                    pieces.append(r["turn"][first : first + 36, :])
                low = c * 576 + hi * 288 + quad * 144
                r["h_t"][low : low + 144, :] = jnp.concatenate(pieces, 0).astype(BF16)
    for b in range(8):
        low = 216 * b // 128 * 128
        off = 216 * b - low
        part = r["nat"][:, low : low + 384].astype(F32)
        if off:
            part = pltpu.roll(part, 384 - off, 1)
        r["gpad"][b] = part[:, 0:256].astype(BF16)

    wait_exchange(2, r["at_recv"])
    r["acc"][:, 0:HD] = r["at_recv"][...].astype(F32).reshape(N, HD)
    r["turn"][0:HD, :] = r["acc"][:, 0:HD].T
    for c in range(2):
        for hi in range(2):
            pieces = []
            for zz in range(8):
                first = zz * 72 + hi * 36 + c * 18
                pieces.append(r["turn"][first : first + 18, :])
            low = c * 288 + hi * 144
            r["att_t"][low : low + 144, :] = jnp.concatenate(pieces, 0).astype(BF16)

    def core_copy(ab, xx):
        if ab == 0:
            src, dst = r["part"].at[1 - core, 0, xx], r["c_recv"].at[0, xx]
        else:
            src, dst = r["part"].at[1 - core, 1, :, xx], r["c_recv"].at[1, :, xx]
        return pltpu.make_async_remote_copy(
            src_ref=src, dst_ref=dst, send_sem=r["c_ssem"].at[ab, xx], recv_sem=r["c_rsem"].at[ab, xx],
            device_id=at_seq(seq + 1 - 2 * core), device_id_type=MESH,
        )

    for xx in range(4):
        for lo in range(2):
            b = 2 * xx + lo
            g_in = dot(r["h_t"][...], r["gpad"][b]).astype(BF16)
            g_out = dot(r["att_t"][...], r["cpad"][b])
            for c in range(2):
                for hi in range(2):
                    for ab in range(2):
                        yy = hi * 2 + lo
                        slot = (c, 0, xx, yy) if ab == 0 else (c, 1, yy, xx)
                        low = c * 576 + hi * 288 + ab * 144
                        low_out = c * 288 + hi * 144 + ab * 72
                        for half in range(2):
                            lanes = slice(half * 128, half * 128 + 128)
                            r["part"][slot + (half, slice(0, 144))] = g_in[low : low + 144, lanes]
                            r["part"][slot + (half, slice(144, 216))] = g_out[low_out : low_out + 72, lanes].astype(BF16)
        core_copy(0, xx).start()
        core_copy(1, xx).start()

    def add_in(dst, dst_at, src, src_at):
        dst[dst_at] = (dst[dst_at].astype(F32) + src[src_at].astype(F32)).astype(BF16)

    for xx in range(4):
        for ab in range(2):
            core_copy(ab, xx).wait_recv()
            for yy in range(4):
                slot = (xx, yy) if ab == 0 else (yy, xx)
                add_in(r["part"], (core, ab) + slot, r["c_recv"], (ab,) + slot)

    def places(first, ab):
        if (ab == 0) == first:
            return x, at_x
        return y, at_y

    def one_copy(ab, way):
        me, where = places(True, ab)
        to = (me + (1, 3)[way]) % 4
        return pltpu.make_async_remote_copy(
            src_ref=r["part"].at[core, ab, (me + 2) % 4, pl.ds(2 * way, 2)], dst_ref=r["one_recv"].at[ab, way],
            send_sem=r["one_ssem"].at[ab, way], recv_sem=r["one_rsem"].at[ab, way],
            device_id=where(to), device_id_type=MESH,
        )

    def two_copy(ab, way, late):
        me, where = places(True, ab)
        to = (me + (1, 3)[way]) % 4
        low = 2 * way if late else 2 - 2 * way
        return pltpu.make_async_remote_copy(
            src_ref=r["part"].at[core, ab, to, pl.ds(low, 2)], dst_ref=r["two_recv"].at[ab, way, pl.ds(low, 2)],
            send_sem=r["two_ssem"].at[ab, way, late], recv_sem=r["two_rsem"].at[ab, way, late],
            device_id=where(to), device_id_type=MESH,
        )

    def three_copy(ab, way):
        me, where = places(False, ab)
        to = (me + (1, 3)[way]) % 4
        return pltpu.make_async_remote_copy(
            src_ref=r["mid"].at[ab, (me + 2) % 4, way], dst_ref=r["three_recv"].at[ab, way],
            send_sem=r["three_ssem"].at[ab, way], recv_sem=r["three_rsem"].at[ab, way],
            device_id=where(to), device_id_type=MESH,
        )

    def four_copy(ab, way, late):
        me, where = places(False, ab)
        to = (me + (1, 3)[way]) % 4
        half = way if late else 1 - way
        return pltpu.make_async_remote_copy(
            src_ref=r["mid"].at[ab, to, half], dst_ref=r["four_recv"].at[ab, way, half],
            send_sem=r["four_ssem"].at[ab, way, late], recv_sem=r["four_rsem"].at[ab, way, late],
            device_id=where(to), device_id_type=MESH,
        )

    both = ((0, 0), (1, 0), (0, 1), (1, 1))
    for ab, way in both:
        one_copy(ab, way).start()
    for ab, way in both:
        two_copy(ab, way, 0).start()

    r["small"][:, 0:HD] = r["acc"][:, 0:HD].astype(BF16)
    for n in range(0, D, 384):
        o_out[:, n : n + 384] = (
            r["res"][:, n : n + 384].astype(F32) + dot(r["small"][:, 0:HD], r["wto"][:, n : n + 384])
        ).astype(BF16)

    for ab, way in both:
        one_copy(ab, way).wait_recv()
        me, _ = places(True, ab)
        to = (me + (1, 3)[way]) % 4
        for yy in range(2):
            add_in(r["part"], (core, ab, to, 2 * way + yy), r["one_recv"], (ab, way, yy))
        two_copy(ab, way, 1).start()

    wait_exchange(3, r["gh_recv"])

    def norm_back_residual(i, carry):
        rows = rows_of(i)
        g = r["gh_recv"][slabs_of(i)].astype(F32).reshape(CHUNK, D)
        inverse = r["t_inv"][rows, 0:1]
        n = (r["res"][rows, :].astype(F32) - r["t_mean"][rows, 0:1]) * inverse
        back = inverse * (g - mean_of(g) - n * mean_of(g * n))
        r["res"][rows, :] = (r["cot"][rows, :].astype(F32) + back).astype(BF16)
        return carry

    lax.fori_loop(0, N // CHUNK, norm_back_residual, 0)
    r["small"][:, 0:HD] = dot_nt(r["res"][...], r["wso"][...]).astype(BF16)
    backward_heads(r["sq"], r["sk"], r["sv"], r["sw"], r["small"], r["accq"], r["acck"], r["accv"])

    for ab in range(2):
        for way in range(2):
            for late in range(2):
                two_copy(ab, way, late).wait_recv()
        me, _ = places(True, ab)
        for j in range(4):
            r["mid"][ab, j] = (
                r["part"][core, ab, me, j].astype(F32)
                + r["two_recv"][ab, 0, j].astype(F32)
                + r["two_recv"][ab, 1, j].astype(F32)
            ).astype(BF16)
        for way in range(2):
            three_copy(ab, way).start()
        for way in range(2):
            four_copy(ab, way, 0).start()

    join(r["nat"], r["accq"], r["acck"], r["accv"])
    for n in range(0, D, 384):
        r["big"][:, n : n + 384] = dot_nt(r["nat"][:, 0 : 3 * HD], r["wsi"][n : n + 384, :])

    for ab, way in both:
        three_copy(ab, way).wait_recv()
        me, _ = places(False, ab)
        to = (me + (1, 3)[way]) % 4
        add_in(r["mid"], (ab, to, way), r["three_recv"], (ab, way))
        four_copy(ab, way, 1).start()

    def norm_back_video(i, carry):
        rows = rows_of(i)
        g = r["big"][rows, :]
        inverse = r["s_inv"][rows, 0:1]
        n = (r["vid"][rows, :].astype(F32) - r["s_mean"][rows, 0:1]) * inverse
        back = inverse * (g - mean_of(g) - n * mean_of(g * n))
        o_gv[rows, :] = (r["res"][rows, :].astype(F32) + back).astype(BF16)
        return carry

    lax.fori_loop(0, N // CHUNK, norm_back_video, 0)

    for ab in range(2):
        for way in range(2):
            for late in range(2):
                four_copy(ab, way, late).wait_recv()
        me, _ = places(False, ab)
        for half in range(2):
            r["zsum"][ab, half] = (
                r["mid"][ab, me, half].astype(F32)
                + r["four_recv"][ab, 0, half].astype(F32)
                + r["four_recv"][ab, 1, half].astype(F32)
            )
            for j in range(4):
                piece = jnp.concatenate(
                    [
                        r["zsum"][ab, half, 36 * j : 36 * j + 36, :],
                        r["zsum"][ab, half, 144 + 18 * j : 144 + 18 * j + 18, :],
                        jnp.zeros((ZROWS - 54, 128), F32),
                    ],
                    0,
                )
                r["z_send"][4 * ab + j, half] = piece.astype(BF16)

    def z_one(k, carry):
        to = lax.rem(z + k, 8)
        pltpu.make_async_remote_copy(
            src_ref=r["z_send"].at[to], dst_ref=r["z_recv"].at[z], send_sem=r["z_ssem"], recv_sem=r["z_rsem"],
            device_id=at_seq(to * 4 + y_hi * 2 + core), device_id_type=MESH,
        ).start()
        return carry

    lax.fori_loop(1, 8, z_one, 0)
    r["z_recv"][z] = r["z_send"][z]
    some = r["z_recv"].at[pl.ds(0, 7)]
    pltpu.make_async_copy(some, some, r["z_rsem"]).wait()
    for half in range(2):
        total = r["z_recv"][0, half].astype(F32)
        for j in range(1, 8):
            total = total + r["z_recv"][j, half].astype(F32)
        if half == 0:
            o_gi[:, 0:128] = total[0:36, :]
            o_go[:, 0:128] = total[36:54, :]
        else:
            o_gi[:, 128:216] = total[0:36, 0:88]
            o_go[:, 128:144] = total[36:54, 0:16]

    for which, name in enumerate(("ga_send", "h_send", "at_send", "gh_send")):
        wait_sent(which, r[name])
    for ab in range(2):
        for xx in range(4):
            core_copy(ab, xx).wait_send()
        for way in range(2):
            one_copy(ab, way).wait_send()
            three_copy(ab, way).wait_send()
            for late in range(2):
                two_copy(ab, way, late).wait_send()
                four_copy(ab, way, late).wait_send()
    some = r["z_send"].at[pl.ds(0, 7)]
    pltpu.make_async_copy(some, some, r["z_ssem"]).wait()


def local(video, spatial_in, spatial_out, temporal_in, temporal_out, cotangent):
    shapes = scratch_shapes()
    names = tuple(shapes)
    anywhere = pl.BlockSpec(memory_space=pl.ANY)
    whole = pl.BlockSpec(memory_space=pltpu.VMEM)

    def body(*refs):
        kernel(*refs[:10], names, *refs[10:])

    out, grad_video, grad_in, grad_out = pl.pallas_call(
        body,
        out_shape=(
            jax.ShapeDtypeStruct((N, D), BF16),
            jax.ShapeDtypeStruct((N, D), BF16),
            jax.ShapeDtypeStruct((36, 216), F32),
            jax.ShapeDtypeStruct((18, 144), F32),
        ),
        in_specs=[anywhere] * 6,
        out_specs=(whole,) * 4,
        scratch_shapes=list(shapes.values()),
        compiler_params=pltpu.CompilerParams(
            collective_id=0, has_side_effects=True, vmem_limit_bytes=60 * 1024 * 1024
        ),
        cost_estimate=pl.CostEstimate(flops=9_000_000_000, bytes_accessed=13_000_000, transcendentals=1_100_000),
    )(video.reshape(N, D), spatial_in, spatial_out, temporal_in, temporal_out, cotangent.reshape(N, D))
    return (out.reshape(video.shape), grad_video.reshape(video.shape), grad_in, grad_out)


def solution(mesh):
    in_specs = (P("dp", "seq", None, None), P(), P(), P(), P(), P("dp", "seq", None, None))
    out_specs = (
        P("dp", "seq", None, None),
        P("dp", "seq", None, None),
        P("seq", "dp"),
        P("seq", "dp"),
    )
    return jax.shard_map(local, mesh=mesh, in_specs=in_specs, out_specs=out_specs, check_vma=False)
```

```python
import jax
import jax.numpy as jnp
from jax import lax
from jax.experimental import pallas as pl
from jax.experimental.pallas import tpu as pltpu
from jax.sharding import PartitionSpec as P

HEADS = 8
HEAD = 72
D = 1152
HD = 576
N = 256
PAD = 640
FACTOR = HEAD ** (-0.5)
F32 = jnp.float32
BF16 = jnp.bfloat16
MESH = pl.DeviceIdType.MESH
CHUNK = 32
ROWS = 224
ZROWS = 64


def dot(a, b):
    return jnp.dot(a, b, preferred_element_type=F32)


def dot_nt(a, b):
    return lax.dot_general(a, b, (((1,), (1,)), ((), ())), preferred_element_type=F32)


def dot_tn(a, b):
    return lax.dot_general(a, b, (((0,), (0,)), ((), ())), preferred_element_type=F32)


def remote(kind, **ends):
    return pltpu.make_async_remote_copy(**ends)


def drain(kind, some, sem):
    pltpu.make_async_copy(some, some, sem).wait()


def window(head):
    start = head * HEAD
    low = start // 128 * 128
    wide = 128 if start + HEAD <= low + 128 else 256
    return start - low, slice(low, low + wide), wide


def head_mask(offset, wide):
    lane = lax.broadcasted_iota(jnp.int32, (N, wide), 1)
    return (lane >= offset) & (lane < offset + HEAD)


def scratch_shapes():
    slab = (2, ROWS, 128)
    vm = lambda *shape: pltpu.VMEM(shape, BF16)
    vf = lambda *shape: pltpu.VMEM(shape, F32)
    dma = pltpu.SemaphoreType.DMA
    return dict(
        vid=vm(N, D), cot=vm(N, D), wsi=vm(3 * HD, D), wso=vm(HD, D), wti=vm(3 * HD, D), wto=vm(HD, D),
        ga_send=vm(32, 8, HD), ga_recv=vm(32, 8, HD), h_send=vm(32, 8, D), h_recv=vm(32, 8, D),
        at_send=vm(32, 8, HD), at_recv=vm(32, 8, HD), gh_send=vm(32, 8, D), gh_recv=vm(32, 8, D),
        sh=vm(N, D), sq=vm(N, PAD), sk=vm(N, PAD), sv=vm(N, PAD), sw=vm(HEADS, N, N),
        th=vm(N, D), tq=vm(N, PAD), tk=vm(N, PAD), tv=vm(N, PAD), tw=vm(HEADS, N, N),
        acc=vf(N, PAD), accq=vf(N, PAD), acck=vf(N, PAD), accv=vf(N, PAD),
        small=vm(N, PAD), nat=vm(N, 1792), big=vf(N, D),
        res=vm(N, D), s_mean=vf(N, 128), s_inv=vf(N, 128), t_mean=vf(N, 128), t_inv=vf(N, 128),
        turn=vf(D, N), h_t=vm(D, N), att_t=vm(HD, N),
        gpad=vm(8, N, 256), cpad=vm(8, N, 256),
        part=vm(2, 2, 4, 4, *slab), c_recv=vm(2, 4, 4, *slab),
        one_recv=vm(2, 2, 2, *slab), two_recv=vm(2, 2, 4, *slab),
        mid=vm(2, 4, *slab), three_recv=vm(2, 2, ROWS, 128), four_recv=vm(2, 2, *slab),
        zsum=vf(2, *slab), z_send=vm(8, 2, ZROWS, 128), z_recv=vm(8, 2, ZROWS, 128),
        load=dma((6,)), a_send=dma((4,)), a_recv=dma((4,)), c_ssem=dma((2, 2, 4)), c_rsem=dma((2, 2, 4)),
        one_ssem=dma((2, 2)), one_rsem=dma((2, 2)), two_ssem=dma((2, 2, 2)), two_rsem=dma((2, 2, 2)),
        three_ssem=dma((2, 2)), three_rsem=dma((2, 2)), four_ssem=dma((2, 2, 2)), four_rsem=dma((2, 2, 2)),
        z_ssem=dma, z_rsem=dma,
    )


def rows_of(step, size=CHUNK):
    return pl.ds(pl.multiple_of(step * size, size), size)


def slabs_of(step, size=CHUNK // 8):
    return pl.ds(step * size, size)


def mean_of(x):
    return jnp.sum(x, -1, keepdims=True) * (1.0 / D)


def normalize(x):
    center = x - mean_of(x)
    inverse = lax.rsqrt(mean_of(center * center) + 1e-06)
    return center, inverse


def project(src, w, q, k, v):
    x = src[...]
    q[...] = dot_nt(x, w[0:PAD, :]).astype(BF16)
    k[...] = dot_nt(x, w[HD : HD + PAD, :]).astype(BF16)
    v[:, 512:PAD] = jnp.zeros((N, 128), BF16)
    v[:, 0:HD] = dot_nt(x, w[D : 3 * HD, :]).astype(BF16)


def forward_heads(q, k, v, weights, acc, keep):
    for head in range(HEADS):
        offset, cut, wide = window(head)
        mine = head_mask(offset, wide)
        queries = jnp.where(mine, q[:, cut].astype(F32), 0.0).astype(BF16)
        p = jnp.exp(dot_nt(queries, k[:, cut]) * FACTOR)
        if keep is not None:
            p = jnp.where(keep, p, 0.0)
        w = (p * (1.0 / jnp.sum(p, -1, keepdims=True))).astype(BF16)
        weights[head] = w
        out = dot(w, v[:, cut])
        acc[:, cut] = out if head == 0 else jnp.where(mine, out, acc[:, cut])


def backward_heads(q, k, v, weights, grad, accq, acck, accv):
    for head in range(HEADS):
        offset, cut, wide = window(head)
        mine = head_mask(offset, wide)
        g = grad[:, cut]
        w = weights[head]
        e = dot_nt(jnp.where(mine, g.astype(F32), 0.0).astype(BF16), v[:, cut])
        p = w.astype(F32)
        r = (p * (e - jnp.sum(e * p, -1, keepdims=True)) * FACTOR).astype(BF16)
        for acc, out in ((accv, dot_tn(w, g)), (accq, dot(r, k[:, cut])), (acck, dot_tn(r, q[:, cut]))):
            acc[:, cut] = out if head == 0 else jnp.where(mine, out, acc[:, cut])


def join(nat, accq, acck, accv):
    lane = lax.broadcasted_iota(jnp.int32, (N, 128), 1)
    moved = pltpu.roll(acck[...], 64, 1)
    nat[:, 0:512] = accq[:, 0:512].astype(BF16)
    nat[:, 512:640] = jnp.where(lane < 64, accq[:, 512:640], moved[:, 0:128]).astype(BF16)
    nat[:, 640:1152] = moved[:, 128:640].astype(BF16)
    nat[:, 1152:1664] = accv[:, 0:512].astype(BF16)
    nat[:, 1664:1792] = jnp.where(lane < 64, accv[:, 512:640], 0.0).astype(BF16)


def kernel(vid_hbm, wsi_hbm, wso_hbm, wti_hbm, wto_hbm, cot_hbm, o_out, o_gv, o_gi, o_go, names, *refs):
    r = dict(zip(names, refs))
    seq = lax.axis_index("seq")
    dp = lax.axis_index("dp")
    z, y_hi, core = seq // 4, seq // 2 % 2, seq % 2
    x, y_lo = dp // 2, dp % 2
    y = y_hi * 2 + y_lo

    def at_seq(s):
        return {"seq": s, "dp": dp}

    def at_x(to):
        return {"seq": seq, "dp": to * 2 + y_lo}

    def at_y(to):
        return {"seq": z * 4 + to // 2 * 2 + core, "dp": x * 2 + to % 2}

    loads = []
    for i, (src, dst) in enumerate(
        ((vid_hbm, "vid"), (cot_hbm, "cot"), (wto_hbm, "wto"), (wsi_hbm, "wsi"), (wso_hbm, "wso"), (wti_hbm, "wti"))
    ):
        copy = pltpu.make_async_copy(src, r[dst], r["load"].at[i])
        copy.start()
        loads.append(copy)

    barrier = pltpu.get_barrier_semaphore()

    def greet(k, carry):
        pl.semaphore_signal(barrier, inc=1, device_id=at_seq(lax.rem(seq + k, 32)), device_id_type=MESH)
        return carry

    lax.fori_loop(1, 32, greet, 0)
    for step in (1, 3):
        pl.semaphore_signal(barrier, inc=1, device_id=at_x((x + step) % 4), device_id_type=MESH)
        pl.semaphore_signal(barrier, inc=1, device_id=at_y((y + step) % 4), device_id_type=MESH)

    def slab_copy(which, send, recv, to):
        return remote(
            "swap",
            src_ref=send.at[to],
            dst_ref=recv.at[seq],
            send_sem=r["a_send"].at[which],
            recv_sem=r["a_recv"].at[which],
            device_id=at_seq(to),
            device_id_type=MESH,
        )

    def exchange(which, send, recv):
        def one(i, carry):
            k = 16 + (i + 1) // 2 * (1 - 2 * (i % 2))
            slab_copy(which, send, recv, lax.rem(seq + k, 32)).start()
            return carry

        lax.fori_loop(0, 31, one, 0)
        recv[seq] = send[seq]

    def wait_exchange(which, recv):
        drain("swap", recv.at[pl.ds(0, 31)], r["a_recv"].at[which])

    def wait_sent(which, send):
        drain("swap", send.at[pl.ds(0, 31)], r["a_send"].at[which])

    loads[0].wait()

    def norm_video(i, carry):
        rows = rows_of(i)
        v = r["vid"][rows, :].astype(F32)
        mean = mean_of(v)
        center = v - mean
        inverse = lax.rsqrt(mean_of(center * center) + 1e-06)
        r["s_mean"][rows, :] = jnp.broadcast_to(mean, (CHUNK, 128))
        r["s_inv"][rows, :] = jnp.broadcast_to(inverse, (CHUNK, 128))
        r["sh"][rows, :] = (center * inverse).astype(BF16)
        return carry

    lax.fori_loop(0, N // CHUNK, norm_video, 0)
    loads[1].wait()
    loads[2].wait()
    ga = dot_nt(r["cot"][...], r["wto"][...])
    r["ga_send"][...] = ga.reshape(32, 8, HD).astype(BF16)
    pl.semaphore_wait(barrier, 35)
    exchange(0, r["ga_send"], r["ga_recv"])

    loads[3].wait()
    project(r["sh"], r["wsi"], r["sq"], r["sk"], r["sv"])
    forward_heads(r["sq"], r["sk"], r["sv"], r["sw"], r["acc"], None)
    r["small"][...] = r["acc"][...].astype(BF16)
    loads[4].wait()
    for n in range(0, D, 384):
        r["big"][:, n : n + 384] = dot(r["small"][:, 0:HD], r["wso"][:, n : n + 384])

    def norm_residual(step, carry):
        i = lax.rem(z + 4 + (step + 1) // 2 * (1 - 2 * (step % 2)), 8)
        rows = rows_of(i)
        v = (r["vid"][rows, :].astype(F32) + r["big"][rows, :]).astype(BF16)
        r["res"][rows, :] = v
        v = v.astype(F32)
        mean = mean_of(v)
        center = v - mean
        inverse = lax.rsqrt(mean_of(center * center) + 1e-06)
        r["t_mean"][rows, :] = jnp.broadcast_to(mean, (CHUNK, 128))
        r["t_inv"][rows, :] = jnp.broadcast_to(inverse, (CHUNK, 128))
        r["h_send"][slabs_of(i)] = (center * inverse).reshape(CHUNK // 8, 8, D).astype(BF16)
        for j in range(4):
            to = i * 4 + lax.rem(seq + 2 + j, 4)

            @pl.when(to != seq)
            def _():
                slab_copy(1, r["h_send"], r["h_recv"], to).start()

        return carry

    lax.fori_loop(0, N // CHUNK, norm_residual, 0)
    r["h_recv"][seq] = r["h_send"][seq]

    for b in range(8):
        part = r["cot"][:, 128 * b : 128 * b + 256].astype(F32)
        if b:
            part = pltpu.roll(part, 256 - 16 * b, 1)
        r["cpad"][b] = part.astype(BF16)
    loads[5].wait()

    wait_exchange(0, r["ga_recv"])
    r["small"][:, 512:PAD] = jnp.zeros((N, 128), BF16)
    r["small"][:, 0:HD] = r["ga_recv"][...].astype(F32).reshape(N, HD).astype(BF16)
    wait_exchange(1, r["h_recv"])

    def take_h(i, carry):
        v = r["h_recv"][slabs_of(i)].astype(F32).reshape(CHUNK, D)
        r["th"][rows_of(i), :] = v.astype(BF16)
        return carry

    lax.fori_loop(0, N // CHUNK, take_h, 0)
    project(r["th"], r["wti"], r["tq"], r["tk"], r["tv"])
    place = lax.broadcasted_iota(jnp.int32, (N, N), 0) % 8
    other = lax.broadcasted_iota(jnp.int32, (N, N), 1) % 8
    forward_heads(r["tq"], r["tk"], r["tv"], r["tw"], r["acc"], place == other)
    r["at_send"][...] = r["acc"][:, 0:HD].reshape(32, 8, HD).astype(BF16)
    exchange(2, r["at_send"], r["at_recv"])

    backward_heads(r["tq"], r["tk"], r["tv"], r["tw"], r["small"], r["accq"], r["acck"], r["accv"])
    join(r["nat"], r["accq"], r["acck"], r["accv"])
    for n in range(0, D, 384):
        r["big"][:, n : n + 384] = dot(r["nat"][:, 0 : 3 * HD], r["wti"][:, n : n + 384])

    def give_gh(i, carry):
        r["gh_send"][slabs_of(i)] = r["big"][rows_of(i), :].reshape(CHUNK // 8, 8, D).astype(BF16)
        return carry

    lax.fori_loop(0, N // CHUNK, give_gh, 0)
    exchange(3, r["gh_send"], r["gh_recv"])

    r["turn"][...] = r["th"][...].astype(F32).T
    for c in range(2):
        for hi in range(2):
            for quad in range(2):
                pieces = []
                for zz in range(4 * quad, 4 * quad + 4):
                    first = zz * 144 + hi * 72 + c * 36
                    pieces.append(r["turn"][first : first + 36, :])
                low = c * 576 + hi * 288 + quad * 144
                r["h_t"][low : low + 144, :] = jnp.concatenate(pieces, 0).astype(BF16)
    for b in range(8):
        low = 216 * b // 128 * 128
        off = 216 * b - low
        part = r["nat"][:, low : low + 384].astype(F32)
        if off:
            part = pltpu.roll(part, 384 - off, 1)
        r["gpad"][b] = part[:, 0:256].astype(BF16)

    def core_copy(which, ab, xx):
        rows = (pl.ds(0, 144), pl.ds(144, ROWS - 144))[which]
        if ab == 0:
            src, dst = r["part"].at[1 - core, 0, xx, :, :, rows], r["c_recv"].at[0, xx, :, :, rows]
        else:
            src, dst = r["part"].at[1 - core, 1, :, xx, :, rows], r["c_recv"].at[1, :, xx, :, rows]
        return remote(
            "core",
            src_ref=src, dst_ref=dst, send_sem=r["c_ssem"].at[which, ab, xx], recv_sem=r["c_rsem"].at[which, ab, xx],
            device_id=at_seq(seq + 1 - 2 * core), device_id_type=MESH,
        )

    def fill(which, xx, lo, value):
        size = (144, 72)[which]
        for c in range(2):
            for hi in range(2):
                for ab in range(2):
                    yy = hi * 2 + lo
                    slot = (c, 0, xx, yy) if ab == 0 else (c, 1, yy, xx)
                    low = size * (c * 4 + hi * 2 + ab)
                    for half in range(2):
                        to = slot + (half, slice(144 * which, 144 * which + size))
                        r["part"][to] = value[low : low + size, half * 128 : half * 128 + 128].astype(BF16)

    for xx in range(4):
        for lo in range(2):
            fill(0, xx, lo, dot(r["h_t"][...], r["gpad"][2 * xx + lo]))
        core_copy(0, 0, xx).start()
        core_copy(0, 1, xx).start()

    wait_exchange(2, r["at_recv"])
    r["acc"][:, 0:HD] = r["at_recv"][...].astype(F32).reshape(N, HD)
    r["turn"][0:HD, :] = r["acc"][:, 0:HD].T
    for c in range(2):
        for hi in range(2):
            pieces = []
            for zz in range(8):
                first = zz * 72 + hi * 36 + c * 18
                pieces.append(r["turn"][first : first + 18, :])
            low = c * 288 + hi * 144
            r["att_t"][low : low + 144, :] = jnp.concatenate(pieces, 0).astype(BF16)

    for xx in range(4):
        for lo in range(2):
            fill(1, xx, lo, dot(r["att_t"][...], r["cpad"][2 * xx + lo]))
        core_copy(1, 0, xx).start()
        core_copy(1, 1, xx).start()

    r["small"][:, 0:HD] = r["acc"][:, 0:HD].astype(BF16)
    for n in range(0, D, 384):
        o_out[:, n : n + 384] = (
            r["res"][:, n : n + 384].astype(F32) + dot(r["small"][:, 0:HD], r["wto"][:, n : n + 384])
        ).astype(BF16)

    def add_in(dst, dst_at, src, src_at):
        dst[dst_at] = (dst[dst_at].astype(F32) + src[src_at].astype(F32)).astype(BF16)

    for xx in range(4):
        for ab in range(2):
            core_copy(0, ab, xx).wait_recv()
            core_copy(1, ab, xx).wait_recv()
            for yy in range(4):
                slot = (xx, yy) if ab == 0 else (yy, xx)
                add_in(r["part"], (core, ab) + slot, r["c_recv"], (ab,) + slot)

    def places(first, ab):
        if (ab == 0) == first:
            return x, at_x
        return y, at_y

    def one_copy(ab, way):
        me, where = places(True, ab)
        to = (me + (1, 3)[way]) % 4
        return remote(
            "one",
            src_ref=r["part"].at[core, ab, (me + 2) % 4, pl.ds(2 * way, 2)], dst_ref=r["one_recv"].at[ab, way],
            send_sem=r["one_ssem"].at[ab, way], recv_sem=r["one_rsem"].at[ab, way],
            device_id=where(to), device_id_type=MESH,
        )

    def two_copy(ab, way, late):
        me, where = places(True, ab)
        to = (me + (1, 3)[way]) % 4
        low = 2 * way if late else 2 - 2 * way
        return remote(
            "two",
            src_ref=r["part"].at[core, ab, to, pl.ds(low, 2)], dst_ref=r["two_recv"].at[ab, way, pl.ds(low, 2)],
            send_sem=r["two_ssem"].at[ab, way, late], recv_sem=r["two_rsem"].at[ab, way, late],
            device_id=where(to), device_id_type=MESH,
        )

    def three_copy(ab, way):
        me, where = places(False, ab)
        to = (me + (1, 3)[way]) % 4
        return remote(
            "three",
            src_ref=r["mid"].at[ab, (me + 2) % 4, way], dst_ref=r["three_recv"].at[ab, way],
            send_sem=r["three_ssem"].at[ab, way], recv_sem=r["three_rsem"].at[ab, way],
            device_id=where(to), device_id_type=MESH,
        )

    def four_copy(ab, way, late):
        me, where = places(False, ab)
        to = (me + (1, 3)[way]) % 4
        half = way if late else 1 - way
        return remote(
            "four",
            src_ref=r["mid"].at[ab, to, half], dst_ref=r["four_recv"].at[ab, way, half],
            send_sem=r["four_ssem"].at[ab, way, late], recv_sem=r["four_rsem"].at[ab, way, late],
            device_id=where(to), device_id_type=MESH,
        )

    both = ((0, 0), (1, 0), (0, 1), (1, 1))
    for ab, way in both:
        one_copy(ab, way).start()
    for ab, way in both:
        two_copy(ab, way, 0).start()

    for ab, way in both:
        one_copy(ab, way).wait_recv()
        me, _ = places(True, ab)
        to = (me + (1, 3)[way]) % 4
        for yy in range(2):
            add_in(r["part"], (core, ab, to, 2 * way + yy), r["one_recv"], (ab, way, yy))
        two_copy(ab, way, 1).start()

    wait_exchange(3, r["gh_recv"])

    def norm_back_residual(i, carry):
        rows = rows_of(i)
        g = r["gh_recv"][slabs_of(i)].astype(F32).reshape(CHUNK, D)
        inverse = r["t_inv"][rows, 0:1]
        n = (r["res"][rows, :].astype(F32) - r["t_mean"][rows, 0:1]) * inverse
        back = inverse * (g - mean_of(g) - n * mean_of(g * n))
        r["res"][rows, :] = (r["cot"][rows, :].astype(F32) + back).astype(BF16)
        return carry

    lax.fori_loop(0, N // CHUNK, norm_back_residual, 0)
    r["small"][:, 0:HD] = dot_nt(r["res"][...], r["wso"][...]).astype(BF16)
    backward_heads(r["sq"], r["sk"], r["sv"], r["sw"], r["small"], r["accq"], r["acck"], r["accv"])

    for ab in range(2):
        for way in range(2):
            for late in range(2):
                two_copy(ab, way, late).wait_recv()
        me, _ = places(True, ab)
        for j in range(4):
            r["mid"][ab, j] = (
                r["part"][core, ab, me, j].astype(F32)
                + r["two_recv"][ab, 0, j].astype(F32)
                + r["two_recv"][ab, 1, j].astype(F32)
            ).astype(BF16)
        for way in range(2):
            three_copy(ab, way).start()
        for way in range(2):
            four_copy(ab, way, 0).start()

    join(r["nat"], r["accq"], r["acck"], r["accv"])
    for n in range(0, D, 384):
        r["big"][:, n : n + 384] = dot(r["nat"][:, 0 : 3 * HD], r["wsi"][:, n : n + 384])

    for ab, way in both:
        three_copy(ab, way).wait_recv()
        me, _ = places(False, ab)
        to = (me + (1, 3)[way]) % 4
        add_in(r["mid"], (ab, to, way), r["three_recv"], (ab, way))
        four_copy(ab, way, 1).start()

    def norm_back_video(i, carry):
        rows = rows_of(i)
        g = r["big"][rows, :]
        inverse = r["s_inv"][rows, 0:1]
        n = (r["vid"][rows, :].astype(F32) - r["s_mean"][rows, 0:1]) * inverse
        back = inverse * (g - mean_of(g) - n * mean_of(g * n))
        o_gv[rows, :] = (r["res"][rows, :].astype(F32) + back).astype(BF16)
        return carry

    lax.fori_loop(0, N // CHUNK, norm_back_video, 0)

    for ab in range(2):
        for way in range(2):
            for late in range(2):
                four_copy(ab, way, late).wait_recv()
        me, _ = places(False, ab)
        for half in range(2):
            r["zsum"][ab, half] = (
                r["mid"][ab, me, half].astype(F32)
                + r["four_recv"][ab, 0, half].astype(F32)
                + r["four_recv"][ab, 1, half].astype(F32)
            )
            for j in range(4):
                piece = jnp.concatenate(
                    [
                        r["zsum"][ab, half, 36 * j : 36 * j + 36, :],
                        r["zsum"][ab, half, 144 + 18 * j : 144 + 18 * j + 18, :],
                        jnp.zeros((ZROWS - 54, 128), F32),
                    ],
                    0,
                )
                r["z_send"][4 * ab + j, half] = piece.astype(BF16)

    def z_one(k, carry):
        to = lax.rem(z + k, 8)
        remote(
            "z",
            src_ref=r["z_send"].at[to], dst_ref=r["z_recv"].at[z], send_sem=r["z_ssem"], recv_sem=r["z_rsem"],
            device_id=at_seq(to * 4 + y_hi * 2 + core), device_id_type=MESH,
        ).start()
        return carry

    lax.fori_loop(1, 8, z_one, 0)
    r["z_recv"][z] = r["z_send"][z]
    drain("z", r["z_recv"].at[pl.ds(0, 7)], r["z_rsem"])
    for half in range(2):
        total = r["z_recv"][0, half].astype(F32)
        for j in range(1, 8):
            total = total + r["z_recv"][j, half].astype(F32)
        if half == 0:
            o_gi[:, 0:128] = total[0:36, :]
            o_go[:, 0:128] = total[36:54, :]
        else:
            o_gi[:, 128:216] = total[0:36, 0:88]
            o_go[:, 128:144] = total[36:54, 0:16]

    for which, name in enumerate(("ga_send", "h_send", "at_send", "gh_send")):
        wait_sent(which, r[name])
    for ab in range(2):
        for xx in range(4):
            core_copy(0, ab, xx).wait_send()
            core_copy(1, ab, xx).wait_send()
        for way in range(2):
            one_copy(ab, way).wait_send()
            three_copy(ab, way).wait_send()
            for late in range(2):
                two_copy(ab, way, late).wait_send()
                four_copy(ab, way, late).wait_send()
    drain("z", r["z_send"].at[pl.ds(0, 7)], r["z_ssem"])


def hand_over(*refs):
    for source, result in zip(refs[:4], refs[4:]):
        result[...] = source[...]


def local(video, spatial_in, spatial_out, temporal_in, temporal_out, cotangent):
    shapes = scratch_shapes()
    names = tuple(shapes)
    anywhere = pl.BlockSpec(memory_space=pl.ANY)
    whole = pl.BlockSpec(memory_space=pltpu.VMEM)

    def body(*refs):
        kernel(*refs[:10], names, *refs[10:])

    results = (
        jax.ShapeDtypeStruct((N, D), BF16),
        jax.ShapeDtypeStruct((N, D), BF16),
        jax.ShapeDtypeStruct((36, 216), F32),
        jax.ShapeDtypeStruct((18, 144), F32),
    )
    held = pl.pallas_call(
        body,
        out_shape=results,
        in_specs=[anywhere] * 6,
        out_specs=(whole,) * 4,
        scratch_shapes=list(shapes.values()),
        compiler_params=pltpu.CompilerParams(
            collective_id=0, has_side_effects=True, vmem_limit_bytes=60 * 1024 * 1024
        ),
        cost_estimate=pl.CostEstimate(flops=9_000_000_000, bytes_accessed=13_000_000, transcendentals=1_100_000),
    )(video.reshape(N, D), spatial_in.T, spatial_out, temporal_in.T, temporal_out, cotangent.reshape(N, D))
    out, grad_video, grad_in, grad_out = pl.pallas_call(
        hand_over,
        out_shape=results,
        in_specs=[whole] * 4,
        out_specs=(whole,) * 4,
        cost_estimate=pl.CostEstimate(flops=0, bytes_accessed=2_400_000, transcendentals=0),
    )(*held)
    return (out.reshape(video.shape), grad_video.reshape(video.shape), grad_in, grad_out)


def solution(mesh):
    in_specs = (P("dp", "seq", None, None), P(), P(), P(), P(), P("dp", "seq", None, None))
    out_specs = (
        P("dp", "seq", None, None),
        P("dp", "seq", None, None),
        P("seq", "dp"),
        P("seq", "dp"),
    )
    return jax.shard_map(local, mesh=mesh, in_specs=in_specs, out_specs=out_specs, check_vma=False)
```

```python
import jax
import jax.numpy as jnp
from jax import lax
from jax.experimental import pallas as pl
from jax.experimental.pallas import tpu as pltpu
from jax.sharding import PartitionSpec as P

HEADS = 8
HEAD = 72
D = 1152
HD = 576
N = 256
PAD = 640
FACTOR = HEAD ** (-0.5)
F32 = jnp.float32
BF16 = jnp.bfloat16
MESH = pl.DeviceIdType.MESH
CHUNK = 32
ZROWS = 56


def dot(a, b):
    return jnp.dot(a, b, preferred_element_type=F32)


def dot_nt(a, b):
    return lax.dot_general(a, b, (((1,), (1,)), ((), ())), preferred_element_type=F32)


def dot_tn(a, b):
    return lax.dot_general(a, b, (((0,), (0,)), ((), ())), preferred_element_type=F32)


def remote(kind, **ends):
    return pltpu.make_async_remote_copy(**ends)


def drain(kind, some, sem):
    pltpu.make_async_copy(some, some, sem).wait()


def window(head):
    start = head * HEAD
    low = start // 128 * 128
    wide = 128 if start + HEAD <= low + 128 else 256
    return start - low, slice(low, low + wide), wide


def head_mask(offset, wide):
    lane = lax.broadcasted_iota(jnp.int32, (N, wide), 1)
    return (lane >= offset) & (lane < offset + HEAD)


def scratch_shapes():
    slab, thin = (2, 144, 128), (2, 48, 128)
    vm = lambda *shape: pltpu.VMEM(shape, BF16)
    vf = lambda *shape: pltpu.VMEM(shape, F32)
    dma = pltpu.SemaphoreType.DMA
    return dict(
        vid=vm(N, D), cot=vm(N, D), wsi=vm(3 * HD, D), wso=vm(HD, D), wti=vm(3 * HD, D), wto=vm(HD, D),
        ga_send=vm(32, 8, HD), ga_recv=vm(32, 8, HD), h_send=vm(32, 8, D), h_recv=vm(32, 8, D),
        at_send=vm(32, 8, HD), at_recv=vm(32, 8, HD), gh_send=vm(32, 8, D), gh_recv=vm(32, 8, D),
        sh=vm(N, D), sq=vm(N, PAD), sk=vm(N, PAD), sv=vm(N, PAD), sw=vm(HEADS, N, N),
        th=vm(N, D), tq=vm(N, PAD), tk=vm(N, PAD), tv=vm(N, PAD), tw=vm(HEADS, N, N),
        acc=vf(N, PAD), accq=vf(N, PAD), acck=vf(N, PAD), accv=vf(N, PAD),
        small=vm(N, PAD), nat=vm(N, 1792), big=vf(N, D),
        res=vm(N, D), s_mean=vf(N, 128), s_inv=vf(N, 128), t_mean=vf(N, 128), t_inv=vf(N, 128),
        turn=vf(D, N), h_t=vm(D, N), att_t=vm(HD, N),
        gpad=vm(8, N, 256), cpad=vm(8, N, 256),
        part_in=vm(2, 2, 4, 4, *slab), part_out=vm(2, 2, 4, 4, *thin),
        c_recv_in=vm(2, 4, 4, *slab), c_recv_out=vm(2, 4, 4, *thin),
        one_in=vm(2, 2, 2, *slab), one_out=vm(2, 2, 2, *thin), two_in=vm(2, 2, 4, *slab), two_out=vm(2, 2, 4, *thin),
        mid_in=vm(2, 4, *slab), mid_out=vm(2, 4, *thin),
        three_in=vm(2, 2, *slab[1:]), three_out=vm(2, 2, *thin[1:]), four_in=vm(2, 2, *slab), four_out=vm(2, 2, *thin),
        zsum=vf(2, 2, 216, 128), z_send=vm(8, 2, ZROWS, 128), z_recv=vm(8, 2, ZROWS, 128),
        load=dma((6,)), a_send=dma((4,)), a_recv=dma((4,)), c_ssem=dma((2, 2, 4)), c_rsem=dma((2, 2, 4)),
        one_ssem=dma((2, 2, 2)), one_rsem=dma((2, 2, 2)), two_ssem=dma((2, 2, 2, 2)), two_rsem=dma((2, 2, 2, 2)),
        three_ssem=dma((2, 2, 2)), three_rsem=dma((2, 2, 2)), four_ssem=dma((2, 2, 2, 2)), four_rsem=dma((2, 2, 2, 2)),
        z_ssem=dma, z_rsem=dma,
    )


def rows_of(step, size=CHUNK):
    return pl.ds(pl.multiple_of(step * size, size), size)


def slabs_of(step, size=CHUNK // 8):
    return pl.ds(step * size, size)


def mean_of(x):
    return jnp.sum(x, -1, keepdims=True) * (1.0 / D)


def normalize(x):
    center = x - mean_of(x)
    inverse = lax.rsqrt(mean_of(center * center) + 1e-06)
    return center, inverse


def project(src, w, q, k, v):
    x = src[...]
    q[...] = dot_nt(x, w[0:PAD, :]).astype(BF16)
    k[...] = dot_nt(x, w[HD : HD + PAD, :]).astype(BF16)
    v[:, 512:PAD] = jnp.zeros((N, 128), BF16)
    v[:, 0:HD] = dot_nt(x, w[D : 3 * HD, :]).astype(BF16)


def forward_heads(q, k, v, weights, acc, keep):
    for head in range(HEADS):
        offset, cut, wide = window(head)
        mine = head_mask(offset, wide)
        queries = jnp.where(mine, q[:, cut].astype(F32), 0.0).astype(BF16)
        p = jnp.exp(dot_nt(queries, k[:, cut]) * FACTOR)
        if keep is not None:
            p = jnp.where(keep, p, 0.0)
        w = (p * (1.0 / jnp.sum(p, -1, keepdims=True))).astype(BF16)
        weights[head] = w
        out = dot(w, v[:, cut])
        acc[:, cut] = out if head == 0 else jnp.where(mine, out, acc[:, cut])


def backward_heads(q, k, v, weights, grad, accq, acck, accv):
    for head in range(HEADS):
        offset, cut, wide = window(head)
        mine = head_mask(offset, wide)
        g = grad[:, cut]
        w = weights[head]
        e = dot_nt(jnp.where(mine, g.astype(F32), 0.0).astype(BF16), v[:, cut])
        p = w.astype(F32)
        r = (p * (e - jnp.sum(e * p, -1, keepdims=True)) * FACTOR).astype(BF16)
        for acc, out in ((accv, dot_tn(w, g)), (accq, dot(r, k[:, cut])), (acck, dot_tn(r, q[:, cut]))):
            acc[:, cut] = out if head == 0 else jnp.where(mine, out, acc[:, cut])


def join(nat, accq, acck, accv):
    lane = lax.broadcasted_iota(jnp.int32, (N, 128), 1)
    moved = pltpu.roll(acck[...], 64, 1)
    nat[:, 0:512] = accq[:, 0:512].astype(BF16)
    nat[:, 512:640] = jnp.where(lane < 64, accq[:, 512:640], moved[:, 0:128]).astype(BF16)
    nat[:, 640:1152] = moved[:, 128:640].astype(BF16)
    nat[:, 1152:1664] = accv[:, 0:512].astype(BF16)
    nat[:, 1664:1792] = jnp.where(lane < 64, accv[:, 512:640], 0.0).astype(BF16)


def kernel(vid_hbm, wsi_hbm, wso_hbm, wti_hbm, wto_hbm, cot_hbm, o_out, o_gv, o_gi, o_go, names, *refs):
    r = dict(zip(names, refs))
    seq = lax.axis_index("seq")
    dp = lax.axis_index("dp")
    z, y_hi, core = seq // 4, seq // 2 % 2, seq % 2
    x, y_lo = dp // 2, dp % 2
    y = y_hi * 2 + y_lo

    def at_seq(s):
        return {"seq": s, "dp": dp}

    def at_x(to):
        return {"seq": seq, "dp": to * 2 + y_lo}

    def at_y(to):
        return {"seq": z * 4 + to // 2 * 2 + core, "dp": x * 2 + to % 2}

    loads = []
    for i, (src, dst) in enumerate(
        ((vid_hbm, "vid"), (cot_hbm, "cot"), (wto_hbm, "wto"), (wsi_hbm, "wsi"), (wso_hbm, "wso"), (wti_hbm, "wti"))
    ):
        copy = pltpu.make_async_copy(src, r[dst], r["load"].at[i])
        copy.start()
        loads.append(copy)

    barrier = pltpu.get_barrier_semaphore()

    def greet(k, carry):
        pl.semaphore_signal(barrier, inc=1, device_id=at_seq(lax.rem(seq + k, 32)), device_id_type=MESH)
        return carry

    lax.fori_loop(1, 32, greet, 0)
    for step in (1, 3):
        pl.semaphore_signal(barrier, inc=1, device_id=at_x((x + step) % 4), device_id_type=MESH)
        pl.semaphore_signal(barrier, inc=1, device_id=at_y((y + step) % 4), device_id_type=MESH)

    def slab_copy(which, send, recv, to):
        return remote(
            "swap",
            src_ref=send.at[to],
            dst_ref=recv.at[seq],
            send_sem=r["a_send"].at[which],
            recv_sem=r["a_recv"].at[which],
            device_id=at_seq(to),
            device_id_type=MESH,
        )

    def exchange(which, send, recv):
        def one(i, carry):
            k = 16 + (i + 1) // 2 * (1 - 2 * (i % 2))
            slab_copy(which, send, recv, lax.rem(seq + k, 32)).start()
            return carry

        lax.fori_loop(0, 31, one, 0)
        recv[seq] = send[seq]

    def wait_exchange(which, recv):
        drain("swap", recv.at[pl.ds(0, 31)], r["a_recv"].at[which])

    def wait_sent(which, send):
        drain("swap", send.at[pl.ds(0, 31)], r["a_send"].at[which])

    loads[0].wait()

    def norm_video(i, carry):
        rows = rows_of(i)
        v = r["vid"][rows, :].astype(F32)
        mean = mean_of(v)
        center = v - mean
        inverse = lax.rsqrt(mean_of(center * center) + 1e-06)
        r["s_mean"][rows, :] = jnp.broadcast_to(mean, (CHUNK, 128))
        r["s_inv"][rows, :] = jnp.broadcast_to(inverse, (CHUNK, 128))
        r["sh"][rows, :] = (center * inverse).astype(BF16)
        return carry

    lax.fori_loop(0, N // CHUNK, norm_video, 0, unroll=2)
    loads[1].wait()
    loads[2].wait()
    ga = dot_nt(r["cot"][...], r["wto"][...])
    r["ga_send"][...] = ga.reshape(32, 8, HD).astype(BF16)
    pl.semaphore_wait(barrier, 35)
    exchange(0, r["ga_send"], r["ga_recv"])

    loads[3].wait()
    project(r["sh"], r["wsi"], r["sq"], r["sk"], r["sv"])
    forward_heads(r["sq"], r["sk"], r["sv"], r["sw"], r["acc"], None)
    r["small"][...] = r["acc"][...].astype(BF16)
    loads[4].wait()
    for n in range(0, D, 384):
        r["big"][:, n : n + 384] = dot(r["small"][:, 0:HD], r["wso"][:, n : n + 384])

    def norm_residual(step, carry):
        i = lax.rem(z + 4 + (step + 1) // 2 * (1 - 2 * (step % 2)), 8)
        rows = rows_of(i)
        v = (r["vid"][rows, :].astype(F32) + r["big"][rows, :]).astype(BF16)
        r["res"][rows, :] = v
        v = v.astype(F32)
        mean = mean_of(v)
        center = v - mean
        inverse = lax.rsqrt(mean_of(center * center) + 1e-06)
        r["t_mean"][rows, :] = jnp.broadcast_to(mean, (CHUNK, 128))
        r["t_inv"][rows, :] = jnp.broadcast_to(inverse, (CHUNK, 128))
        r["h_send"][slabs_of(i)] = (center * inverse).reshape(CHUNK // 8, 8, D).astype(BF16)
        for j in range(4):
            to = i * 4 + lax.rem(seq + 2 + j, 4)

            @pl.when(to != seq)
            def _():
                slab_copy(1, r["h_send"], r["h_recv"], to).start()

        return carry

    lax.fori_loop(0, N // CHUNK, norm_residual, 0)
    r["h_recv"][seq] = r["h_send"][seq]

    for b in range(8):
        part = r["cot"][:, 128 * b : 128 * b + 256].astype(F32)
        if b:
            part = pltpu.roll(part, 256 - 16 * b, 1)
        r["cpad"][b] = part.astype(BF16)
    loads[5].wait()

    wait_exchange(0, r["ga_recv"])
    r["small"][:, 512:PAD] = jnp.zeros((N, 128), BF16)
    r["small"][:, 0:HD] = r["ga_recv"][...].astype(F32).reshape(N, HD).astype(BF16)
    wait_exchange(1, r["h_recv"])

    def take_h(i, carry):
        v = r["h_recv"][slabs_of(i)].astype(F32).reshape(CHUNK, D)
        r["th"][rows_of(i), :] = v.astype(BF16)
        return carry

    lax.fori_loop(0, N // CHUNK, take_h, 0)
    project(r["th"], r["wti"], r["tq"], r["tk"], r["tv"])
    place = lax.broadcasted_iota(jnp.int32, (N, N), 0) % 8
    other = lax.broadcasted_iota(jnp.int32, (N, N), 1) % 8
    forward_heads(r["tq"], r["tk"], r["tv"], r["tw"], r["acc"], place == other)
    r["at_send"][...] = r["acc"][:, 0:HD].reshape(32, 8, HD).astype(BF16)
    exchange(2, r["at_send"], r["at_recv"])

    backward_heads(r["tq"], r["tk"], r["tv"], r["tw"], r["small"], r["accq"], r["acck"], r["accv"])
    join(r["nat"], r["accq"], r["acck"], r["accv"])
    for n in range(0, D, 384):
        r["big"][:, n : n + 384] = dot(r["nat"][:, 0 : 3 * HD], r["wti"][:, n : n + 384])

    def give_gh(i, carry):
        r["gh_send"][slabs_of(i)] = r["big"][rows_of(i), :].reshape(CHUNK // 8, 8, D).astype(BF16)
        return carry

    lax.fori_loop(0, N // CHUNK, give_gh, 0)
    exchange(3, r["gh_send"], r["gh_recv"])

    r["turn"][...] = r["th"][...].astype(F32).T
    for ab in range(2):
        for c in range(2):
            for hi in range(2):
                pieces = []
                for zz in range(4 * ab, 4 * ab + 4):
                    first = zz * 144 + hi * 72 + c * 36
                    pieces.append(r["turn"][first : first + 36, :])
                low = ab * 576 + c * 288 + hi * 144
                r["h_t"][low : low + 144, :] = jnp.concatenate(pieces, 0).astype(BF16)
    for b in range(8):
        low = 216 * b // 128 * 128
        off = 216 * b - low
        part = r["nat"][:, low : low + 384].astype(F32)
        if off:
            part = pltpu.roll(part, 384 - off, 1)
        r["gpad"][b] = part[:, 0:256].astype(BF16)

    parts = (r["part_in"], r["part_out"])
    c_recv = (r["c_recv_in"], r["c_recv_out"])
    one_recv = (r["one_in"], r["one_out"])
    two_recv = (r["two_in"], r["two_out"])
    mid = (r["mid_in"], r["mid_out"])
    three_recv = (r["three_in"], r["three_out"])
    four_recv = (r["four_in"], r["four_out"])
    turns = (2, 1, 3, 0)
    both = ((0, 0), (1, 0), (0, 1), (1, 1))

    def places(first, ab):
        if (ab == 0) == first:
            return x, at_x
        return y, at_y

    def target(ab, k):
        me, _ = places(True, ab)
        return (me + turns[k]) % 4

    def core_copy(w, ab, k):
        to = target(ab, k)
        return remote(
            "core",
            src_ref=parts[w].at[1 - core, ab, to], dst_ref=c_recv[w].at[ab, to],
            send_sem=r["c_ssem"].at[w, ab, k], recv_sem=r["c_rsem"].at[w, ab, k],
            device_id=at_seq(seq + 1 - 2 * core), device_id_type=MESH,
        )

    def one_copy(w, ab, way):
        me, where = places(True, ab)
        to = (me + (1, 3)[way]) % 4
        return remote(
            "one",
            src_ref=parts[w].at[core, ab, (me + 2) % 4, pl.ds(2 * way, 2)], dst_ref=one_recv[w].at[ab, way],
            send_sem=r["one_ssem"].at[w, ab, way], recv_sem=r["one_rsem"].at[w, ab, way],
            device_id=where(to), device_id_type=MESH,
        )

    def two_copy(w, ab, way, late):
        me, where = places(True, ab)
        to = (me + (1, 3)[way]) % 4
        low = 2 * way if late else 2 - 2 * way
        return remote(
            "two",
            src_ref=parts[w].at[core, ab, to, pl.ds(low, 2)], dst_ref=two_recv[w].at[ab, way, pl.ds(low, 2)],
            send_sem=r["two_ssem"].at[w, ab, way, late], recv_sem=r["two_rsem"].at[w, ab, way, late],
            device_id=where(to), device_id_type=MESH,
        )

    def three_copy(w, ab, way):
        me, where = places(False, ab)
        to = (me + (1, 3)[way]) % 4
        return remote(
            "three",
            src_ref=mid[w].at[ab, (me + 2) % 4, way], dst_ref=three_recv[w].at[ab, way],
            send_sem=r["three_ssem"].at[w, ab, way], recv_sem=r["three_rsem"].at[w, ab, way],
            device_id=where(to), device_id_type=MESH,
        )

    def four_copy(w, ab, way, late):
        me, where = places(False, ab)
        to = (me + (1, 3)[way]) % 4
        half = way if late else 1 - way
        return remote(
            "four",
            src_ref=mid[w].at[ab, to, half], dst_ref=four_recv[w].at[ab, way, half],
            send_sem=r["four_ssem"].at[w, ab, way, late], recv_sem=r["four_rsem"].at[w, ab, way, late],
            device_id=where(to), device_id_type=MESH,
        )

    def add_in(dst, dst_at, src, src_at):
        dst[dst_at] = (dst[dst_at].astype(F32) + src[src_at].astype(F32)).astype(BF16)

    lane8 = lax.broadcasted_iota(jnp.int32, (8, 128), 1) // 16

    def store(w, ab, slot, value):
        if w == 0:
            for half in range(2):
                parts[0][slot + (half,)] = value[:, half * 128 : half * 128 + 128].astype(BF16)
            return
        tail = value[:, 128:256]
        packed = tail[0:8, :]
        for g in range(1, 8):
            packed = jnp.where(lane8 == g, pltpu.roll(tail[8 * g : 8 * g + 8, :], 16 * g, 1), packed)
        parts[1][slot + (0,)] = value[0:48, 0:128].astype(BF16)
        rest = [value[48:72, 0:128], packed, tail[64:72, :], jnp.zeros((8, 128), F32)]
        parts[1][slot + (1,)] = jnp.concatenate(rest, 0).astype(BF16)

    def fill(w, ab, at):
        left, right, size = ((r["h_t"], r["gpad"], 144), (r["att_t"], r["cpad"], 72))[w]
        for i in range(2 if ab == 0 else 4):
            xx, lo = (at, i) if ab == 0 else (i, at)
            value = dot(left[ab * 4 * size : ab * 4 * size + 4 * size, :], right[2 * xx + lo])
            for c in range(2):
                for hi in range(2):
                    yy = hi * 2 + lo
                    slot = (c, 0, xx, yy) if ab == 0 else (c, 1, yy, xx)
                    low = size * (c * 2 + hi)
                    store(w, ab, slot, value[low : low + size, :])

    def core_add(w, ab, k):
        core_copy(w, ab, k).wait_recv()
        to = target(ab, k)
        for j in range(4):
            add_in(parts[w], (core, ab, to, j), c_recv[w], (ab, to, j))
        if k == 0:
            one_copy(w, ab, 0).start()
            one_copy(w, ab, 1).start()
        elif k < 3:
            two_copy(w, ab, k - 1, 0).start()

    def pass_on(w, ab, way):
        one_copy(w, ab, way).wait_recv()
        me, _ = places(True, ab)
        to = (me + (1, 3)[way]) % 4
        for j in range(2):
            add_in(parts[w], (core, ab, to, 2 * way + j), one_recv[w], (ab, way, j))
        two_copy(w, ab, way, 1).start()

    def second_ring(w, ab):
        for way in range(2):
            for late in range(2):
                two_copy(w, ab, way, late).wait_recv()
        me, _ = places(True, ab)
        for j in range(4):
            mid[w][ab, j] = (
                parts[w][core, ab, me, j].astype(F32)
                + two_recv[w][ab, 0, j].astype(F32)
                + two_recv[w][ab, 1, j].astype(F32)
            ).astype(BF16)
        for way in range(2):
            three_copy(w, ab, way).start()
        for way in range(2):
            four_copy(w, ab, way, 0).start()

    def pass_on_again(w, ab, way):
        three_copy(w, ab, way).wait_recv()
        me, _ = places(False, ab)
        add_in(mid[w], (ab, (me + (1, 3)[way]) % 4, way), three_recv[w], (ab, way))
        four_copy(w, ab, way, 1).start()

    def ring_sum(w, ab, half):
        me, _ = places(False, ab)
        return (
            mid[w][ab, me, half].astype(F32)
            + four_recv[w][ab, 0, half].astype(F32)
            + four_recv[w][ab, 1, half].astype(F32)
        )

    def ring_wait(w, ab):
        for way in range(2):
            for late in range(2):
                four_copy(w, ab, way, late).wait_recv()

    fill(0, 0, target(0, 0))
    core_copy(0, 0, 0).start()
    fill(0, 1, y_lo)
    core_copy(0, 1, 0).start()
    core_add(0, 0, 0)
    fill(0, 0, target(0, 1))
    core_copy(0, 0, 1).start()
    core_add(0, 1, 0)
    fill(0, 1, 1 - y_lo)
    core_copy(0, 1, 1).start()
    core_copy(0, 1, 2).start()
    fill(0, 0, target(0, 2))
    core_copy(0, 0, 2).start()
    fill(0, 0, target(0, 3))
    core_copy(0, 0, 3).start()
    core_copy(0, 1, 3).start()
    for k in (1, 2):
        core_add(0, 0, k)
        core_add(0, 1, k)

    wait_exchange(2, r["at_recv"])
    r["acc"][:, 0:HD] = r["at_recv"][...].astype(F32).reshape(N, HD)
    r["small"][:, 0:HD] = r["acc"][:, 0:HD].astype(BF16)
    r["turn"][0:HD, :] = r["acc"][:, 0:HD].T
    for ab in range(2):
        for c in range(2):
            pieces = []
            for hi in range(2):
                for zz in range(4 * ab, 4 * ab + 4):
                    first = zz * 72 + hi * 36 + c * 18
                    pieces.append(r["turn"][first : first + 18, :])
            low = ab * 288 + c * 144
            r["att_t"][low : low + 144, :] = jnp.concatenate(pieces, 0).astype(BF16)
    fill(1, 0, target(0, 0))
    core_copy(1, 0, 0).start()
    fill(1, 1, y_lo)
    core_copy(1, 1, 0).start()
    for k in range(1, 4):
        fill(1, 0, target(0, k))
        core_copy(1, 0, k).start()
    fill(1, 1, 1 - y_lo)
    for k in range(1, 4):
        core_copy(1, 1, k).start()
    for ab, way in both:
        pass_on(0, ab, way)
    for k in range(3):
        core_add(1, 0, k)
        core_add(1, 1, k)
    for w in range(2):
        for ab in range(2):
            core_add(w, ab, 3)

    for n in range(0, D, 384):
        o_out[:, n : n + 384] = (
            r["res"][:, n : n + 384].astype(F32) + dot(r["small"][:, 0:HD], r["wto"][:, n : n + 384])
        ).astype(BF16)

    for ab, way in both:
        pass_on(1, ab, way)

    for ab in range(2):
        second_ring(0, ab)
    wait_exchange(3, r["gh_recv"])

    def norm_back_residual(i, carry):
        rows = rows_of(i)
        g = r["gh_recv"][slabs_of(i)].astype(F32).reshape(CHUNK, D)
        inverse = r["t_inv"][rows, 0:1]
        n = (r["res"][rows, :].astype(F32) - r["t_mean"][rows, 0:1]) * inverse
        back = inverse * (g - mean_of(g) - n * mean_of(g * n))
        r["res"][rows, :] = (r["cot"][rows, :].astype(F32) + back).astype(BF16)
        return carry

    lax.fori_loop(0, N // CHUNK, norm_back_residual, 0, unroll=2)
    r["small"][:, 0:HD] = dot_nt(r["res"][...], r["wso"][...]).astype(BF16)
    for ab, way in both:
        pass_on_again(0, ab, way)
    for ab in range(2):
        second_ring(1, ab)
    backward_heads(r["sq"], r["sk"], r["sv"], r["sw"], r["small"], r["accq"], r["acck"], r["accv"])
    for ab, way in both:
        pass_on_again(1, ab, way)
    for ab in range(2):
        ring_wait(0, ab)
        for half in range(2):
            r["zsum"][ab, half, 0:144] = ring_sum(0, ab, half)
    join(r["nat"], r["accq"], r["acck"], r["accv"])
    for ab in range(2):
        ring_wait(1, ab)
        first, rest = ring_sum(1, ab, 0), ring_sum(1, ab, 1)
        r["zsum"][ab, 0, 144:192] = first
        r["zsum"][ab, 0, 192:216] = rest[0:24, :]
        for g in range(8):
            tail = rest[24:32, :]
            r["zsum"][ab, 1, 144 + 8 * g : 152 + 8 * g] = pltpu.roll(tail, 128 - 16 * g, 1) if g else tail
        r["zsum"][ab, 1, 208:216] = rest[32:40, :]
        for half in range(2):
            for j in range(4):
                piece = jnp.concatenate(
                    [
                        r["zsum"][ab, half, 36 * j : 36 * j + 36, :],
                        r["zsum"][ab, half, 144 + 18 * j : 144 + 18 * j + 18, :],
                        jnp.zeros((ZROWS - 54, 128), F32),
                    ],
                    0,
                )
                r["z_send"][4 * ab + j, half] = piece.astype(BF16)

    def z_one(k, carry):
        to = lax.rem(z + k, 8)
        remote(
            "z",
            src_ref=r["z_send"].at[to], dst_ref=r["z_recv"].at[z], send_sem=r["z_ssem"], recv_sem=r["z_rsem"],
            device_id=at_seq(to * 4 + y_hi * 2 + core), device_id_type=MESH,
        ).start()
        return carry

    lax.fori_loop(1, 8, z_one, 0)
    r["z_recv"][z] = r["z_send"][z]

    for n in range(0, D, 384):
        r["big"][:, n : n + 384] = dot(r["nat"][:, 0 : 3 * HD], r["wsi"][:, n : n + 384])

    def norm_back_video(i, carry):
        rows = rows_of(i)
        g = r["big"][rows, :]
        inverse = r["s_inv"][rows, 0:1]
        n = (r["vid"][rows, :].astype(F32) - r["s_mean"][rows, 0:1]) * inverse
        back = inverse * (g - mean_of(g) - n * mean_of(g * n))
        o_gv[rows, :] = (r["res"][rows, :].astype(F32) + back).astype(BF16)
        return carry

    lax.fori_loop(0, N // CHUNK, norm_back_video, 0, unroll=2)

    drain("z", r["z_recv"].at[pl.ds(0, 7)], r["z_rsem"])
    for half in range(2):
        total = r["z_recv"][0, half].astype(F32)
        for j in range(1, 8):
            total = total + r["z_recv"][j, half].astype(F32)
        if half == 0:
            o_gi[:, 0:128] = total[0:36, :]
            o_go[:, 0:128] = total[36:54, :]
        else:
            o_gi[:, 128:216] = total[0:36, 0:88]
            o_go[:, 128:144] = total[36:54, 0:16]

    for which, name in enumerate(("ga_send", "h_send", "at_send", "gh_send")):
        wait_sent(which, r[name])
    for w in range(2):
        for ab in range(2):
            for k in range(4):
                core_copy(w, ab, k).wait_send()
            for way in range(2):
                one_copy(w, ab, way).wait_send()
                three_copy(w, ab, way).wait_send()
                for late in range(2):
                    two_copy(w, ab, way, late).wait_send()
                    four_copy(w, ab, way, late).wait_send()
    drain("z", r["z_send"].at[pl.ds(0, 7)], r["z_ssem"])


def hand_over(*refs):
    for source, result in zip(refs[:4], refs[4:]):
        result[...] = source[...]


def local(video, spatial_in, spatial_out, temporal_in, temporal_out, cotangent):
    shapes = scratch_shapes()
    names = tuple(shapes)
    anywhere = pl.BlockSpec(memory_space=pl.ANY)
    whole = pl.BlockSpec(memory_space=pltpu.VMEM)

    def body(*refs):
        kernel(*refs[:10], names, *refs[10:])

    results = (
        jax.ShapeDtypeStruct((N, D), BF16),
        jax.ShapeDtypeStruct((N, D), BF16),
        jax.ShapeDtypeStruct((36, 216), F32),
        jax.ShapeDtypeStruct((18, 144), F32),
    )
    held = pl.pallas_call(
        body,
        out_shape=results,
        in_specs=[anywhere] * 6,
        out_specs=(whole,) * 4,
        scratch_shapes=list(shapes.values()),
        compiler_params=pltpu.CompilerParams(
            collective_id=0, has_side_effects=True, vmem_limit_bytes=60 * 1024 * 1024
        ),
        cost_estimate=pl.CostEstimate(flops=9_000_000_000, bytes_accessed=13_000_000, transcendentals=1_100_000),
    )(video.reshape(N, D), spatial_in.T, spatial_out, temporal_in.T, temporal_out, cotangent.reshape(N, D))
    out, grad_video, grad_in, grad_out = pl.pallas_call(
        hand_over,
        out_shape=results,
        in_specs=[whole] * 4,
        out_specs=(whole,) * 4,
        cost_estimate=pl.CostEstimate(flops=0, bytes_accessed=2_400_000, transcendentals=0),
    )(*held)
    return (out.reshape(video.shape), grad_video.reshape(video.shape), grad_in, grad_out)


def solution(mesh):
    in_specs = (P("dp", "seq", None, None), P(), P(), P(), P(), P("dp", "seq", None, None))
    out_specs = (
        P("dp", "seq", None, None),
        P("dp", "seq", None, None),
        P("seq", "dp"),
        P("seq", "dp"),
    )
    return jax.shard_map(local, mesh=mesh, in_specs=in_specs, out_specs=out_specs, check_vma=False)
```

```python
import jax
import jax.numpy as jnp
from jax import lax
from jax.experimental import pallas as pl
from jax.experimental.pallas import tpu as pltpu
from jax.sharding import PartitionSpec as P

HEADS = 8
HEAD = 72
D = 1152
HD = 576
N = 256
PAD = 640
FACTOR = HEAD ** (-0.5)
F32 = jnp.float32
BF16 = jnp.bfloat16
MESH = pl.DeviceIdType.MESH
CHUNK = 32


def dot(a, b):
    return jnp.dot(a, b, preferred_element_type=F32)


def dot_nt(a, b):
    return lax.dot_general(a, b, (((1,), (1,)), ((), ())), preferred_element_type=F32)


def dot_tn(a, b):
    return lax.dot_general(a, b, (((0,), (0,)), ((), ())), preferred_element_type=F32)


def remote(kind, **ends):
    return pltpu.make_async_remote_copy(**ends)


def drain(kind, some, sem):
    pltpu.make_async_copy(some, some, sem).wait()


def window(head):
    start = head * HEAD
    low = start // 128 * 128
    wide = 128 if start + HEAD <= low + 128 else 256
    return start - low, slice(low, low + wide), wide


def head_mask(offset, wide):
    lane = lax.broadcasted_iota(jnp.int32, (N, wide), 1)
    return (lane >= offset) & (lane < offset + HEAD)


def scratch_shapes():
    slab, thin = (2, 144, 128), (2, 48, 128)
    vm = lambda *shape: pltpu.VMEM(shape, BF16)
    vf = lambda *shape: pltpu.VMEM(shape, F32)
    dma = pltpu.SemaphoreType.DMA
    return dict(
        vid=vm(N, D), cot=vm(N, D), wsi=vm(3 * HD, D), wso=vm(HD, D), wti=vm(3 * HD, D), wto=vm(HD, D),
        ga_send=vm(32, 8, HD), ga_recv=vm(32, 8, HD), h_send=vm(32, 8, D), h_recv=vm(32, 8, D),
        at_send=vm(32, 8, HD), at_recv=vm(32, 8, HD), gh_send=vm(32, 8, D), gh_recv=vm(32, 8, D),
        sh=vm(N, D), sq=vm(N, PAD), sk=vm(N, PAD), sv=vm(N, PAD), sw=vm(HEADS, N, N),
        th=vm(N, D), tq=vm(N, PAD), tk=vm(N, PAD), tv=vm(N, PAD), tw=vm(HEADS, N, N),
        acc=vf(N, PAD), accq=vf(N, PAD), acck=vf(N, PAD), accv=vf(N, PAD),
        small=vm(N, PAD), nat=vm(N, 1792), big=vf(N, D),
        res=vm(N, D), gres=vm(N, D), att=vm(N, HD), s_mean=vf(N, 128), s_inv=vf(N, 128), t_mean=vf(N, 128), t_inv=vf(N, 128),
        turn=vf(D, N), h_t=vm(D, N), att_t=vm(HD, N),
        gpad=vm(8, N, 256), cpad=vm(8, N, 256),
        part_in=vm(2, 2, 4, 4, *slab), part_out=vm(2, 2, 4, 4, *thin),
        c_recv_in=vm(2, 4, 4, *slab), c_recv_out=vm(2, 4, 4, *thin),
        one_in=vm(2, 2, 2, *slab), one_out=vm(2, 2, 2, *thin), two_in=vm(2, 2, 4, *slab), two_out=vm(2, 2, 4, *thin),
        mid_in=vm(2, 4, *slab), mid_out=vm(2, 4, *thin),
        three_in=vm(2, 2, *slab[1:]), three_out=vm(2, 2, *thin[1:]), four_in=vm(2, 2, *slab), four_out=vm(2, 2, *thin),
        zsum=vf(2, 2, 216, 128), z_send_in=vm(8, 2, 40, 128), z_recv_in=vm(8, 2, 40, 128),
        z_send_out=vm(8, 2, 24, 128), z_recv_out=vm(8, 2, 24, 128),
        load=dma((6,)), a_send=dma((4,)), a_recv=dma((4,)), c_ssem=dma((2, 2, 4)), c_rsem=dma((2, 2, 4)),
        one_ssem=dma((2, 2, 2)), one_rsem=dma((2, 2, 2)), two_ssem=dma((2, 2, 2, 2)), two_rsem=dma((2, 2, 2, 2)),
        three_ssem=dma((2, 2, 2)), three_rsem=dma((2, 2, 2)), four_ssem=dma((2, 2, 2, 2)), four_rsem=dma((2, 2, 2, 2)),
        z_ssem=dma((2,)), z_rsem=dma((2,)),
    )


def rows_of(step, size=CHUNK):
    return pl.ds(pl.multiple_of(step * size, size), size)


def slabs_of(step, size=CHUNK // 8):
    return pl.ds(step * size, size)


def mean_of(x):
    return jnp.sum(x, -1, keepdims=True) * (1.0 / D)


def normalize(x):
    center = x - mean_of(x)
    inverse = lax.rsqrt(mean_of(center * center) + 1e-06)
    return center, inverse


def project(src, w, q, k, v):
    x = src[...]
    q[...] = dot_nt(x, w[0:PAD, :]).astype(BF16)
    k[...] = dot_nt(x, w[HD : HD + PAD, :]).astype(BF16)
    v[:, 512:PAD] = jnp.zeros((N, 128), BF16)
    v[:, 0:HD] = dot_nt(x, w[D : 3 * HD, :]).astype(BF16)


def forward_heads(q, k, v, weights, acc, keep):
    for head in range(HEADS):
        offset, cut, wide = window(head)
        mine = head_mask(offset, wide)
        queries = jnp.where(mine, q[:, cut].astype(F32), 0.0).astype(BF16)
        p = jnp.exp(dot_nt(queries, k[:, cut]) * FACTOR)
        if keep is not None:
            p = jnp.where(keep, p, 0.0)
        w = (p * (1.0 / jnp.sum(p, -1, keepdims=True))).astype(BF16)
        weights[head] = w
        out = dot(w, v[:, cut])
        acc[:, cut] = out if head == 0 else jnp.where(mine, out, acc[:, cut])


def backward_heads(q, k, v, weights, grad, accq, acck, accv):
    for head in range(HEADS):
        offset, cut, wide = window(head)
        mine = head_mask(offset, wide)
        g = grad[:, cut]
        w = weights[head]
        e = dot_nt(jnp.where(mine, g.astype(F32), 0.0).astype(BF16), v[:, cut])
        p = w.astype(F32)
        r = (p * (e - jnp.sum(e * p, -1, keepdims=True)) * FACTOR).astype(BF16)
        for acc, out in ((accv, dot_tn(w, g)), (accq, dot(r, k[:, cut])), (acck, dot_tn(r, q[:, cut]))):
            acc[:, cut] = out if head == 0 else jnp.where(mine, out, acc[:, cut])


def join(nat, accq, acck, accv):
    lane = lax.broadcasted_iota(jnp.int32, (N, 128), 1)
    moved = pltpu.roll(acck[...], 64, 1)
    nat[:, 0:512] = accq[:, 0:512].astype(BF16)
    nat[:, 512:640] = jnp.where(lane < 64, accq[:, 512:640], moved[:, 0:128]).astype(BF16)
    nat[:, 640:1152] = moved[:, 128:640].astype(BF16)
    nat[:, 1152:1664] = accv[:, 0:512].astype(BF16)
    nat[:, 1664:1792] = jnp.where(lane < 64, accv[:, 512:640], 0.0).astype(BF16)


def kernel(vid_hbm, wsi_hbm, wso_hbm, wti_hbm, wto_hbm, cot_hbm, o_out, o_gv, o_gi, o_go, names, *refs):
    r = dict(zip(names, refs))
    seq = lax.axis_index("seq")
    dp = lax.axis_index("dp")
    z, y_hi, core = seq // 4, seq // 2 % 2, seq % 2
    x, y_lo = dp // 2, dp % 2
    y = y_hi * 2 + y_lo

    def at_seq(s):
        return {"seq": s, "dp": dp}

    def at_x(to):
        return {"seq": seq, "dp": to * 2 + y_lo}

    def at_y(to):
        return {"seq": z * 4 + to // 2 * 2 + core, "dp": x * 2 + to % 2}

    loads = []
    for i, (src, dst) in enumerate(
        ((cot_hbm, "cot"), (wto_hbm, "wto"), (vid_hbm, "vid"), (wsi_hbm, "wsi"), (wso_hbm, "wso"), (wti_hbm, "wti"))
    ):
        copy = pltpu.make_async_copy(src, r[dst], r["load"].at[i])
        copy.start()
        loads.append(copy)

    barrier = pltpu.get_barrier_semaphore()

    def greet(k, carry):
        pl.semaphore_signal(barrier, inc=1, device_id=at_seq(lax.rem(seq + k, 32)), device_id_type=MESH)
        return carry

    lax.fori_loop(1, 32, greet, 0)
    for step in (1, 3):
        pl.semaphore_signal(barrier, inc=1, device_id=at_x((x + step) % 4), device_id_type=MESH)
        pl.semaphore_signal(barrier, inc=1, device_id=at_y((y + step) % 4), device_id_type=MESH)

    def slab_copy(which, send, recv, to):
        return remote(
            "swap",
            src_ref=send.at[to],
            dst_ref=recv.at[seq],
            send_sem=r["a_send"].at[which],
            recv_sem=r["a_recv"].at[which],
            device_id=at_seq(to),
            device_id_type=MESH,
        )

    def send_chunk(which, send, recv, i):
        for j in range(4):
            to = i * 4 + lax.rem(seq + 2 + j, 4)

            @pl.when(to != seq)
            def _():
                slab_copy(which, send, recv, to).start()

    def exchange(which, send, recv):
        def one(i, carry):
            k = 16 + (i + 1) // 2 * (1 - 2 * (i % 2))
            slab_copy(which, send, recv, lax.rem(seq + k, 32)).start()
            return carry

        lax.fori_loop(0, 31, one, 0)
        recv[seq] = send[seq]

    def wait_exchange(which, recv):
        drain("swap", recv.at[pl.ds(0, 31)], r["a_recv"].at[which])

    def wait_sent(which, send):
        drain("swap", send.at[pl.ds(0, 31)], r["a_send"].at[which])

    loads[0].wait()
    loads[1].wait()
    ga = dot_nt(r["cot"][...], r["wto"][...])
    r["ga_send"][...] = ga.reshape(32, 8, HD).astype(BF16)
    pl.semaphore_wait(barrier, 35)
    exchange(0, r["ga_send"], r["ga_recv"])

    loads[2].wait()

    def norm_video(i, carry):
        rows = rows_of(i)
        v = r["vid"][rows, :].astype(F32)
        mean = mean_of(v)
        center = v - mean
        inverse = lax.rsqrt(mean_of(center * center) + 1e-06)
        r["s_mean"][rows, :] = jnp.broadcast_to(mean, (CHUNK, 128))
        r["s_inv"][rows, :] = jnp.broadcast_to(inverse, (CHUNK, 128))
        r["sh"][rows, :] = (center * inverse).astype(BF16)
        return carry

    lax.fori_loop(0, N // CHUNK, norm_video, 0, unroll=2)
    loads[3].wait()
    project(r["sh"], r["wsi"], r["sq"], r["sk"], r["sv"])
    forward_heads(r["sq"], r["sk"], r["sv"], r["sw"], r["acc"], None)
    r["small"][...] = r["acc"][...].astype(BF16)
    loads[4].wait()
    for n in range(0, D, 384):
        r["big"][:, n : n + 384] = dot(r["small"][:, 0:HD], r["wso"][:, n : n + 384])

    def norm_residual(step, carry):
        i = lax.rem(z + 4 + (step + 1) // 2 * (1 - 2 * (step % 2)), 8)
        rows = rows_of(i)
        v = (r["vid"][rows, :].astype(F32) + r["big"][rows, :]).astype(BF16)
        r["res"][rows, :] = v
        v = v.astype(F32)
        mean = mean_of(v)
        center = v - mean
        inverse = lax.rsqrt(mean_of(center * center) + 1e-06)
        r["t_mean"][rows, :] = jnp.broadcast_to(mean, (CHUNK, 128))
        r["t_inv"][rows, :] = jnp.broadcast_to(inverse, (CHUNK, 128))
        r["h_send"][slabs_of(i)] = (center * inverse).reshape(CHUNK // 8, 8, D).astype(BF16)
        send_chunk(1, r["h_send"], r["h_recv"], i)
        return carry

    lax.fori_loop(0, N // CHUNK, norm_residual, 0)
    r["h_recv"][seq] = r["h_send"][seq]

    for b in range(8):
        part = r["cot"][:, 128 * b : 128 * b + 256].astype(F32)
        if b:
            part = pltpu.roll(part, 256 - 16 * b, 1)
        r["cpad"][b] = part.astype(BF16)
    loads[5].wait()

    wait_exchange(0, r["ga_recv"])
    r["small"][:, 512:PAD] = jnp.zeros((N, 128), BF16)
    r["small"][:, 0:HD] = r["ga_recv"][...].astype(F32).reshape(N, HD).astype(BF16)
    wait_exchange(1, r["h_recv"])

    def take_h(i, carry):
        v = r["h_recv"][slabs_of(i)].astype(F32).reshape(CHUNK, D)
        r["th"][rows_of(i), :] = v.astype(BF16)
        return carry

    lax.fori_loop(0, N // CHUNK, take_h, 0)
    project(r["th"], r["wti"], r["tq"], r["tk"], r["tv"])
    place = lax.broadcasted_iota(jnp.int32, (N, N), 0) % 8
    other = lax.broadcasted_iota(jnp.int32, (N, N), 1) % 8
    forward_heads(r["tq"], r["tk"], r["tv"], r["tw"], r["acc"], place == other)
    r["at_send"][...] = r["acc"][:, 0:HD].reshape(32, 8, HD).astype(BF16)
    exchange(2, r["at_send"], r["at_recv"])

    backward_heads(r["tq"], r["tk"], r["tv"], r["tw"], r["small"], r["accq"], r["acck"], r["accv"])
    join(r["nat"], r["accq"], r["acck"], r["accv"])
    for n in range(0, D, 384):
        r["big"][:, n : n + 384] = dot(r["nat"][:, 0 : 3 * HD], r["wti"][:, n : n + 384])

    def give_gh(step, carry):
        i = lax.rem(z + 4 + (step + 1) // 2 * (1 - 2 * (step % 2)), 8)
        r["gh_send"][slabs_of(i)] = r["big"][rows_of(i), :].reshape(CHUNK // 8, 8, D).astype(BF16)
        send_chunk(3, r["gh_send"], r["gh_recv"], i)
        return carry

    lax.fori_loop(0, N // CHUNK, give_gh, 0)
    r["gh_recv"][seq] = r["gh_send"][seq]

    r["turn"][...] = r["th"][...].astype(F32).T
    for ab in range(2):
        for c in range(2):
            for hi in range(2):
                pieces = []
                for zz in range(4 * ab, 4 * ab + 4):
                    first = zz * 144 + hi * 72 + c * 36
                    pieces.append(r["turn"][first : first + 36, :])
                low = ab * 576 + c * 288 + hi * 144
                r["h_t"][low : low + 144, :] = jnp.concatenate(pieces, 0).astype(BF16)
    for b in range(8):
        low = 216 * b // 128 * 128
        off = 216 * b - low
        part = r["nat"][:, low : low + 384].astype(F32)
        if off:
            part = pltpu.roll(part, 384 - off, 1)
        r["gpad"][b] = part[:, 0:256].astype(BF16)

    parts = (r["part_in"], r["part_out"])
    c_recv = (r["c_recv_in"], r["c_recv_out"])
    one_recv = (r["one_in"], r["one_out"])
    two_recv = (r["two_in"], r["two_out"])
    mid = (r["mid_in"], r["mid_out"])
    three_recv = (r["three_in"], r["three_out"])
    four_recv = (r["four_in"], r["four_out"])
    turns = (2, 1, 3, 0)
    both = ((0, 0), (1, 0), (0, 1), (1, 1))

    def x_first(w, ab):
        return w == 1 or ab == 0

    def places(first, w, ab):
        if x_first(w, ab) == first:
            return x, at_x
        return y, at_y

    def target(w, ab, k):
        me, _ = places(True, w, ab)
        return (me + turns[k]) % 4

    def core_copy(w, ab, k):
        to = target(w, ab, k)
        return remote(
            "core",
            src_ref=parts[w].at[1 - core, ab, to], dst_ref=c_recv[w].at[ab, to],
            send_sem=r["c_ssem"].at[w, ab, k], recv_sem=r["c_rsem"].at[w, ab, k],
            device_id=at_seq(seq + 1 - 2 * core), device_id_type=MESH,
        )

    def one_copy(w, ab, way):
        me, where = places(True, w, ab)
        to = (me + (1, 3)[way]) % 4
        return remote(
            "one",
            src_ref=parts[w].at[core, ab, (me + 2) % 4, pl.ds(2 * way, 2)], dst_ref=one_recv[w].at[ab, way],
            send_sem=r["one_ssem"].at[w, ab, way], recv_sem=r["one_rsem"].at[w, ab, way],
            device_id=where(to), device_id_type=MESH,
        )

    def two_copy(w, ab, way, late):
        me, where = places(True, w, ab)
        to = (me + (1, 3)[way]) % 4
        low = 2 * way if late else 2 - 2 * way
        return remote(
            "two",
            src_ref=parts[w].at[core, ab, to, pl.ds(low, 2)], dst_ref=two_recv[w].at[ab, way, pl.ds(low, 2)],
            send_sem=r["two_ssem"].at[w, ab, way, late], recv_sem=r["two_rsem"].at[w, ab, way, late],
            device_id=where(to), device_id_type=MESH,
        )

    def three_copy(w, ab, way):
        me, where = places(False, w, ab)
        to = (me + (1, 3)[way]) % 4
        return remote(
            "three",
            src_ref=mid[w].at[ab, (me + 2) % 4, way], dst_ref=three_recv[w].at[ab, way],
            send_sem=r["three_ssem"].at[w, ab, way], recv_sem=r["three_rsem"].at[w, ab, way],
            device_id=where(to), device_id_type=MESH,
        )

    def four_copy(w, ab, way, late):
        me, where = places(False, w, ab)
        to = (me + (1, 3)[way]) % 4
        half = way if late else 1 - way
        return remote(
            "four",
            src_ref=mid[w].at[ab, to, half], dst_ref=four_recv[w].at[ab, way, half],
            send_sem=r["four_ssem"].at[w, ab, way, late], recv_sem=r["four_rsem"].at[w, ab, way, late],
            device_id=where(to), device_id_type=MESH,
        )

    def add_in(dst, dst_at, src, src_at):
        dst[dst_at] = (dst[dst_at].astype(F32) + src[src_at].astype(F32)).astype(BF16)

    lane8 = lax.broadcasted_iota(jnp.int32, (8, 128), 1) // 16

    def store(w, ab, slot, value):
        if w == 0:
            for half in range(2):
                parts[0][slot + (half,)] = value[:, half * 128 : half * 128 + 128].astype(BF16)
            return
        tail = value[:, 128:256]
        packed = tail[0:8, :]
        for g in range(1, 8):
            packed = jnp.where(lane8 == g, pltpu.roll(tail[8 * g : 8 * g + 8, :], 16 * g, 1), packed)
        parts[1][slot + (0,)] = value[0:48, 0:128].astype(BF16)
        rest = [value[48:72, 0:128], packed, tail[64:72, :], jnp.zeros((8, 128), F32)]
        parts[1][slot + (1,)] = jnp.concatenate(rest, 0).astype(BF16)

    def fill(w, ab, at):
        left, right, size = ((r["h_t"], r["gpad"], 144), (r["att_t"], r["cpad"], 72))[w]
        for i in range(2 if x_first(w, ab) else 4):
            xx, lo = (at, i) if x_first(w, ab) else (i, at)
            value = dot(left[ab * 4 * size : ab * 4 * size + 4 * size, :], right[2 * xx + lo])
            for c in range(2):
                for hi in range(2):
                    yy = hi * 2 + lo
                    slot = (c, ab, xx, yy) if x_first(w, ab) else (c, ab, yy, xx)
                    low = size * (c * 2 + hi)
                    store(w, ab, slot, value[low : low + size, :])

    def core_add(w, ab, k):
        core_copy(w, ab, k).wait_recv()
        to = target(w, ab, k)
        for j in range(4):
            add_in(parts[w], (core, ab, to, j), c_recv[w], (ab, to, j))
        if k == 0:
            one_copy(w, ab, 0).start()
            one_copy(w, ab, 1).start()
        elif k < 3:
            two_copy(w, ab, k - 1, 0).start()

    def pass_on(w, ab, way):
        one_copy(w, ab, way).wait_recv()
        me, _ = places(True, w, ab)
        to = (me + (1, 3)[way]) % 4
        for j in range(2):
            add_in(parts[w], (core, ab, to, 2 * way + j), one_recv[w], (ab, way, j))
        two_copy(w, ab, way, 1).start()

    def second_ring(w, ab):
        for way in range(2):
            for late in range(2):
                two_copy(w, ab, way, late).wait_recv()
        me, _ = places(True, w, ab)
        for j in range(4):
            mid[w][ab, j] = (
                parts[w][core, ab, me, j].astype(F32)
                + two_recv[w][ab, 0, j].astype(F32)
                + two_recv[w][ab, 1, j].astype(F32)
            ).astype(BF16)
        for way in range(2):
            three_copy(w, ab, way).start()
        for way in range(2):
            four_copy(w, ab, way, 0).start()

    def pass_on_again(w, ab, way):
        three_copy(w, ab, way).wait_recv()
        me, _ = places(False, w, ab)
        add_in(mid[w], (ab, (me + (1, 3)[way]) % 4, way), three_recv[w], (ab, way))
        four_copy(w, ab, way, 1).start()

    def ring_sum(w, ab, half):
        me, _ = places(False, w, ab)
        return (
            mid[w][ab, me, half].astype(F32)
            + four_recv[w][ab, 0, half].astype(F32)
            + four_recv[w][ab, 1, half].astype(F32)
        )

    def ring_wait(w, ab):
        for way in range(2):
            for late in range(2):
                four_copy(w, ab, way, late).wait_recv()

    fill(0, 0, target(0, 0, 0))
    core_copy(0, 0, 0).start()
    fill(0, 1, y_lo)
    core_copy(0, 1, 0).start()
    core_add(0, 0, 0)
    fill(0, 0, target(0, 0, 1))
    core_copy(0, 0, 1).start()
    core_add(0, 1, 0)
    fill(0, 1, 1 - y_lo)
    core_copy(0, 1, 1).start()
    core_copy(0, 1, 2).start()
    fill(0, 0, target(0, 0, 2))
    core_copy(0, 0, 2).start()
    fill(0, 0, target(0, 0, 3))
    core_copy(0, 0, 3).start()
    core_copy(0, 1, 3).start()
    for k in (1, 2):
        core_add(0, 0, k)
        core_add(0, 1, k)

    wait_exchange(2, r["at_recv"])
    r["acc"][:, 0:HD] = r["at_recv"][...].astype(F32).reshape(N, HD)
    r["att"][...] = r["acc"][:, 0:HD].astype(BF16)
    r["turn"][0:HD, :] = r["acc"][:, 0:HD].T
    for ab in range(2):
        for c in range(2):
            pieces = []
            for hi in range(2):
                for zz in range(4 * ab, 4 * ab + 4):
                    first = zz * 72 + hi * 36 + c * 18
                    pieces.append(r["turn"][first : first + 18, :])
            low = ab * 288 + c * 144
            r["att_t"][low : low + 144, :] = jnp.concatenate(pieces, 0).astype(BF16)
    for k in range(4):
        for ab in range(2):
            fill(1, ab, target(1, ab, k))
            core_copy(1, ab, k).start()
    for ab, way in both:
        pass_on(0, ab, way)
    for k in range(3):
        core_add(1, 0, k)
        core_add(1, 1, k)
    for w in range(2):
        for ab in range(2):
            core_add(w, ab, 3)

    for ab, way in both:
        pass_on(1, ab, way)

    for ab in range(2):
        second_ring(0, ab)
    wait_exchange(3, r["gh_recv"])

    def norm_back_residual(i, carry):
        rows = rows_of(i)
        g = r["gh_recv"][slabs_of(i)].astype(F32).reshape(CHUNK, D)
        inverse = r["t_inv"][rows, 0:1]
        n = (r["res"][rows, :].astype(F32) - r["t_mean"][rows, 0:1]) * inverse
        back = inverse * (g - mean_of(g) - n * mean_of(g * n))
        r["gres"][rows, :] = (r["cot"][rows, :].astype(F32) + back).astype(BF16)
        return carry

    lax.fori_loop(0, N // CHUNK, norm_back_residual, 0, unroll=2)
    r["small"][:, 0:HD] = dot_nt(r["gres"][...], r["wso"][...]).astype(BF16)
    for ab, way in both:
        pass_on_again(0, ab, way)
    for ab in range(2):
        second_ring(1, ab)
    backward_heads(r["sq"], r["sk"], r["sv"], r["sw"], r["small"], r["accq"], r["acck"], r["accv"])
    z_send = (r["z_send_in"], r["z_send_out"])
    z_recv = (r["z_recv_in"], r["z_recv_out"])

    def give_z(w):
        first, size, pad = ((0, 36, 4), (144, 18, 6))[w]
        for ab in range(2):
            for half in range(2):
                for j in range(4):
                    low = first + size * j
                    piece = jnp.concatenate([r["zsum"][ab, half, low : low + size, :], jnp.zeros((pad, 128), F32)], 0)
                    z_send[w][4 * ab + j, half] = piece.astype(BF16)

        def z_one(k, carry):
            to = lax.rem(z + 4 + (k + 1) // 2 * (1 - 2 * (k % 2)), 8)
            remote(
                "z",
                src_ref=z_send[w].at[to], dst_ref=z_recv[w].at[z],
                send_sem=r["z_ssem"].at[w], recv_sem=r["z_rsem"].at[w],
                device_id=at_seq(to * 4 + y_hi * 2 + core), device_id_type=MESH,
            ).start()
            return carry

        lax.fori_loop(0, 7, z_one, 0)
        z_recv[w][z] = z_send[w][z]

    for ab in range(2):
        ring_wait(0, ab)
        for half in range(2):
            r["zsum"][ab, half, 0:144] = ring_sum(0, ab, half)
    give_z(0)
    for ab, way in both:
        pass_on_again(1, ab, way)
    join(r["nat"], r["accq"], r["acck"], r["accv"])
    for n in range(0, D, 384):
        r["big"][:, n : n + 384] = dot(r["nat"][:, 0 : 3 * HD], r["wsi"][:, n : n + 384])

    for ab in range(2):
        ring_wait(1, ab)
        first, rest = ring_sum(1, ab, 0), ring_sum(1, ab, 1)
        r["zsum"][ab, 0, 144:192] = first
        r["zsum"][ab, 0, 192:216] = rest[0:24, :]
        for g in range(8):
            tail = rest[24:32, :]
            r["zsum"][ab, 1, 144 + 8 * g : 152 + 8 * g] = pltpu.roll(tail, 128 - 16 * g, 1) if g else tail
        r["zsum"][ab, 1, 208:216] = rest[32:40, :]
    give_z(1)

    def norm_back_video(i, carry):
        rows = rows_of(i)
        g = r["big"][rows, :]
        inverse = r["s_inv"][rows, 0:1]
        n = (r["vid"][rows, :].astype(F32) - r["s_mean"][rows, 0:1]) * inverse
        back = inverse * (g - mean_of(g) - n * mean_of(g * n))
        o_gv[rows, :] = (r["gres"][rows, :].astype(F32) + back).astype(BF16)
        return carry

    lax.fori_loop(0, N // CHUNK, norm_back_video, 0, unroll=2)

    for n in range(0, D, 384):
        o_out[:, n : n + 384] = (
            r["res"][:, n : n + 384].astype(F32) + dot(r["att"][...], r["wto"][:, n : n + 384])
        ).astype(BF16)

    for w in range(2):
        drain("z", z_recv[w].at[pl.ds(0, 7)], r["z_rsem"].at[w])
        for half in range(2):
            total = z_recv[w][0, half].astype(F32)
            for j in range(1, 8):
                total = total + z_recv[w][j, half].astype(F32)
            if w == 0:
                o_gi[:, half * 128 : (128, 216)[half]] = total[0:36, 0 : (128, 88)[half]]
            else:
                o_go[:, half * 128 : (128, 144)[half]] = total[0:18, 0 : (128, 16)[half]]

    for which, name in enumerate(("ga_send", "h_send", "at_send", "gh_send")):
        wait_sent(which, r[name])
    for w in range(2):
        for ab in range(2):
            for k in range(4):
                core_copy(w, ab, k).wait_send()
            for way in range(2):
                one_copy(w, ab, way).wait_send()
                three_copy(w, ab, way).wait_send()
                for late in range(2):
                    two_copy(w, ab, way, late).wait_send()
                    four_copy(w, ab, way, late).wait_send()
    for w in range(2):
        drain("z", z_send[w].at[pl.ds(0, 7)], r["z_ssem"].at[w])


def hand_over(*refs):
    for source, result in zip(refs[:4], refs[4:]):
        result[...] = source[...]


def local(video, spatial_in, spatial_out, temporal_in, temporal_out, cotangent):
    shapes = scratch_shapes()
    names = tuple(shapes)
    anywhere = pl.BlockSpec(memory_space=pl.ANY)
    whole = pl.BlockSpec(memory_space=pltpu.VMEM)

    def body(*refs):
        kernel(*refs[:10], names, *refs[10:])

    results = (
        jax.ShapeDtypeStruct((N, D), BF16),
        jax.ShapeDtypeStruct((N, D), BF16),
        jax.ShapeDtypeStruct((36, 216), F32),
        jax.ShapeDtypeStruct((18, 144), F32),
    )
    held = pl.pallas_call(
        body,
        out_shape=results,
        in_specs=[anywhere] * 6,
        out_specs=(whole,) * 4,
        scratch_shapes=list(shapes.values()),
        compiler_params=pltpu.CompilerParams(
            collective_id=0, has_side_effects=True, vmem_limit_bytes=60 * 1024 * 1024
        ),
        cost_estimate=pl.CostEstimate(flops=9_000_000_000, bytes_accessed=13_000_000, transcendentals=1_100_000),
    )(video.reshape(N, D), spatial_in.T, spatial_out, temporal_in.T, temporal_out, cotangent.reshape(N, D))
    out, grad_video, grad_in, grad_out = pl.pallas_call(
        hand_over,
        out_shape=results,
        in_specs=[whole] * 4,
        out_specs=(whole,) * 4,
        cost_estimate=pl.CostEstimate(flops=0, bytes_accessed=2_400_000, transcendentals=0),
    )(*held)
    return (out.reshape(video.shape), grad_video.reshape(video.shape), grad_in, grad_out)


def solution(mesh):
    in_specs = (P("dp", "seq", None, None), P(), P(), P(), P(), P("dp", "seq", None, None))
    out_specs = (
        P("dp", "seq", None, None),
        P("dp", "seq", None, None),
        P("seq", "dp"),
        P("seq", "dp"),
    )
    return jax.shard_map(local, mesh=mesh, in_specs=in_specs, out_specs=out_specs, check_vma=False)
```

```python
import jax
import jax.numpy as jnp
from jax import lax
from jax.experimental import pallas as pl
from jax.experimental.pallas import tpu as pltpu
from jax.sharding import PartitionSpec as P

HEADS = 8
HEAD = 72
D = 1152
HD = 576
N = 256
PAD = 640
FACTOR = HEAD ** (-0.5)
F32 = jnp.float32
BF16 = jnp.bfloat16
MESH = pl.DeviceIdType.MESH
CHUNK = 32


def dot(a, b):
    return jnp.dot(a, b, preferred_element_type=F32)


def dot_nt(a, b):
    return lax.dot_general(a, b, (((1,), (1,)), ((), ())), preferred_element_type=F32)


def dot_tn(a, b):
    return lax.dot_general(a, b, (((0,), (0,)), ((), ())), preferred_element_type=F32)


def remote(kind, **ends):
    return pltpu.make_async_remote_copy(**ends)


def drain(kind, some, sem):
    pltpu.make_async_copy(some, some, sem).wait()


def window(head):
    start = head * HEAD
    low = start // 128 * 128
    wide = 128 if start + HEAD <= low + 128 else 256
    return start - low, slice(low, low + wide), wide


def head_mask(offset, wide):
    lane = lax.broadcasted_iota(jnp.int32, (N, wide), 1)
    return (lane >= offset) & (lane < offset + HEAD)


def scratch_shapes():
    slab, thin = (2, 144, 128), (2, 48, 128)
    vm = lambda *shape: pltpu.VMEM(shape, BF16)
    vf = lambda *shape: pltpu.VMEM(shape, F32)
    dma = pltpu.SemaphoreType.DMA
    return dict(
        vid=vm(N, D), cot=vm(N, D), wsi=vm(3 * HD, D), wso=vm(HD, D), wti=vm(3 * HD, D), wto=vm(HD, D),
        ga_send=vm(32, 8, HD), ga_recv=vm(32, 8, HD), h_send=vm(32, 8, D), h_recv=vm(32, 8, D),
        at_send=vm(32, 8, HD), at_recv=vm(32, 8, HD), gh_send=vm(32, 8, D), gh_recv=vm(32, 8, D),
        sh=vm(N, D), sq=vm(N, PAD), sk=vm(N, PAD), sv=vm(N, PAD), sw=vm(HEADS, N, N),
        th=vm(N, D), tq=vm(N, PAD), tk=vm(N, PAD), tv=vm(N, PAD), tw=vm(HEADS, N, N),
        acc=vf(N, PAD), accq=vf(N, PAD), acck=vf(N, PAD), accv=vf(N, PAD),
        small=vm(N, PAD), nat=vm(N, 1792), big=vf(N, D),
        res=vm(N, D), gres=vm(N, D), att=vm(N, HD), s_mean=vf(N, 128), s_inv=vf(N, 128), t_mean=vf(N, 128), t_inv=vf(N, 128),
        turn=vf(D, N), h_t=vm(2, HD, N), att_t=vm(2, HD // 2, N), h_t_pair=vm(HD, N), att_t_pair=vm(HD // 2, N),
        gpad=vm(8, N, 256), cpad=vm(8, N, 256), gpad_pair=vm(8, N, 256), cpad_pair=vm(8, N, 256),
        part_in=vm(2, 4, 4, *slab), part_out=vm(2, 4, 4, *thin),
        one_in=vm(2, 2, 2, *slab), one_out=vm(2, 2, 2, *thin), two_in=vm(2, 2, 4, *slab), two_out=vm(2, 2, 4, *thin),
        mid_in=vm(2, 4, *slab), mid_out=vm(2, 4, *thin),
        three_in=vm(2, 2, *slab[1:]), three_out=vm(2, 2, *thin[1:]), four_in=vm(2, 2, *slab), four_out=vm(2, 2, *thin),
        zsum=vf(2, 2, 216, 128), z_send_in=vm(8, 2, 40, 128), z_recv_in=vm(8, 2, 40, 128),
        z_send_out=vm(8, 2, 24, 128), z_recv_out=vm(8, 2, 24, 128),
        load=dma((6,)), a_send=dma((4,)), a_recv=dma((4,)), c_ssem=dma((7,)), c_rsem=dma((7,)),
        one_ssem=dma((2, 2, 2)), one_rsem=dma((2, 2, 2)), two_ssem=dma((2, 2, 2, 2)), two_rsem=dma((2, 2, 2, 2)),
        three_ssem=dma((2, 2, 2)), three_rsem=dma((2, 2, 2)), four_ssem=dma((2, 2, 2, 2)), four_rsem=dma((2, 2, 2, 2)),
        z_ssem=dma((2,)), z_rsem=dma((2,)),
    )


def rows_of(step, size=CHUNK):
    return pl.ds(pl.multiple_of(step * size, size), size)


def slabs_of(step, size=CHUNK // 8):
    return pl.ds(step * size, size)


def mean_of(x):
    return jnp.sum(x, -1, keepdims=True) * (1.0 / D)


def normalize(x):
    center = x - mean_of(x)
    inverse = lax.rsqrt(mean_of(center * center) + 1e-06)
    return center, inverse


def project(src, w, q, k, v):
    x = src[...]
    q[...] = dot_nt(x, w[0:PAD, :]).astype(BF16)
    k[...] = dot_nt(x, w[HD : HD + PAD, :]).astype(BF16)
    v[:, 512:PAD] = jnp.zeros((N, 128), BF16)
    v[:, 0:HD] = dot_nt(x, w[D : 3 * HD, :]).astype(BF16)


def forward_heads(q, k, v, weights, acc, keep):
    for head in range(HEADS):
        offset, cut, wide = window(head)
        mine = head_mask(offset, wide)
        queries = jnp.where(mine, q[:, cut].astype(F32), 0.0).astype(BF16)
        p = jnp.exp(dot_nt(queries, k[:, cut]) * FACTOR)
        if keep is not None:
            p = jnp.where(keep, p, 0.0)
        w = (p * (1.0 / jnp.sum(p, -1, keepdims=True))).astype(BF16)
        weights[head] = w
        out = dot(w, v[:, cut])
        acc[:, cut] = out if head == 0 else jnp.where(mine, out, acc[:, cut])


def backward_heads(q, k, v, weights, grad, accq, acck, accv):
    for head in range(HEADS):
        offset, cut, wide = window(head)
        mine = head_mask(offset, wide)
        g = grad[:, cut]
        w = weights[head]
        e = dot_nt(jnp.where(mine, g.astype(F32), 0.0).astype(BF16), v[:, cut])
        p = w.astype(F32)
        r = (p * (e - jnp.sum(e * p, -1, keepdims=True)) * FACTOR).astype(BF16)
        for acc, out in ((accv, dot_tn(w, g)), (accq, dot(r, k[:, cut])), (acck, dot_tn(r, q[:, cut]))):
            acc[:, cut] = out if head == 0 else jnp.where(mine, out, acc[:, cut])


def join(nat, accq, acck, accv):
    lane = lax.broadcasted_iota(jnp.int32, (N, 128), 1)
    moved = pltpu.roll(acck[...], 64, 1)
    nat[:, 0:512] = accq[:, 0:512].astype(BF16)
    nat[:, 512:640] = jnp.where(lane < 64, accq[:, 512:640], moved[:, 0:128]).astype(BF16)
    nat[:, 640:1152] = moved[:, 128:640].astype(BF16)
    nat[:, 1152:1664] = accv[:, 0:512].astype(BF16)
    nat[:, 1664:1792] = jnp.where(lane < 64, accv[:, 512:640], 0.0).astype(BF16)


def kernel(vid_hbm, wsi_hbm, wso_hbm, wti_hbm, wto_hbm, cot_hbm, o_out, o_gv, o_gi, o_go, names, *refs):
    r = dict(zip(names, refs))
    seq = lax.axis_index("seq")
    dp = lax.axis_index("dp")
    z, y_hi, core = seq // 4, seq // 2 % 2, seq % 2
    x, y_lo = dp // 2, dp % 2
    y = y_hi * 2 + y_lo

    def at_seq(s):
        return {"seq": s, "dp": dp}

    def at_x(to):
        return {"seq": seq, "dp": to * 2 + y_lo}

    def at_y(to):
        return {"seq": z * 4 + to // 2 * 2 + core, "dp": x * 2 + to % 2}

    loads = []
    for i, (src, dst) in enumerate(
        ((cot_hbm, "cot"), (wto_hbm, "wto"), (vid_hbm, "vid"), (wsi_hbm, "wsi"), (wso_hbm, "wso"), (wti_hbm, "wti"))
    ):
        copy = pltpu.make_async_copy(src, r[dst], r["load"].at[i])
        copy.start()
        loads.append(copy)

    barrier = pltpu.get_barrier_semaphore()

    def greet(k, carry):
        pl.semaphore_signal(barrier, inc=1, device_id=at_seq(lax.rem(seq + k, 32)), device_id_type=MESH)
        return carry

    lax.fori_loop(1, 32, greet, 0)
    for step in (1, 3):
        pl.semaphore_signal(barrier, inc=1, device_id=at_x((x + step) % 4), device_id_type=MESH)
        pl.semaphore_signal(barrier, inc=1, device_id=at_y((y + step) % 4), device_id_type=MESH)

    def slab_copy(which, send, recv, to):
        return remote(
            "swap",
            src_ref=send.at[to],
            dst_ref=recv.at[seq],
            send_sem=r["a_send"].at[which],
            recv_sem=r["a_recv"].at[which],
            device_id=at_seq(to),
            device_id_type=MESH,
        )

    def send_chunk(which, send, recv, i):
        for j in range(4):
            to = i * 4 + lax.rem(seq + 2 + j, 4)

            @pl.when(to != seq)
            def _():
                slab_copy(which, send, recv, to).start()

    def exchange(which, send, recv):
        def one(i, carry):
            k = 16 + (i + 1) // 2 * (1 - 2 * (i % 2))
            slab_copy(which, send, recv, lax.rem(seq + k, 32)).start()
            return carry

        lax.fori_loop(0, 31, one, 0)
        recv[seq] = send[seq]

    def wait_exchange(which, recv):
        drain("swap", recv.at[pl.ds(0, 31)], r["a_recv"].at[which])

    def wait_sent(which, send):
        drain("swap", send.at[pl.ds(0, 31)], r["a_send"].at[which])

    loads[0].wait()
    loads[1].wait()
    ga = dot_nt(r["cot"][...], r["wto"][...])
    r["ga_send"][...] = ga.reshape(32, 8, HD).astype(BF16)
    pl.semaphore_wait(barrier, 35)
    exchange(0, r["ga_send"], r["ga_recv"])

    loads[2].wait()

    def norm_video(i, carry):
        rows = rows_of(i)
        v = r["vid"][rows, :].astype(F32)
        mean = mean_of(v)
        center = v - mean
        inverse = lax.rsqrt(mean_of(center * center) + 1e-06)
        r["s_mean"][rows, :] = jnp.broadcast_to(mean, (CHUNK, 128))
        r["s_inv"][rows, :] = jnp.broadcast_to(inverse, (CHUNK, 128))
        r["sh"][rows, :] = (center * inverse).astype(BF16)
        return carry

    lax.fori_loop(0, N // CHUNK, norm_video, 0, unroll=2)
    loads[3].wait()
    project(r["sh"], r["wsi"], r["sq"], r["sk"], r["sv"])
    forward_heads(r["sq"], r["sk"], r["sv"], r["sw"], r["acc"], None)
    r["small"][...] = r["acc"][...].astype(BF16)
    loads[4].wait()
    for n in range(0, D, 384):
        r["big"][:, n : n + 384] = dot(r["small"][:, 0:HD], r["wso"][:, n : n + 384])

    def norm_residual(step, carry):
        i = lax.rem(z + 4 + (step + 1) // 2 * (1 - 2 * (step % 2)), 8)
        rows = rows_of(i)
        v = (r["vid"][rows, :].astype(F32) + r["big"][rows, :]).astype(BF16)
        r["res"][rows, :] = v
        v = v.astype(F32)
        mean = mean_of(v)
        center = v - mean
        inverse = lax.rsqrt(mean_of(center * center) + 1e-06)
        r["t_mean"][rows, :] = jnp.broadcast_to(mean, (CHUNK, 128))
        r["t_inv"][rows, :] = jnp.broadcast_to(inverse, (CHUNK, 128))
        r["h_send"][slabs_of(i)] = (center * inverse).reshape(CHUNK // 8, 8, D).astype(BF16)
        send_chunk(1, r["h_send"], r["h_recv"], i)
        return carry

    lax.fori_loop(0, N // CHUNK, norm_residual, 0)
    r["h_recv"][seq] = r["h_send"][seq]

    turns = (2, 1, 3, 0)

    def pair_copy(i):
        if i < 4:
            blocks = pl.ds(2 * ((x + turns[i]) % 4), 2)
            src, dst = r["gpad"].at[blocks], r["gpad_pair"].at[blocks]
        elif i == 4:
            src, dst = r["cpad"], r["cpad_pair"]
        elif i == 5:
            src, dst = r["h_t"].at[1 - core], r["h_t_pair"]
        else:
            src, dst = r["att_t"].at[1 - core], r["att_t_pair"]
        return remote(
            "core",
            src_ref=src, dst_ref=dst, send_sem=r["c_ssem"].at[i], recv_sem=r["c_rsem"].at[i],
            device_id=at_seq(seq + 1 - 2 * core), device_id_type=MESH,
        )

    for b in range(8):
        part = r["cot"][:, 128 * b : 128 * b + 256].astype(F32)
        if b:
            part = pltpu.roll(part, 256 - 16 * b, 1)
        r["cpad"][b] = part.astype(BF16)
    pair_copy(4).start()
    loads[5].wait()

    wait_exchange(0, r["ga_recv"])
    r["small"][:, 512:PAD] = jnp.zeros((N, 128), BF16)
    r["small"][:, 0:HD] = r["ga_recv"][...].astype(F32).reshape(N, HD).astype(BF16)
    wait_exchange(1, r["h_recv"])

    def take_h(i, carry):
        v = r["h_recv"][slabs_of(i)].astype(F32).reshape(CHUNK, D)
        r["th"][rows_of(i), :] = v.astype(BF16)
        return carry

    lax.fori_loop(0, N // CHUNK, take_h, 0)
    project(r["th"], r["wti"], r["tq"], r["tk"], r["tv"])
    place = lax.broadcasted_iota(jnp.int32, (N, N), 0) % 8
    other = lax.broadcasted_iota(jnp.int32, (N, N), 1) % 8
    forward_heads(r["tq"], r["tk"], r["tv"], r["tw"], r["acc"], place == other)
    r["at_send"][...] = r["acc"][:, 0:HD].reshape(32, 8, HD).astype(BF16)
    exchange(2, r["at_send"], r["at_recv"])

    r["turn"][...] = r["th"][...].astype(F32).T
    for ab in range(2):
        for c in range(2):
            for hi in range(2):
                pieces = []
                for zz in range(4 * ab, 4 * ab + 4):
                    first = zz * 144 + hi * 72 + c * 36
                    pieces.append(r["turn"][first : first + 36, :])
                low = ab * 288 + hi * 144
                r["h_t"][c, low : low + 144, :] = jnp.concatenate(pieces, 0).astype(BF16)
    pair_copy(5).start()

    backward_heads(r["tq"], r["tk"], r["tv"], r["tw"], r["small"], r["accq"], r["acck"], r["accv"])
    join(r["nat"], r["accq"], r["acck"], r["accv"])
    for b in range(8):
        low = 216 * b // 128 * 128
        off = 216 * b - low
        part = r["nat"][:, low : low + 384].astype(F32)
        if off:
            part = pltpu.roll(part, 384 - off, 1)
        r["gpad"][b] = part[:, 0:256].astype(BF16)
    for k in range(4):
        pair_copy(k).start()
    for n in range(0, D, 384):
        r["big"][:, n : n + 384] = dot(r["nat"][:, 0 : 3 * HD], r["wti"][:, n : n + 384])

    def give_gh(step, carry):
        i = lax.rem(z + 4 + (step + 1) // 2 * (1 - 2 * (step % 2)), 8)
        r["gh_send"][slabs_of(i)] = r["big"][rows_of(i), :].reshape(CHUNK // 8, 8, D).astype(BF16)
        send_chunk(3, r["gh_send"], r["gh_recv"], i)
        return carry

    lax.fori_loop(0, N // CHUNK, give_gh, 0)
    r["gh_recv"][seq] = r["gh_send"][seq]

    parts = (r["part_in"], r["part_out"])
    one_recv = (r["one_in"], r["one_out"])
    two_recv = (r["two_in"], r["two_out"])
    mid = (r["mid_in"], r["mid_out"])
    three_recv = (r["three_in"], r["three_out"])
    four_recv = (r["four_in"], r["four_out"])
    both = ((0, 0), (1, 0), (0, 1), (1, 1))

    def x_first(w, ab):
        return w == 1 or ab == 0

    def places(first, w, ab):
        if x_first(w, ab) == first:
            return x, at_x
        return y, at_y

    def target(w, ab, k):
        me, _ = places(True, w, ab)
        return (me + turns[k]) % 4

    def one_copy(w, ab, way):
        me, where = places(True, w, ab)
        to = (me + (1, 3)[way]) % 4
        return remote(
            "one",
            src_ref=parts[w].at[ab, (me + 2) % 4, pl.ds(2 * way, 2)], dst_ref=one_recv[w].at[ab, way],
            send_sem=r["one_ssem"].at[w, ab, way], recv_sem=r["one_rsem"].at[w, ab, way],
            device_id=where(to), device_id_type=MESH,
        )

    def two_copy(w, ab, way, late):
        me, where = places(True, w, ab)
        to = (me + (1, 3)[way]) % 4
        low = 2 * way if late else 2 - 2 * way
        return remote(
            "two",
            src_ref=parts[w].at[ab, to, pl.ds(low, 2)], dst_ref=two_recv[w].at[ab, way, pl.ds(low, 2)],
            send_sem=r["two_ssem"].at[w, ab, way, late], recv_sem=r["two_rsem"].at[w, ab, way, late],
            device_id=where(to), device_id_type=MESH,
        )

    def three_copy(w, ab, way):
        me, where = places(False, w, ab)
        to = (me + (1, 3)[way]) % 4
        return remote(
            "three",
            src_ref=mid[w].at[ab, (me + 2) % 4, way], dst_ref=three_recv[w].at[ab, way],
            send_sem=r["three_ssem"].at[w, ab, way], recv_sem=r["three_rsem"].at[w, ab, way],
            device_id=where(to), device_id_type=MESH,
        )

    def four_copy(w, ab, way, late):
        me, where = places(False, w, ab)
        to = (me + (1, 3)[way]) % 4
        half = way if late else 1 - way
        return remote(
            "four",
            src_ref=mid[w].at[ab, to, half], dst_ref=four_recv[w].at[ab, way, half],
            send_sem=r["four_ssem"].at[w, ab, way, late], recv_sem=r["four_rsem"].at[w, ab, way, late],
            device_id=where(to), device_id_type=MESH,
        )

    def add_in(dst, dst_at, src, src_at):
        dst[dst_at] = (dst[dst_at].astype(F32) + src[src_at].astype(F32)).astype(BF16)

    lane8 = lax.broadcasted_iota(jnp.int32, (8, 128), 1) // 16

    def store(w, ab, slot, value):
        if w == 0:
            for half in range(2):
                parts[0][slot + (half,)] = value[:, half * 128 : half * 128 + 128].astype(BF16)
            return
        tail = value[:, 128:256]
        packed = tail[0:8, :]
        for g in range(1, 8):
            packed = jnp.where(lane8 == g, pltpu.roll(tail[8 * g : 8 * g + 8, :], 16 * g, 1), packed)
        parts[1][slot + (0,)] = value[0:48, 0:128].astype(BF16)
        rest = [value[48:72, 0:128], packed, tail[64:72, :], jnp.zeros((8, 128), F32)]
        parts[1][slot + (1,)] = jnp.concatenate(rest, 0).astype(BF16)

    def fill(w, ab, at):
        left, right, size = ((r["h_t"], r["gpad"], 144), (r["att_t"], r["cpad"], 72))[w]
        left_pair, right_pair = ((r["h_t_pair"], r["gpad_pair"]), (r["att_t_pair"], r["cpad_pair"]))[w]
        rows = slice(ab * 2 * size, ab * 2 * size + 2 * size)
        for i in range(2 if x_first(w, ab) else 4):
            xx, lo = (at, i) if x_first(w, ab) else (i, at)
            b = 2 * xx + lo
            value = dot(left[core, rows, :], right[b]) + dot(left_pair[rows, :], right_pair[b])
            for hi in range(2):
                yy = hi * 2 + lo
                slot = (ab, xx, yy) if x_first(w, ab) else (ab, yy, xx)
                store(w, ab, slot, value[size * hi : size * hi + size, :])

    def start_ring(w, ab, k):
        if k == 0:
            one_copy(w, ab, 0).start()
            one_copy(w, ab, 1).start()
        elif k < 3:
            two_copy(w, ab, k - 1, 0).start()

    def pass_on(w, ab, way):
        one_copy(w, ab, way).wait_recv()
        me, _ = places(True, w, ab)
        to = (me + (1, 3)[way]) % 4
        for j in range(2):
            add_in(parts[w], (ab, to, 2 * way + j), one_recv[w], (ab, way, j))
        two_copy(w, ab, way, 1).start()

    def second_ring(w, ab):
        for way in range(2):
            for late in range(2):
                two_copy(w, ab, way, late).wait_recv()
        me, _ = places(True, w, ab)
        for j in range(4):
            mid[w][ab, j] = (
                parts[w][ab, me, j].astype(F32)
                + two_recv[w][ab, 0, j].astype(F32)
                + two_recv[w][ab, 1, j].astype(F32)
            ).astype(BF16)
        for way in range(2):
            three_copy(w, ab, way).start()
        for way in range(2):
            four_copy(w, ab, way, 0).start()

    def pass_on_again(w, ab, way):
        three_copy(w, ab, way).wait_recv()
        me, _ = places(False, w, ab)
        add_in(mid[w], (ab, (me + (1, 3)[way]) % 4, way), three_recv[w], (ab, way))
        four_copy(w, ab, way, 1).start()

    def ring_sum(w, ab, half):
        me, _ = places(False, w, ab)
        return (
            mid[w][ab, me, half].astype(F32)
            + four_recv[w][ab, 0, half].astype(F32)
            + four_recv[w][ab, 1, half].astype(F32)
        )

    def ring_wait(w, ab):
        for way in range(2):
            for late in range(2):
                four_copy(w, ab, way, late).wait_recv()

    pair_copy(5).wait_recv()
    for k in range(4):
        pair_copy(k).wait_recv()
        if k < 3:
            fill(0, 0, target(0, 0, k))
            start_ring(0, 0, k)
    fill(0, 1, y_lo)
    start_ring(0, 1, 0)
    fill(0, 1, 1 - y_lo)
    start_ring(0, 1, 1)
    start_ring(0, 1, 2)
    fill(0, 0, target(0, 0, 3))

    wait_exchange(2, r["at_recv"])
    r["acc"][:, 0:HD] = r["at_recv"][...].astype(F32).reshape(N, HD)
    r["att"][...] = r["acc"][:, 0:HD].astype(BF16)
    r["turn"][0:HD, :] = r["acc"][:, 0:HD].T
    for ab in range(2):
        for c in range(2):
            pieces = []
            for hi in range(2):
                for zz in range(4 * ab, 4 * ab + 4):
                    first = zz * 72 + hi * 36 + c * 18
                    pieces.append(r["turn"][first : first + 18, :])
            r["att_t"][c, ab * 144 : ab * 144 + 144, :] = jnp.concatenate(pieces, 0).astype(BF16)
    pair_copy(6).start()
    for ab, way in both:
        pass_on(0, ab, way)
    pair_copy(4).wait_recv()
    pair_copy(6).wait_recv()
    for k in range(4):
        for ab in range(2):
            fill(1, ab, target(1, ab, k))
            start_ring(1, ab, k)
    for ab, way in both:
        pass_on(1, ab, way)

    for ab in range(2):
        second_ring(0, ab)
    wait_exchange(3, r["gh_recv"])

    def norm_back_residual(i, carry):
        rows = rows_of(i)
        g = r["gh_recv"][slabs_of(i)].astype(F32).reshape(CHUNK, D)
        inverse = r["t_inv"][rows, 0:1]
        n = (r["res"][rows, :].astype(F32) - r["t_mean"][rows, 0:1]) * inverse
        back = inverse * (g - mean_of(g) - n * mean_of(g * n))
        r["gres"][rows, :] = (r["cot"][rows, :].astype(F32) + back).astype(BF16)
        return carry

    lax.fori_loop(0, N // CHUNK, norm_back_residual, 0, unroll=2)
    r["small"][:, 0:HD] = dot_nt(r["gres"][...], r["wso"][...]).astype(BF16)
    for ab, way in both:
        pass_on_again(0, ab, way)
    for ab in range(2):
        second_ring(1, ab)
    backward_heads(r["sq"], r["sk"], r["sv"], r["sw"], r["small"], r["accq"], r["acck"], r["accv"])
    z_send = (r["z_send_in"], r["z_send_out"])
    z_recv = (r["z_recv_in"], r["z_recv_out"])

    def give_z(w):
        first, size, pad = ((0, 36, 4), (144, 18, 6))[w]
        for ab in range(2):
            for half in range(2):
                for j in range(4):
                    low = first + size * j
                    piece = jnp.concatenate([r["zsum"][ab, half, low : low + size, :], jnp.zeros((pad, 128), F32)], 0)
                    z_send[w][4 * ab + j, half] = piece.astype(BF16)

        def z_one(k, carry):
            to = lax.rem(z + 4 + (k + 1) // 2 * (1 - 2 * (k % 2)), 8)
            remote(
                "z",
                src_ref=z_send[w].at[to], dst_ref=z_recv[w].at[z],
                send_sem=r["z_ssem"].at[w], recv_sem=r["z_rsem"].at[w],
                device_id=at_seq(to * 4 + y_hi * 2 + core), device_id_type=MESH,
            ).start()
            return carry

        lax.fori_loop(0, 7, z_one, 0)
        z_recv[w][z] = z_send[w][z]

    for ab in range(2):
        ring_wait(0, ab)
        for half in range(2):
            r["zsum"][ab, half, 0:144] = ring_sum(0, ab, half)
    give_z(0)
    for ab, way in both:
        pass_on_again(1, ab, way)
    join(r["nat"], r["accq"], r["acck"], r["accv"])
    for n in range(0, D, 384):
        r["big"][:, n : n + 384] = dot(r["nat"][:, 0 : 3 * HD], r["wsi"][:, n : n + 384])

    for ab in range(2):
        ring_wait(1, ab)
        first, rest = ring_sum(1, ab, 0), ring_sum(1, ab, 1)
        r["zsum"][ab, 0, 144:192] = first
        r["zsum"][ab, 0, 192:216] = rest[0:24, :]
        for g in range(8):
            tail = rest[24:32, :]
            r["zsum"][ab, 1, 144 + 8 * g : 152 + 8 * g] = pltpu.roll(tail, 128 - 16 * g, 1) if g else tail
        r["zsum"][ab, 1, 208:216] = rest[32:40, :]
    give_z(1)

    def norm_back_video(i, carry):
        rows = rows_of(i)
        g = r["big"][rows, :]
        inverse = r["s_inv"][rows, 0:1]
        n = (r["vid"][rows, :].astype(F32) - r["s_mean"][rows, 0:1]) * inverse
        back = inverse * (g - mean_of(g) - n * mean_of(g * n))
        o_gv[rows, :] = (r["gres"][rows, :].astype(F32) + back).astype(BF16)
        return carry

    lax.fori_loop(0, N // CHUNK, norm_back_video, 0, unroll=2)

    for n in range(0, D, 384):
        o_out[:, n : n + 384] = (
            r["res"][:, n : n + 384].astype(F32) + dot(r["att"][...], r["wto"][:, n : n + 384])
        ).astype(BF16)

    for w in range(2):
        drain("z", z_recv[w].at[pl.ds(0, 7)], r["z_rsem"].at[w])
        for half in range(2):
            total = z_recv[w][0, half].astype(F32)
            for j in range(1, 8):
                total = total + z_recv[w][j, half].astype(F32)
            if w == 0:
                o_gi[:, half * 128 : (128, 216)[half]] = total[0:36, 0 : (128, 88)[half]]
            else:
                o_go[:, half * 128 : (128, 144)[half]] = total[0:18, 0 : (128, 16)[half]]

    for which, name in enumerate(("ga_send", "h_send", "at_send", "gh_send")):
        wait_sent(which, r[name])
    for i in range(7):
        pair_copy(i).wait_send()
    for w in range(2):
        for ab in range(2):
            for way in range(2):
                one_copy(w, ab, way).wait_send()
                three_copy(w, ab, way).wait_send()
                for late in range(2):
                    two_copy(w, ab, way, late).wait_send()
                    four_copy(w, ab, way, late).wait_send()
    for w in range(2):
        drain("z", z_send[w].at[pl.ds(0, 7)], r["z_ssem"].at[w])


def hand_over(*refs):
    for source, result in zip(refs[:4], refs[4:]):
        result[...] = source[...]


def local(video, spatial_in, spatial_out, temporal_in, temporal_out, cotangent):
    shapes = scratch_shapes()
    names = tuple(shapes)
    anywhere = pl.BlockSpec(memory_space=pl.ANY)
    whole = pl.BlockSpec(memory_space=pltpu.VMEM)

    def body(*refs):
        kernel(*refs[:10], names, *refs[10:])

    results = (
        jax.ShapeDtypeStruct((N, D), BF16),
        jax.ShapeDtypeStruct((N, D), BF16),
        jax.ShapeDtypeStruct((36, 216), F32),
        jax.ShapeDtypeStruct((18, 144), F32),
    )
    held = pl.pallas_call(
        body,
        out_shape=results,
        in_specs=[anywhere] * 6,
        out_specs=(whole,) * 4,
        scratch_shapes=list(shapes.values()),
        compiler_params=pltpu.CompilerParams(
            collective_id=0, has_side_effects=True, vmem_limit_bytes=60 * 1024 * 1024
        ),
        cost_estimate=pl.CostEstimate(flops=9_000_000_000, bytes_accessed=13_000_000, transcendentals=1_100_000),
    )(video.reshape(N, D), spatial_in.T, spatial_out, temporal_in.T, temporal_out, cotangent.reshape(N, D))
    out, grad_video, grad_in, grad_out = pl.pallas_call(
        hand_over,
        out_shape=results,
        in_specs=[whole] * 4,
        out_specs=(whole,) * 4,
        cost_estimate=pl.CostEstimate(flops=0, bytes_accessed=2_400_000, transcendentals=0),
    )(*held)
    return (out.reshape(video.shape), grad_video.reshape(video.shape), grad_in, grad_out)


def solution(mesh):
    in_specs = (P("dp", "seq", None, None), P(), P(), P(), P(), P("dp", "seq", None, None))
    out_specs = (
        P("dp", "seq", None, None),
        P("dp", "seq", None, None),
        P("seq", "dp"),
        P("seq", "dp"),
    )
    return jax.shard_map(local, mesh=mesh, in_specs=in_specs, out_specs=out_specs, check_vma=False)
```

```python
import jax
import jax.numpy as jnp
from jax import lax
from jax.experimental import pallas as pl
from jax.experimental.pallas import tpu as pltpu
from jax.sharding import PartitionSpec as P

HEADS = 8
HEAD = 72
D = 1152
HD = 576
N = 256
PAD = 640
FACTOR = HEAD ** (-0.5)
F32 = jnp.float32
BF16 = jnp.bfloat16
MESH = pl.DeviceIdType.MESH
CHUNK = 32


def dot(a, b):
    return jnp.dot(a, b, preferred_element_type=F32)


def dot_nt(a, b):
    return lax.dot_general(a, b, (((1,), (1,)), ((), ())), preferred_element_type=F32)


def dot_tn(a, b):
    return lax.dot_general(a, b, (((0,), (0,)), ((), ())), preferred_element_type=F32)


def remote(kind, **ends):
    return pltpu.make_async_remote_copy(**ends)


def drain(kind, some, sem):
    pltpu.make_async_copy(some, some, sem).wait()


def window(head):
    start = head * HEAD
    low = start // 128 * 128
    wide = 128 if start + HEAD <= low + 128 else 256
    return start - low, slice(low, low + wide), wide


def head_mask(offset, wide):
    lane = lax.broadcasted_iota(jnp.int32, (N, wide), 1)
    return (lane >= offset) & (lane < offset + HEAD)


def scratch_shapes():
    slab, thin = (2, 144, 128), (2, 48, 128)
    vm = lambda *shape: pltpu.VMEM(shape, BF16)
    vf = lambda *shape: pltpu.VMEM(shape, F32)
    dma = pltpu.SemaphoreType.DMA
    return dict(
        vid=vm(N, D), cot=vm(N, D), wsi=vm(3 * HD, D), wso=vm(HD, D), wti=vm(3 * HD, D), wto=vm(HD, D),
        ga_send=vm(32, 8, HD), ga_recv=vm(32, 8, HD), h_send=vm(32, 8, D), h_recv=vm(32, 8, D),
        at_send=vm(32, 8, HD), at_recv=vm(32, 8, HD), gh_send=vm(32, 8, D), gh_recv=vm(32, 8, D),
        sh=vm(N, D), sq=vm(N, PAD), sk=vm(N, PAD), sv=vm(N, PAD), sw=vm(HEADS, N, N),
        th=vm(N, D), tq=vm(N, PAD), tk=vm(N, PAD), tv=vm(N, PAD), tw=vm(HEADS, N, N),
        acc=vf(N, PAD), accq=vf(N, PAD), acck=vf(N, PAD), accv=vf(N, PAD),
        small=vm(N, PAD), nat=vm(N, 1792), big=vf(N, D),
        res=vm(N, D), gres=vm(N, D), att=vm(N, HD), s_mean=vf(N, 128), s_inv=vf(N, 128), t_mean=vf(N, 128), t_inv=vf(N, 128),
        turn=vf(D, N), h_t=vm(2, HD, N), att_t=vm(2, HD // 2, N), h_t_pair=vm(HD, N), att_t_pair=vm(HD // 2, N),
        gpad=vm(8, N, 256), cpad=vm(8, N, 256), gpad_pair=vm(8, N, 256), cpad_pair=vm(8, N, 256),
        part_in=vm(2, 4, 4, *slab), part_out=vm(2, 4, 4, *thin),
        one_in=vm(2, 2, 2, *slab), one_out=vm(2, 2, 2, *thin), two_in=vm(2, 2, 4, *slab), two_out=vm(2, 2, 4, *thin),
        mid_in=vm(2, 4, *slab), mid_out=vm(2, 4, *thin),
        last_in=vm(2, 3, *slab), last_out=vm(2, 3, *thin),
        zsum=vf(2, 2, 216, 128), z_send_in=vm(8, 2, 40, 128), z_recv_in=vm(8, 2, 40, 128),
        z_send_out=vm(8, 24, 128), z_recv_out=vm(8, 24, 128),
        load=dma((6,)), a_send=dma((4,)), a_recv=dma((4,)), c_ssem=dma((7,)), c_rsem=dma((7,)),
        one_ssem=dma((2, 2, 2)), one_rsem=dma((2, 2, 2)), two_ssem=dma((2, 2, 2, 2)), two_rsem=dma((2, 2, 2, 2)),
        last_ssem=dma((2, 2, 3)), last_rsem=dma((2, 2, 3)),
        z_ssem=dma((2,)), z_rsem=dma((2,)),
    )


def rows_of(step, size=CHUNK):
    return pl.ds(pl.multiple_of(step * size, size), size)


def slabs_of(step, size=CHUNK // 8):
    return pl.ds(step * size, size)


def mean_of(x):
    return jnp.sum(x, -1, keepdims=True) * (1.0 / D)


def normalize(x):
    center = x - mean_of(x)
    inverse = lax.rsqrt(mean_of(center * center) + 1e-06)
    return center, inverse


def project(src, w, q, k, v):
    x = src[...]
    q[...] = dot_nt(x, w[0:PAD, :]).astype(BF16)
    k[...] = dot_nt(x, w[HD : HD + PAD, :]).astype(BF16)
    v[:, 512:PAD] = jnp.zeros((N, 128), BF16)
    v[:, 0:HD] = dot_nt(x, w[D : 3 * HD, :]).astype(BF16)


def forward_heads(q, k, v, weights, acc, keep):
    for head in range(HEADS):
        offset, cut, wide = window(head)
        mine = head_mask(offset, wide)
        queries = jnp.where(mine, q[:, cut].astype(F32), 0.0).astype(BF16)
        p = jnp.exp(dot_nt(queries, k[:, cut]) * FACTOR)
        if keep is not None:
            p = jnp.where(keep, p, 0.0)
        w = (p * (1.0 / jnp.sum(p, -1, keepdims=True))).astype(BF16)
        weights[head] = w
        out = dot(w, v[:, cut])
        acc[:, cut] = out if head == 0 else jnp.where(mine, out, acc[:, cut])


def backward_heads(q, k, v, weights, grad, accq, acck, accv):
    for head in range(HEADS):
        offset, cut, wide = window(head)
        mine = head_mask(offset, wide)
        g = grad[:, cut]
        w = weights[head]
        e = dot_nt(jnp.where(mine, g.astype(F32), 0.0).astype(BF16), v[:, cut])
        p = w.astype(F32)
        r = (p * (e - jnp.sum(e * p, -1, keepdims=True)) * FACTOR).astype(BF16)
        for acc, out in ((accv, dot_tn(w, g)), (accq, dot(r, k[:, cut])), (acck, dot_tn(r, q[:, cut]))):
            acc[:, cut] = out if head == 0 else jnp.where(mine, out, acc[:, cut])


def join(nat, accq, acck, accv):
    lane = lax.broadcasted_iota(jnp.int32, (N, 128), 1)
    moved = pltpu.roll(acck[...], 64, 1)
    nat[:, 0:512] = accq[:, 0:512].astype(BF16)
    nat[:, 512:640] = jnp.where(lane < 64, accq[:, 512:640], moved[:, 0:128]).astype(BF16)
    nat[:, 640:1152] = moved[:, 128:640].astype(BF16)
    nat[:, 1152:1664] = accv[:, 0:512].astype(BF16)
    nat[:, 1664:1792] = jnp.where(lane < 64, accv[:, 512:640], 0.0).astype(BF16)


def kernel(vid_hbm, wsi_hbm, wso_hbm, wti_hbm, wto_hbm, cot_hbm, o_out, o_gv, o_gi, o_go, names, *refs):
    r = dict(zip(names, refs))
    seq = lax.axis_index("seq")
    dp = lax.axis_index("dp")
    z, y_hi, core = seq // 4, seq // 2 % 2, seq % 2
    x, y_lo = dp // 2, dp % 2
    y = y_hi * 2 + y_lo

    def at_seq(s):
        return {"seq": s, "dp": dp}

    def at_x(to):
        return {"seq": seq, "dp": to * 2 + y_lo}

    def at_y(to):
        return {"seq": z * 4 + to // 2 * 2 + core, "dp": x * 2 + to % 2}

    loads = []
    for i, (src, dst) in enumerate(
        ((cot_hbm, "cot"), (wto_hbm, "wto"), (vid_hbm, "vid"), (wsi_hbm, "wsi"), (wso_hbm, "wso"), (wti_hbm, "wti"))
    ):
        copy = pltpu.make_async_copy(src, r[dst], r["load"].at[i])
        copy.start()
        loads.append(copy)

    barrier = pltpu.get_barrier_semaphore()

    def greet(k, carry):
        pl.semaphore_signal(barrier, inc=1, device_id=at_seq(lax.rem(seq + k, 32)), device_id_type=MESH)
        return carry

    lax.fori_loop(1, 32, greet, 0)
    for step in (1, 2, 3):
        pl.semaphore_signal(barrier, inc=1, device_id=at_x((x + step) % 4), device_id_type=MESH)
    for step in (1, 3):
        pl.semaphore_signal(barrier, inc=1, device_id=at_y((y + step) % 4), device_id_type=MESH)

    def slab_copy(which, send, recv, to):
        return remote(
            "swap",
            src_ref=send.at[to],
            dst_ref=recv.at[seq],
            send_sem=r["a_send"].at[which],
            recv_sem=r["a_recv"].at[which],
            device_id=at_seq(to),
            device_id_type=MESH,
        )

    def send_chunk(which, send, recv, i):
        for j in range(4):
            to = i * 4 + lax.rem(seq + 2 + j, 4)

            @pl.when(to != seq)
            def _():
                slab_copy(which, send, recv, to).start()

    def exchange(which, send, recv):
        def one(i, carry):
            k = 16 + (i + 1) // 2 * (1 - 2 * (i % 2))
            slab_copy(which, send, recv, lax.rem(seq + k, 32)).start()
            return carry

        lax.fori_loop(0, 31, one, 0)
        recv[seq] = send[seq]

    def wait_exchange(which, recv):
        drain("swap", recv.at[pl.ds(0, 31)], r["a_recv"].at[which])

    def wait_sent(which, send):
        drain("swap", send.at[pl.ds(0, 31)], r["a_send"].at[which])

    loads[0].wait()
    loads[1].wait()
    ga = dot_nt(r["cot"][...], r["wto"][...])
    r["ga_send"][...] = ga.reshape(32, 8, HD).astype(BF16)
    pl.semaphore_wait(barrier, 36)
    exchange(0, r["ga_send"], r["ga_recv"])

    loads[2].wait()

    def norm_video(i, carry):
        rows = rows_of(i)
        v = r["vid"][rows, :].astype(F32)
        mean = mean_of(v)
        center = v - mean
        inverse = lax.rsqrt(mean_of(center * center) + 1e-06)
        r["s_mean"][rows, :] = jnp.broadcast_to(mean, (CHUNK, 128))
        r["s_inv"][rows, :] = jnp.broadcast_to(inverse, (CHUNK, 128))
        r["sh"][rows, :] = (center * inverse).astype(BF16)
        return carry

    lax.fori_loop(0, N // CHUNK, norm_video, 0, unroll=2)
    loads[3].wait()
    project(r["sh"], r["wsi"], r["sq"], r["sk"], r["sv"])
    forward_heads(r["sq"], r["sk"], r["sv"], r["sw"], r["acc"], None)
    r["small"][...] = r["acc"][...].astype(BF16)
    loads[4].wait()
    for n in range(0, D, 384):
        r["big"][:, n : n + 384] = dot(r["small"][:, 0:HD], r["wso"][:, n : n + 384])

    def norm_residual(step, carry):
        i = lax.rem(z + 4 + (step + 1) // 2 * (1 - 2 * (step % 2)), 8)
        rows = rows_of(i)
        v = (r["vid"][rows, :].astype(F32) + r["big"][rows, :]).astype(BF16)
        r["res"][rows, :] = v
        v = v.astype(F32)
        mean = mean_of(v)
        center = v - mean
        inverse = lax.rsqrt(mean_of(center * center) + 1e-06)
        r["t_mean"][rows, :] = jnp.broadcast_to(mean, (CHUNK, 128))
        r["t_inv"][rows, :] = jnp.broadcast_to(inverse, (CHUNK, 128))
        r["h_send"][slabs_of(i)] = (center * inverse).reshape(CHUNK // 8, 8, D).astype(BF16)
        send_chunk(1, r["h_send"], r["h_recv"], i)
        return carry

    lax.fori_loop(0, N // CHUNK, norm_residual, 0)
    r["h_recv"][seq] = r["h_send"][seq]

    turns = (2, 1, 3, 0)

    def pair_copy(i):
        if i < 4:
            blocks = pl.ds(2 * ((x + turns[i]) % 4), 2)
            src, dst = r["gpad"].at[blocks], r["gpad_pair"].at[blocks]
        elif i == 4:
            src, dst = r["cpad"], r["cpad_pair"]
        elif i == 5:
            src, dst = r["h_t"].at[1 - core], r["h_t_pair"]
        else:
            src, dst = r["att_t"].at[1 - core], r["att_t_pair"]
        return remote(
            "core",
            src_ref=src, dst_ref=dst, send_sem=r["c_ssem"].at[i], recv_sem=r["c_rsem"].at[i],
            device_id=at_seq(seq + 1 - 2 * core), device_id_type=MESH,
        )

    for b in range(8):
        part = r["cot"][:, 128 * b : 128 * b + 256].astype(F32)
        if b:
            part = pltpu.roll(part, 256 - 16 * b, 1)
        r["cpad"][b] = part.astype(BF16)
    pair_copy(4).start()
    loads[5].wait()

    wait_exchange(0, r["ga_recv"])
    r["small"][:, 512:PAD] = jnp.zeros((N, 128), BF16)
    r["small"][:, 0:HD] = r["ga_recv"][...].astype(F32).reshape(N, HD).astype(BF16)
    wait_exchange(1, r["h_recv"])

    def take_h(i, carry):
        v = r["h_recv"][slabs_of(i)].astype(F32).reshape(CHUNK, D)
        r["th"][rows_of(i), :] = v.astype(BF16)
        return carry

    lax.fori_loop(0, N // CHUNK, take_h, 0)
    project(r["th"], r["wti"], r["tq"], r["tk"], r["tv"])
    place = lax.broadcasted_iota(jnp.int32, (N, N), 0) % 8
    other = lax.broadcasted_iota(jnp.int32, (N, N), 1) % 8
    forward_heads(r["tq"], r["tk"], r["tv"], r["tw"], r["acc"], place == other)
    r["at_send"][...] = r["acc"][:, 0:HD].reshape(32, 8, HD).astype(BF16)
    exchange(2, r["at_send"], r["at_recv"])

    r["turn"][...] = r["th"][...].astype(F32).T
    for ab in range(2):
        for c in range(2):
            for hi in range(2):
                pieces = []
                for zz in range(4 * ab, 4 * ab + 4):
                    first = zz * 144 + hi * 72 + c * 36
                    pieces.append(r["turn"][first : first + 36, :])
                low = ab * 288 + hi * 144
                r["h_t"][c, low : low + 144, :] = jnp.concatenate(pieces, 0).astype(BF16)
    pair_copy(5).start()

    backward_heads(r["tq"], r["tk"], r["tv"], r["tw"], r["small"], r["accq"], r["acck"], r["accv"])
    join(r["nat"], r["accq"], r["acck"], r["accv"])
    for b in range(8):
        low = 216 * b // 128 * 128
        off = 216 * b - low
        part = r["nat"][:, low : low + 384].astype(F32)
        if off:
            part = pltpu.roll(part, 384 - off, 1)
        r["gpad"][b] = part[:, 0:256].astype(BF16)
    for k in range(4):
        pair_copy(k).start()
    for n in range(0, D, 384):
        r["big"][:, n : n + 384] = dot(r["nat"][:, 0 : 3 * HD], r["wti"][:, n : n + 384])

    def give_gh(step, carry):
        i = lax.rem(z + 4 + (step + 1) // 2 * (1 - 2 * (step % 2)), 8)
        r["gh_send"][slabs_of(i)] = r["big"][rows_of(i), :].reshape(CHUNK // 8, 8, D).astype(BF16)
        send_chunk(3, r["gh_send"], r["gh_recv"], i)
        return carry

    lax.fori_loop(0, N // CHUNK, give_gh, 0)
    r["gh_recv"][seq] = r["gh_send"][seq]

    parts = (r["part_in"], r["part_out"])
    one_recv = (r["one_in"], r["one_out"])
    two_recv = (r["two_in"], r["two_out"])
    mid = (r["mid_in"], r["mid_out"])
    last_recv = (r["last_in"], r["last_out"])
    both = ((0, 0), (1, 0), (0, 1), (1, 1))

    def x_first(w, ab):
        return w == 1 or ab == 0

    def places(first, w, ab):
        if x_first(w, ab) == first:
            return x, at_x
        return y, at_y

    def target(w, ab, k):
        me, _ = places(True, w, ab)
        return (me + turns[k]) % 4

    def one_copy(w, ab, way):
        me, where = places(True, w, ab)
        to = (me + (1, 3)[way]) % 4
        return remote(
            "one",
            src_ref=parts[w].at[ab, (me + 2) % 4, pl.ds(2 * way, 2)], dst_ref=one_recv[w].at[ab, way],
            send_sem=r["one_ssem"].at[w, ab, way], recv_sem=r["one_rsem"].at[w, ab, way],
            device_id=where(to), device_id_type=MESH,
        )

    def two_copy(w, ab, way, late):
        me, where = places(True, w, ab)
        to = (me + (1, 3)[way]) % 4
        low = 2 * way if late else 2 - 2 * way
        return remote(
            "two",
            src_ref=parts[w].at[ab, to, pl.ds(low, 2)], dst_ref=two_recv[w].at[ab, way, pl.ds(low, 2)],
            send_sem=r["two_ssem"].at[w, ab, way, late], recv_sem=r["two_rsem"].at[w, ab, way, late],
            device_id=where(to), device_id_type=MESH,
        )

    def last_copy(w, ab, step):
        me, where = places(False, w, ab)
        to = (me + step) % 4
        return remote(
            "last",
            src_ref=mid[w].at[ab, to], dst_ref=last_recv[w].at[ab, step - 1],
            send_sem=r["last_ssem"].at[w, ab, step - 1], recv_sem=r["last_rsem"].at[w, ab, step - 1],
            device_id=where(to), device_id_type=MESH,
        )

    def add_in(dst, dst_at, src, src_at):
        dst[dst_at] = (dst[dst_at].astype(F32) + src[src_at].astype(F32)).astype(BF16)

    lane8 = lax.broadcasted_iota(jnp.int32, (8, 128), 1) // 16

    def store(w, ab, slot, value):
        if w == 0:
            for half in range(2):
                parts[0][slot + (half,)] = value[:, half * 128 : half * 128 + 128].astype(BF16)
            return
        tail = value[:, 128:256]
        packed = tail[0:8, :]
        for g in range(1, 8):
            packed = jnp.where(lane8 == g, pltpu.roll(tail[8 * g : 8 * g + 8, :], 16 * g, 1), packed)
        parts[1][slot + (0,)] = value[0:48, 0:128].astype(BF16)
        rest = [value[48:72, 0:128], packed, tail[64:72, :], jnp.zeros((8, 128), F32)]
        parts[1][slot + (1,)] = jnp.concatenate(rest, 0).astype(BF16)

    def fill(w, ab, at):
        left, right, size = ((r["h_t"], r["gpad"], 144), (r["att_t"], r["cpad"], 72))[w]
        left_pair, right_pair = ((r["h_t_pair"], r["gpad_pair"]), (r["att_t_pair"], r["cpad_pair"]))[w]
        rows = slice(ab * 2 * size, ab * 2 * size + 2 * size)
        for i in range(2 if x_first(w, ab) else 4):
            xx, lo = (at, i) if x_first(w, ab) else (i, at)
            b = 2 * xx + lo
            value = dot(left[core, rows, :], right[b]) + dot(left_pair[rows, :], right_pair[b])
            for hi in range(2):
                yy = hi * 2 + lo
                slot = (ab, xx, yy) if x_first(w, ab) else (ab, yy, xx)
                store(w, ab, slot, value[size * hi : size * hi + size, :])

    def start_ring(w, ab, k):
        if k == 0:
            one_copy(w, ab, 0).start()
            one_copy(w, ab, 1).start()
        elif k < 3:
            two_copy(w, ab, k - 1, 0).start()

    def pass_on(w, ab, way):
        one_copy(w, ab, way).wait_recv()
        me, _ = places(True, w, ab)
        to = (me + (1, 3)[way]) % 4
        for j in range(2):
            add_in(parts[w], (ab, to, 2 * way + j), one_recv[w], (ab, way, j))
        two_copy(w, ab, way, 1).start()

    def second_ring(w, ab):
        for way in range(2):
            for late in range(2):
                two_copy(w, ab, way, late).wait_recv()
        me, _ = places(True, w, ab)
        for j in range(4):
            mid[w][ab, j] = (
                parts[w][ab, me, j].astype(F32)
                + two_recv[w][ab, 0, j].astype(F32)
                + two_recv[w][ab, 1, j].astype(F32)
            ).astype(BF16)
        for step in (2, 1, 3):
            last_copy(w, ab, step).start()

    def ring_sum(w, ab, half):
        me, _ = places(False, w, ab)
        total = mid[w][ab, me, half].astype(F32)
        for i in range(3):
            total = total + last_recv[w][ab, i, half].astype(F32)
        return total

    def ring_wait(w, ab):
        for step in range(1, 4):
            last_copy(w, ab, step).wait_recv()

    pair_copy(5).wait_recv()
    for k in range(4):
        pair_copy(k).wait_recv()
        if k < 3:
            fill(0, 0, target(0, 0, k))
            start_ring(0, 0, k)
    fill(0, 1, y_lo)
    start_ring(0, 1, 0)
    fill(0, 1, 1 - y_lo)
    start_ring(0, 1, 1)
    start_ring(0, 1, 2)
    fill(0, 0, target(0, 0, 3))

    for ab, way in both:
        pass_on(0, ab, way)
    wait_exchange(2, r["at_recv"])
    r["acc"][:, 0:HD] = r["at_recv"][...].astype(F32).reshape(N, HD)
    r["att"][...] = r["acc"][:, 0:HD].astype(BF16)
    r["turn"][0:HD, :] = r["acc"][:, 0:HD].T
    for ab in range(2):
        for c in range(2):
            pieces = []
            for hi in range(2):
                for zz in range(4 * ab, 4 * ab + 4):
                    first = zz * 72 + hi * 36 + c * 18
                    pieces.append(r["turn"][first : first + 18, :])
            r["att_t"][c, ab * 144 : ab * 144 + 144, :] = jnp.concatenate(pieces, 0).astype(BF16)
    pair_copy(6).start()
    pair_copy(4).wait_recv()
    pair_copy(6).wait_recv()
    for k in range(4):
        for ab in range(2):
            fill(1, ab, target(1, ab, k))
            start_ring(1, ab, k)
    for ab, way in both:
        pass_on(1, ab, way)

    for ab in range(2):
        second_ring(0, ab)
    wait_exchange(3, r["gh_recv"])

    def norm_back_residual(i, carry):
        rows = rows_of(i)
        g = r["gh_recv"][slabs_of(i)].astype(F32).reshape(CHUNK, D)
        inverse = r["t_inv"][rows, 0:1]
        n = (r["res"][rows, :].astype(F32) - r["t_mean"][rows, 0:1]) * inverse
        back = inverse * (g - mean_of(g) - n * mean_of(g * n))
        r["gres"][rows, :] = (r["cot"][rows, :].astype(F32) + back).astype(BF16)
        return carry

    lax.fori_loop(0, N // CHUNK, norm_back_residual, 0, unroll=2)
    r["small"][:, 0:HD] = dot_nt(r["gres"][...], r["wso"][...]).astype(BF16)
    for ab in range(2):
        second_ring(1, ab)
    backward_heads(r["sq"], r["sk"], r["sv"], r["sw"], r["small"], r["accq"], r["acck"], r["accv"])
    z_send = (r["z_send_in"], r["z_send_out"])
    z_recv = (r["z_recv_in"], r["z_recv_out"])

    lane6 = lax.broadcasted_iota(jnp.int32, (6, 128), 1) // 16

    def give_z(w):
        for ab in range(2):
            for j in range(4):
                if w == 0:
                    for half in range(2):
                        piece = [r["zsum"][ab, half, 36 * j : 36 * j + 36, :], jnp.zeros((4, 128), F32)]
                        z_send[0][4 * ab + j, half] = jnp.concatenate(piece, 0).astype(BF16)
                else:
                    low = 144 + 18 * j
                    tail = r["zsum"][ab, 1, low : low + 6, :]
                    for g in range(1, 3):
                        more = r["zsum"][ab, 1, low + 6 * g : low + 6 * g + 6, :]
                        tail = jnp.where(lane6 == g, pltpu.roll(more, 16 * g, 1), tail)
                    piece = [r["zsum"][ab, 0, low : low + 18, :], tail]
                    z_send[1][4 * ab + j] = jnp.concatenate(piece, 0).astype(BF16)

        def z_one(k, carry):
            to = lax.rem(z + 4 + (k + 1) // 2 * (1 - 2 * (k % 2)), 8)
            remote(
                "z",
                src_ref=z_send[w].at[to], dst_ref=z_recv[w].at[z],
                send_sem=r["z_ssem"].at[w], recv_sem=r["z_rsem"].at[w],
                device_id=at_seq(to * 4 + y_hi * 2 + core), device_id_type=MESH,
            ).start()
            return carry

        lax.fori_loop(0, 7, z_one, 0)
        z_recv[w][z] = z_send[w][z]

    for ab in range(2):
        ring_wait(0, ab)
        for half in range(2):
            r["zsum"][ab, half, 0:144] = ring_sum(0, ab, half)
    give_z(0)
    join(r["nat"], r["accq"], r["acck"], r["accv"])
    for n in range(0, D, 384):
        r["big"][:, n : n + 384] = dot(r["nat"][:, 0 : 3 * HD], r["wsi"][:, n : n + 384])

    for ab in range(2):
        ring_wait(1, ab)
        first, rest = ring_sum(1, ab, 0), ring_sum(1, ab, 1)
        r["zsum"][ab, 0, 144:192] = first
        r["zsum"][ab, 0, 192:216] = rest[0:24, :]
        for g in range(8):
            tail = rest[24:32, :]
            r["zsum"][ab, 1, 144 + 8 * g : 152 + 8 * g] = pltpu.roll(tail, 128 - 16 * g, 1) if g else tail
        r["zsum"][ab, 1, 208:216] = rest[32:40, :]
    give_z(1)

    def norm_back_video(i, carry):
        rows = rows_of(i)
        g = r["big"][rows, :]
        inverse = r["s_inv"][rows, 0:1]
        n = (r["vid"][rows, :].astype(F32) - r["s_mean"][rows, 0:1]) * inverse
        back = inverse * (g - mean_of(g) - n * mean_of(g * n))
        o_gv[rows, :] = (r["gres"][rows, :].astype(F32) + back).astype(BF16)
        return carry

    lax.fori_loop(0, N // CHUNK, norm_back_video, 0, unroll=2)

    for n in range(0, D, 384):
        o_out[:, n : n + 384] = (
            r["res"][:, n : n + 384].astype(F32) + dot(r["att"][...], r["wto"][:, n : n + 384])
        ).astype(BF16)

    drain("z", z_recv[0].at[pl.ds(0, 7)], r["z_rsem"].at[0])
    for half in range(2):
        total = z_recv[0][0, half].astype(F32)
        for j in range(1, 8):
            total = total + z_recv[0][j, half].astype(F32)
        o_gi[:, half * 128 : (128, 216)[half]] = total[0:36, 0 : (128, 88)[half]]
    drain("z", z_recv[1].at[pl.ds(0, 7)], r["z_rsem"].at[1])
    total = z_recv[1][0].astype(F32)
    for j in range(1, 8):
        total = total + z_recv[1][j].astype(F32)
    o_go[:, 0:128] = total[0:18, :]
    for g in range(3):
        o_go[6 * g : 6 * g + 6, 128:144] = total[18:24, 16 * g : 16 * g + 16]

    for which, name in enumerate(("ga_send", "h_send", "at_send", "gh_send")):
        wait_sent(which, r[name])
    for i in range(7):
        pair_copy(i).wait_send()
    for w in range(2):
        for ab in range(2):
            for way in range(2):
                one_copy(w, ab, way).wait_send()
                for late in range(2):
                    two_copy(w, ab, way, late).wait_send()
            for step in range(1, 4):
                last_copy(w, ab, step).wait_send()
    for w in range(2):
        drain("z", z_send[w].at[pl.ds(0, 7)], r["z_ssem"].at[w])


def hand_over(*refs):
    for source, result in zip(refs[:4], refs[4:]):
        result[...] = source[...]


def local(video, spatial_in, spatial_out, temporal_in, temporal_out, cotangent):
    shapes = scratch_shapes()
    names = tuple(shapes)
    anywhere = pl.BlockSpec(memory_space=pl.ANY)
    whole = pl.BlockSpec(memory_space=pltpu.VMEM)

    def body(*refs):
        kernel(*refs[:10], names, *refs[10:])

    results = (
        jax.ShapeDtypeStruct((N, D), BF16),
        jax.ShapeDtypeStruct((N, D), BF16),
        jax.ShapeDtypeStruct((36, 216), F32),
        jax.ShapeDtypeStruct((18, 144), F32),
    )
    held = pl.pallas_call(
        body,
        out_shape=results,
        in_specs=[anywhere] * 6,
        out_specs=(whole,) * 4,
        scratch_shapes=list(shapes.values()),
        compiler_params=pltpu.CompilerParams(
            collective_id=0, has_side_effects=True, vmem_limit_bytes=60 * 1024 * 1024
        ),
        cost_estimate=pl.CostEstimate(flops=9_000_000_000, bytes_accessed=13_000_000, transcendentals=1_100_000),
    )(video.reshape(N, D), spatial_in.T, spatial_out, temporal_in.T, temporal_out, cotangent.reshape(N, D))
    out, grad_video, grad_in, grad_out = pl.pallas_call(
        hand_over,
        out_shape=results,
        in_specs=[whole] * 4,
        out_specs=(whole,) * 4,
        cost_estimate=pl.CostEstimate(flops=0, bytes_accessed=2_400_000, transcendentals=0),
    )(*held)
    return (out.reshape(video.shape), grad_video.reshape(video.shape), grad_in, grad_out)


def solution(mesh):
    in_specs = (P("dp", "seq", None, None), P(), P(), P(), P(), P("dp", "seq", None, None))
    out_specs = (
        P("dp", "seq", None, None),
        P("dp", "seq", None, None),
        P("seq", "dp"),
        P("seq", "dp"),
    )
    return jax.shard_map(local, mesh=mesh, in_specs=in_specs, out_specs=out_specs, check_vma=False)
```

```python
import jax
import jax.numpy as jnp
from jax import lax
from jax.experimental import pallas as pl
from jax.experimental.pallas import tpu as pltpu
from jax.sharding import PartitionSpec as P

HEADS = 8
HEAD = 72
D = 1152
HD = 576
N = 256
PAD = 640
FACTOR = HEAD ** (-0.5)
F32 = jnp.float32
BF16 = jnp.bfloat16
MESH = pl.DeviceIdType.MESH
CHUNK = 32


def dot(a, b):
    return jnp.dot(a, b, preferred_element_type=F32)


def dot_nt(a, b):
    return lax.dot_general(a, b, (((1,), (1,)), ((), ())), preferred_element_type=F32)


def dot_tn(a, b):
    return lax.dot_general(a, b, (((0,), (0,)), ((), ())), preferred_element_type=F32)


def remote(kind, **ends):
    return pltpu.make_async_remote_copy(**ends)


def drain(kind, some, sem):
    pltpu.make_async_copy(some, some, sem).wait()


def window(head):
    start = head * HEAD
    low = start // 128 * 128
    wide = 128 if start + HEAD <= low + 128 else 256
    return start - low, slice(low, low + wide), wide


def head_mask(offset, wide):
    lane = lax.broadcasted_iota(jnp.int32, (N, wide), 1)
    return (lane >= offset) & (lane < offset + HEAD)


def scratch_shapes():
    slab, thin = (2, 144, 128), (2, 48, 128)
    vm = lambda *shape: pltpu.VMEM(shape, BF16)
    vf = lambda *shape: pltpu.VMEM(shape, F32)
    dma = pltpu.SemaphoreType.DMA
    return dict(
        vid=vm(N, D), cot=vm(N, D), wsi=vm(3 * HD, D), wso=vm(HD, D), wti=vm(3 * HD, D), wto=vm(HD, D),
        ga_send=vm(32, 8, HD), ga_recv=vm(32, 8, HD), h_send=vm(32, 8, D), h_recv=vm(32, 8, D),
        at_send=vm(32, 8, HD), at_recv=vm(32, 8, HD), gh_send=vm(32, 8, D), gh_recv=vm(32, 8, D),
        sh=vm(N, D), sq=vm(N, PAD), sk=vm(N, PAD), sv=vm(N, PAD), sw=vm(HEADS, N, N),
        th=vm(N, D), tq=vm(N, PAD), tk=vm(N, PAD), tv=vm(N, PAD), tw=vm(HEADS, N, N),
        acc=vf(N, PAD), accq=vf(N, PAD), acck=vf(N, PAD), accv=vf(N, PAD),
        small=vm(N, PAD), nat=vm(N, 1792), big=vf(N, D),
        res=vm(N, D), gres=vm(N, D), att=vm(N, HD), s_mean=vf(N, 128), s_inv=vf(N, 128), t_mean=vf(N, 128), t_inv=vf(N, 128),
        turn=vf(D, N), h_t=vm(2, HD, N), att_t=vm(2, HD // 2, N), h_t_pair=vm(HD, N), att_t_pair=vm(HD // 2, N),
        gpad=vm(8, N, 256), cpad=vm(8, N, 256), gpad_pair=vm(8, N, 256), cpad_pair=vm(8, N, 256),
        part_in=vm(2, 4, 4, *slab), part_out=vm(2, 4, 4, *thin),
        one_in=vm(2, 2, 2, *slab), one_out=vm(2, 2, 2, *thin), two_in=vm(2, 2, 4, *slab), two_out=vm(2, 2, 4, *thin),
        mid_in=vm(2, 4, *slab), mid_out=vm(2, 4, *thin),
        last_in=vm(2, 3, *slab), last_out=vm(2, 3, *thin),
        zsum=vf(2, 2, 216, 128), z_send_in=vm(8, 2, 40, 128), z_recv_in=vm(8, 2, 40, 128),
        z_send_out=vm(8, 24, 128), z_recv_out=vm(8, 24, 128),
        load=dma((6,)), a_send=dma((4,)), a_recv=dma((4,)), c_ssem=dma((7,)), c_rsem=dma((7,)),
        one_ssem=dma((2, 2, 2)), one_rsem=dma((2, 2, 2)), two_ssem=dma((2, 2, 2, 2)), two_rsem=dma((2, 2, 2, 2)),
        last_ssem=dma((2, 2, 3)), last_rsem=dma((2, 2, 3)),
        z_ssem=dma((2,)), z_rsem=dma((2,)),
    )


def rows_of(step, size=CHUNK):
    return pl.ds(pl.multiple_of(step * size, size), size)


def slabs_of(step, size=CHUNK // 8):
    return pl.ds(step * size, size)


def mean_of(x):
    return jnp.sum(x, -1, keepdims=True) * (1.0 / D)


def normalize(x):
    center = x - mean_of(x)
    inverse = lax.rsqrt(mean_of(center * center) + 1e-06)
    return center, inverse


def project(src, w, q, k, v):
    x = src[...]
    q[...] = dot_nt(x, w[0:PAD, :]).astype(BF16)
    k[...] = dot_nt(x, w[HD : HD + PAD, :]).astype(BF16)
    v[:, 512:PAD] = jnp.zeros((N, 128), BF16)
    v[:, 0:HD] = dot_nt(x, w[D : 3 * HD, :]).astype(BF16)


def forward_heads(q, k, v, weights, acc, keep):
    for head in range(HEADS):
        offset, cut, wide = window(head)
        mine = head_mask(offset, wide)
        queries = jnp.where(mine, q[:, cut].astype(F32), 0.0).astype(BF16)
        p = jnp.exp(dot_nt(queries, k[:, cut]) * FACTOR)
        if keep is not None:
            p = jnp.where(keep, p, 0.0)
        w = (p * (1.0 / jnp.sum(p, -1, keepdims=True))).astype(BF16)
        weights[head] = w
        out = dot(w, v[:, cut])
        acc[:, cut] = out if head == 0 else jnp.where(mine, out, acc[:, cut])


def backward_heads(q, k, v, weights, grad, accq, acck, accv):
    for head in range(HEADS):
        offset, cut, wide = window(head)
        mine = head_mask(offset, wide)
        g = grad[:, cut]
        w = weights[head]
        e = dot_nt(jnp.where(mine, g.astype(F32), 0.0).astype(BF16), v[:, cut])
        p = w.astype(F32)
        r = (p * (e - jnp.sum(e * p, -1, keepdims=True)) * FACTOR).astype(BF16)
        for acc, out in ((accv, dot_tn(w, g)), (accq, dot(r, k[:, cut])), (acck, dot_tn(r, q[:, cut]))):
            acc[:, cut] = out if head == 0 else jnp.where(mine, out, acc[:, cut])


def join(nat, accq, acck, accv):
    lane = lax.broadcasted_iota(jnp.int32, (N, 128), 1)
    moved = pltpu.roll(acck[...], 64, 1)
    nat[:, 0:512] = accq[:, 0:512].astype(BF16)
    nat[:, 512:640] = jnp.where(lane < 64, accq[:, 512:640], moved[:, 0:128]).astype(BF16)
    nat[:, 640:1152] = moved[:, 128:640].astype(BF16)
    nat[:, 1152:1664] = accv[:, 0:512].astype(BF16)
    nat[:, 1664:1792] = jnp.where(lane < 64, accv[:, 512:640], 0.0).astype(BF16)


def kernel(vid_hbm, wsi_hbm, wso_hbm, wti_hbm, wto_hbm, cot_hbm, o_out, o_gv, o_gi, o_go, names, *refs):
    r = dict(zip(names, refs))
    seq = lax.axis_index("seq")
    dp = lax.axis_index("dp")
    z, y_hi, core = seq // 4, seq // 2 % 2, seq % 2
    x, y_lo = dp // 2, dp % 2
    y = y_hi * 2 + y_lo

    def at_seq(s):
        return {"seq": s, "dp": dp}

    def at_x(to):
        return {"seq": seq, "dp": to * 2 + y_lo}

    def at_y(to):
        return {"seq": z * 4 + to // 2 * 2 + core, "dp": x * 2 + to % 2}

    loads = []
    for i, (src, dst) in enumerate(
        ((cot_hbm, "cot"), (wto_hbm, "wto"), (vid_hbm, "vid"), (wsi_hbm, "wsi"), (wso_hbm, "wso"), (wti_hbm, "wti"))
    ):
        copy = pltpu.make_async_copy(src, r[dst], r["load"].at[i])
        copy.start()
        loads.append(copy)

    barrier = pltpu.get_barrier_semaphore()

    def greet(k, carry):
        pl.semaphore_signal(barrier, inc=1, device_id=at_seq(lax.rem(seq + k, 32)), device_id_type=MESH)
        return carry

    lax.fori_loop(1, 32, greet, 0)
    for step in (1, 2, 3):
        pl.semaphore_signal(barrier, inc=1, device_id=at_x((x + step) % 4), device_id_type=MESH)
    for step in (1, 3):
        pl.semaphore_signal(barrier, inc=1, device_id=at_y((y + step) % 4), device_id_type=MESH)

    def slab_copy(which, send, recv, to):
        return remote(
            "swap",
            src_ref=send.at[to],
            dst_ref=recv.at[seq],
            send_sem=r["a_send"].at[which],
            recv_sem=r["a_recv"].at[which],
            device_id=at_seq(to),
            device_id_type=MESH,
        )

    def send_chunk(which, send, recv, i):
        for j in range(4):
            to = i * 4 + lax.rem(seq + 2 + j, 4)

            @pl.when(to != seq)
            def _():
                slab_copy(which, send, recv, to).start()

    def exchange(which, send, recv):
        def one(i, carry):
            k = 16 + (i + 1) // 2 * (1 - 2 * (i % 2))
            slab_copy(which, send, recv, lax.rem(seq + k, 32)).start()
            return carry

        lax.fori_loop(0, 31, one, 0)
        recv[seq] = send[seq]

    def wait_exchange(which, recv):
        drain("swap", recv.at[pl.ds(0, 31)], r["a_recv"].at[which])

    def wait_sent(which, send):
        drain("swap", send.at[pl.ds(0, 31)], r["a_send"].at[which])

    loads[0].wait()
    loads[1].wait()
    ga = dot_nt(r["cot"][...], r["wto"][...])
    r["ga_send"][...] = ga.reshape(32, 8, HD).astype(BF16)
    pl.semaphore_wait(barrier, 36)
    exchange(0, r["ga_send"], r["ga_recv"])

    loads[2].wait()

    def norm_video(i, carry):
        rows = rows_of(i)
        v = r["vid"][rows, :].astype(F32)
        mean = mean_of(v)
        center = v - mean
        inverse = lax.rsqrt(mean_of(center * center) + 1e-06)
        r["s_mean"][rows, :] = jnp.broadcast_to(mean, (CHUNK, 128))
        r["s_inv"][rows, :] = jnp.broadcast_to(inverse, (CHUNK, 128))
        r["sh"][rows, :] = (center * inverse).astype(BF16)
        return carry

    lax.fori_loop(0, N // CHUNK, norm_video, 0, unroll=2)
    loads[3].wait()
    project(r["sh"], r["wsi"], r["sq"], r["sk"], r["sv"])
    forward_heads(r["sq"], r["sk"], r["sv"], r["sw"], r["acc"], None)
    r["small"][...] = r["acc"][...].astype(BF16)
    loads[4].wait()
    for n in range(0, D, 384):
        r["big"][:, n : n + 384] = dot(r["small"][:, 0:HD], r["wso"][:, n : n + 384])

    def norm_residual(step, carry):
        i = lax.rem(z + 4 + (step + 1) // 2 * (1 - 2 * (step % 2)), 8)
        rows = rows_of(i)
        v = (r["vid"][rows, :].astype(F32) + r["big"][rows, :]).astype(BF16)
        r["res"][rows, :] = v
        v = v.astype(F32)
        mean = mean_of(v)
        center = v - mean
        inverse = lax.rsqrt(mean_of(center * center) + 1e-06)
        r["t_mean"][rows, :] = jnp.broadcast_to(mean, (CHUNK, 128))
        r["t_inv"][rows, :] = jnp.broadcast_to(inverse, (CHUNK, 128))
        r["h_send"][slabs_of(i)] = (center * inverse).reshape(CHUNK // 8, 8, D).astype(BF16)
        send_chunk(1, r["h_send"], r["h_recv"], i)
        return carry

    lax.fori_loop(0, N // CHUNK, norm_residual, 0)
    r["h_recv"][seq] = r["h_send"][seq]

    turns = (2, 1, 3, 0)

    def pair_copy(i):
        if i < 4:
            blocks = pl.ds(2 * ((x + turns[i]) % 4), 2)
            src, dst = r["gpad"].at[blocks], r["gpad_pair"].at[blocks]
        elif i == 4:
            src, dst = r["cpad"], r["cpad_pair"]
        elif i == 5:
            src, dst = r["h_t"].at[1 - core], r["h_t_pair"]
        else:
            src, dst = r["att_t"].at[1 - core], r["att_t_pair"]
        return remote(
            "core",
            src_ref=src, dst_ref=dst, send_sem=r["c_ssem"].at[i], recv_sem=r["c_rsem"].at[i],
            device_id=at_seq(seq + 1 - 2 * core), device_id_type=MESH,
        )

    for b in range(8):
        part = r["cot"][:, 128 * b : 128 * b + 256].astype(F32)
        if b:
            part = pltpu.roll(part, 256 - 16 * b, 1)
        r["cpad"][b] = part.astype(BF16)
    pair_copy(4).start()
    loads[5].wait()

    wait_exchange(0, r["ga_recv"])
    r["small"][:, 512:PAD] = jnp.zeros((N, 128), BF16)
    r["small"][:, 0:HD] = r["ga_recv"][...].astype(F32).reshape(N, HD).astype(BF16)
    wait_exchange(1, r["h_recv"])

    def take_h(i, carry):
        v = r["h_recv"][slabs_of(i)].astype(F32).reshape(CHUNK, D)
        r["th"][rows_of(i), :] = v.astype(BF16)
        return carry

    lax.fori_loop(0, N // CHUNK, take_h, 0)
    project(r["th"], r["wti"], r["tq"], r["tk"], r["tv"])
    place = lax.broadcasted_iota(jnp.int32, (N, N), 0) % 8
    other = lax.broadcasted_iota(jnp.int32, (N, N), 1) % 8
    forward_heads(r["tq"], r["tk"], r["tv"], r["tw"], r["acc"], place == other)
    r["at_send"][...] = r["acc"][:, 0:HD].reshape(32, 8, HD).astype(BF16)
    exchange(2, r["at_send"], r["at_recv"])

    r["turn"][...] = r["th"][...].astype(F32).T
    for ab in range(2):
        for c in range(2):
            for hi in range(2):
                pieces = []
                for zz in range(4 * ab, 4 * ab + 4):
                    first = zz * 144 + hi * 72 + c * 36
                    pieces.append(r["turn"][first : first + 36, :])
                low = ab * 288 + hi * 144
                r["h_t"][c, low : low + 144, :] = jnp.concatenate(pieces, 0).astype(BF16)
    pair_copy(5).start()

    backward_heads(r["tq"], r["tk"], r["tv"], r["tw"], r["small"], r["accq"], r["acck"], r["accv"])
    join(r["nat"], r["accq"], r["acck"], r["accv"])
    for b in range(8):
        low = 216 * b // 128 * 128
        off = 216 * b - low
        part = r["nat"][:, low : low + 384].astype(F32)
        if off:
            part = pltpu.roll(part, 384 - off, 1)
        r["gpad"][b] = part[:, 0:256].astype(BF16)
    for k in range(4):
        pair_copy(k).start()
    for n in range(0, D, 384):
        r["big"][:, n : n + 384] = dot(r["nat"][:, 0 : 3 * HD], r["wti"][:, n : n + 384])

    def give_gh(step, carry):
        i = lax.rem(z + 4 + (step + 1) // 2 * (1 - 2 * (step % 2)), 8)
        r["gh_send"][slabs_of(i)] = r["big"][rows_of(i), :].reshape(CHUNK // 8, 8, D).astype(BF16)
        send_chunk(3, r["gh_send"], r["gh_recv"], i)
        return carry

    lax.fori_loop(0, N // CHUNK, give_gh, 0)
    r["gh_recv"][seq] = r["gh_send"][seq]

    parts = (r["part_in"], r["part_out"])
    one_recv = (r["one_in"], r["one_out"])
    two_recv = (r["two_in"], r["two_out"])
    mid = (r["mid_in"], r["mid_out"])
    last_recv = (r["last_in"], r["last_out"])
    both = ((0, 0), (1, 0), (0, 1), (1, 1))

    def x_first(w, ab):
        return w == 1 or ab == 0

    def places(first, w, ab):
        if x_first(w, ab) == first:
            return x, at_x
        return y, at_y

    def target(w, ab, k):
        me, _ = places(True, w, ab)
        return (me + turns[k]) % 4

    def one_copy(w, ab, way):
        me, where = places(True, w, ab)
        to = (me + (1, 3)[way]) % 4
        return remote(
            "one",
            src_ref=parts[w].at[ab, (me + 2) % 4, pl.ds(2 * way, 2)], dst_ref=one_recv[w].at[ab, way],
            send_sem=r["one_ssem"].at[w, ab, way], recv_sem=r["one_rsem"].at[w, ab, way],
            device_id=where(to), device_id_type=MESH,
        )

    def two_copy(w, ab, way, late):
        me, where = places(True, w, ab)
        to = (me + (1, 3)[way]) % 4
        low = 2 * way if late else 2 - 2 * way
        return remote(
            "two",
            src_ref=parts[w].at[ab, to, pl.ds(low, 2)], dst_ref=two_recv[w].at[ab, way, pl.ds(low, 2)],
            send_sem=r["two_ssem"].at[w, ab, way, late], recv_sem=r["two_rsem"].at[w, ab, way, late],
            device_id=where(to), device_id_type=MESH,
        )

    def last_copy(w, ab, step):
        me, where = places(False, w, ab)
        to = (me + step) % 4
        return remote(
            "last",
            src_ref=mid[w].at[ab, to], dst_ref=last_recv[w].at[ab, step - 1],
            send_sem=r["last_ssem"].at[w, ab, step - 1], recv_sem=r["last_rsem"].at[w, ab, step - 1],
            device_id=where(to), device_id_type=MESH,
        )

    def add_in(dst, dst_at, src, src_at):
        dst[dst_at] = (dst[dst_at].astype(F32) + src[src_at].astype(F32)).astype(BF16)

    lane8 = lax.broadcasted_iota(jnp.int32, (8, 128), 1) // 16

    def store(w, ab, slot, value):
        if w == 0:
            for half in range(2):
                parts[0][slot + (half,)] = value[:, half * 128 : half * 128 + 128].astype(BF16)
            return
        tail = value[:, 128:256]
        packed = tail[0:8, :]
        for g in range(1, 8):
            packed = jnp.where(lane8 == g, pltpu.roll(tail[8 * g : 8 * g + 8, :], 16 * g, 1), packed)
        parts[1][slot + (0,)] = value[0:48, 0:128].astype(BF16)
        rest = [value[48:72, 0:128], packed, tail[64:72, :], jnp.zeros((8, 128), F32)]
        parts[1][slot + (1,)] = jnp.concatenate(rest, 0).astype(BF16)

    def fill(w, ab, at):
        left, right, size = ((r["h_t"], r["gpad"], 144), (r["att_t"], r["cpad"], 72))[w]
        left_pair, right_pair = ((r["h_t_pair"], r["gpad_pair"]), (r["att_t_pair"], r["cpad_pair"]))[w]
        rows = slice(ab * 2 * size, ab * 2 * size + 2 * size)
        for i in range(2 if x_first(w, ab) else 4):
            xx, lo = (at, i) if x_first(w, ab) else (i, at)
            b = 2 * xx + lo
            value = dot(left[core, rows, :], right[b]) + dot(left_pair[rows, :], right_pair[b])
            for hi in range(2):
                yy = hi * 2 + lo
                slot = (ab, xx, yy) if x_first(w, ab) else (ab, yy, xx)
                store(w, ab, slot, value[size * hi : size * hi + size, :])

    def start_ring(w, ab, k):
        if k == 0:
            one_copy(w, ab, 0).start()
            one_copy(w, ab, 1).start()
        elif k < 3:
            two_copy(w, ab, k - 1, 0).start()

    def pass_on(w, ab, way):
        one_copy(w, ab, way).wait_recv()
        me, _ = places(True, w, ab)
        to = (me + (1, 3)[way]) % 4
        for j in range(2):
            add_in(parts[w], (ab, to, 2 * way + j), one_recv[w], (ab, way, j))
        two_copy(w, ab, way, 1).start()

    def second_ring(w, ab):
        for way in range(2):
            for late in range(2):
                two_copy(w, ab, way, late).wait_recv()
        me, _ = places(True, w, ab)
        for j in range(4):
            mid[w][ab, j] = (
                parts[w][ab, me, j].astype(F32)
                + two_recv[w][ab, 0, j].astype(F32)
                + two_recv[w][ab, 1, j].astype(F32)
            ).astype(BF16)
        for step in (2, 1, 3):
            last_copy(w, ab, step).start()

    def ring_sum(w, ab, half):
        me, _ = places(False, w, ab)
        total = mid[w][ab, me, half].astype(F32)
        for i in range(3):
            total = total + last_recv[w][ab, i, half].astype(F32)
        return total

    def ring_wait(w, ab):
        for step in range(1, 4):
            last_copy(w, ab, step).wait_recv()

    pair_copy(5).wait_recv()
    for k in range(4):
        pair_copy(k).wait_recv()
        if k < 3:
            fill(0, 0, target(0, 0, k))
            start_ring(0, 0, k)
    fill(0, 1, y_lo)
    start_ring(0, 1, 0)
    fill(0, 1, 1 - y_lo)
    start_ring(0, 1, 1)
    start_ring(0, 1, 2)
    fill(0, 0, target(0, 0, 3))

    for ab, way in both:
        pass_on(0, ab, way)
    wait_exchange(2, r["at_recv"])
    r["acc"][:, 0:HD] = r["at_recv"][...].astype(F32).reshape(N, HD)
    r["att"][...] = r["acc"][:, 0:HD].astype(BF16)
    r["turn"][0:HD, :] = r["acc"][:, 0:HD].T
    for ab in range(2):
        for c in range(2):
            pieces = []
            for hi in range(2):
                for zz in range(4 * ab, 4 * ab + 4):
                    first = zz * 72 + hi * 36 + c * 18
                    pieces.append(r["turn"][first : first + 18, :])
            r["att_t"][c, ab * 144 : ab * 144 + 144, :] = jnp.concatenate(pieces, 0).astype(BF16)
    pair_copy(6).start()
    pair_copy(4).wait_recv()
    pair_copy(6).wait_recv()
    for k in range(4):
        for ab in range(2):
            fill(1, ab, target(1, ab, k))
            start_ring(1, ab, k)
    for ab, way in both:
        pass_on(1, ab, way)

    for ab in range(2):
        second_ring(0, ab)
    wait_exchange(3, r["gh_recv"])

    def norm_back_residual(i, carry):
        rows = rows_of(i)
        g = r["gh_recv"][slabs_of(i)].astype(F32).reshape(CHUNK, D)
        inverse = r["t_inv"][rows, 0:1]
        n = (r["res"][rows, :].astype(F32) - r["t_mean"][rows, 0:1]) * inverse
        back = inverse * (g - mean_of(g) - n * mean_of(g * n))
        r["gres"][rows, :] = (r["cot"][rows, :].astype(F32) + back).astype(BF16)
        return carry

    lax.fori_loop(0, N // CHUNK, norm_back_residual, 0, unroll=4)
    r["small"][:, 0:HD] = dot_nt(r["gres"][...], r["wso"][...]).astype(BF16)
    for ab in range(2):
        second_ring(1, ab)
    backward_heads(r["sq"], r["sk"], r["sv"], r["sw"], r["small"], r["accq"], r["acck"], r["accv"])
    z_send = (r["z_send_in"], r["z_send_out"])
    z_recv = (r["z_recv_in"], r["z_recv_out"])

    lane6 = lax.broadcasted_iota(jnp.int32, (6, 128), 1) // 16

    def give_z(w):
        for ab in range(2):
            for j in range(4):
                if w == 0:
                    for half in range(2):
                        piece = [r["zsum"][ab, half, 36 * j : 36 * j + 36, :], jnp.zeros((4, 128), F32)]
                        z_send[0][4 * ab + j, half] = jnp.concatenate(piece, 0).astype(BF16)
                else:
                    low = 144 + 18 * j
                    tail = r["zsum"][ab, 1, low : low + 6, :]
                    for g in range(1, 3):
                        more = r["zsum"][ab, 1, low + 6 * g : low + 6 * g + 6, :]
                        tail = jnp.where(lane6 == g, pltpu.roll(more, 16 * g, 1), tail)
                    piece = [r["zsum"][ab, 0, low : low + 18, :], tail]
                    z_send[1][4 * ab + j] = jnp.concatenate(piece, 0).astype(BF16)

        def z_one(k, carry):
            to = lax.rem(z + 4 + (k + 1) // 2 * (1 - 2 * (k % 2)), 8)
            remote(
                "z",
                src_ref=z_send[w].at[to], dst_ref=z_recv[w].at[z],
                send_sem=r["z_ssem"].at[w], recv_sem=r["z_rsem"].at[w],
                device_id=at_seq(to * 4 + y_hi * 2 + core), device_id_type=MESH,
            ).start()
            return carry

        lax.fori_loop(0, 7, z_one, 0)
        z_recv[w][z] = z_send[w][z]

    for ab in range(2):
        ring_wait(0, ab)
        for half in range(2):
            r["zsum"][ab, half, 0:144] = ring_sum(0, ab, half)
    give_z(0)
    join(r["nat"], r["accq"], r["acck"], r["accv"])
    for ab in range(2):
        ring_wait(1, ab)
        first, rest = ring_sum(1, ab, 0), ring_sum(1, ab, 1)
        r["zsum"][ab, 0, 144:192] = first
        r["zsum"][ab, 0, 192:216] = rest[0:24, :]
        for g in range(8):
            tail = rest[24:32, :]
            r["zsum"][ab, 1, 144 + 8 * g : 152 + 8 * g] = pltpu.roll(tail, 128 - 16 * g, 1) if g else tail
        r["zsum"][ab, 1, 208:216] = rest[32:40, :]
    give_z(1)

    for n in range(0, D, 384):
        r["big"][:, n : n + 384] = dot(r["nat"][:, 0 : 3 * HD], r["wsi"][:, n : n + 384])

    def norm_back_video(i, carry):
        rows = rows_of(i)
        g = r["big"][rows, :]
        inverse = r["s_inv"][rows, 0:1]
        n = (r["vid"][rows, :].astype(F32) - r["s_mean"][rows, 0:1]) * inverse
        back = inverse * (g - mean_of(g) - n * mean_of(g * n))
        o_gv[rows, :] = (r["gres"][rows, :].astype(F32) + back).astype(BF16)
        return carry

    lax.fori_loop(0, N // CHUNK, norm_back_video, 0, unroll=4)

    for n in range(0, D, 384):
        o_out[:, n : n + 384] = (
            r["res"][:, n : n + 384].astype(F32) + dot(r["att"][...], r["wto"][:, n : n + 384])
        ).astype(BF16)

    drain("z", z_recv[0].at[pl.ds(0, 7)], r["z_rsem"].at[0])
    for half in range(2):
        total = z_recv[0][0, half].astype(F32)
        for j in range(1, 8):
            total = total + z_recv[0][j, half].astype(F32)
        o_gi[:, half * 128 : (128, 216)[half]] = total[0:36, 0 : (128, 88)[half]]
    drain("z", z_recv[1].at[pl.ds(0, 7)], r["z_rsem"].at[1])
    total = z_recv[1][0].astype(F32)
    for j in range(1, 8):
        total = total + z_recv[1][j].astype(F32)
    o_go[:, 0:128] = total[0:18, :]
    for g in range(3):
        o_go[6 * g : 6 * g + 6, 128:144] = total[18:24, 16 * g : 16 * g + 16]

    for which, name in enumerate(("ga_send", "h_send", "at_send", "gh_send")):
        wait_sent(which, r[name])
    for i in range(7):
        pair_copy(i).wait_send()
    for w in range(2):
        for ab in range(2):
            for way in range(2):
                one_copy(w, ab, way).wait_send()
                for late in range(2):
                    two_copy(w, ab, way, late).wait_send()
            for step in range(1, 4):
                last_copy(w, ab, step).wait_send()
    for w in range(2):
        drain("z", z_send[w].at[pl.ds(0, 7)], r["z_ssem"].at[w])


def hand_over(*refs):
    for source, result in zip(refs[:4], refs[4:]):
        result[...] = source[...]


def local(video, spatial_in, spatial_out, temporal_in, temporal_out, cotangent):
    shapes = scratch_shapes()
    names = tuple(shapes)
    anywhere = pl.BlockSpec(memory_space=pl.ANY)
    whole = pl.BlockSpec(memory_space=pltpu.VMEM)

    def body(*refs):
        kernel(*refs[:10], names, *refs[10:])

    results = (
        jax.ShapeDtypeStruct((N, D), BF16),
        jax.ShapeDtypeStruct((N, D), BF16),
        jax.ShapeDtypeStruct((36, 216), F32),
        jax.ShapeDtypeStruct((18, 144), F32),
    )
    held = pl.pallas_call(
        body,
        out_shape=results,
        in_specs=[anywhere] * 6,
        out_specs=(whole,) * 4,
        scratch_shapes=list(shapes.values()),
        compiler_params=pltpu.CompilerParams(
            collective_id=0, has_side_effects=True, vmem_limit_bytes=60 * 1024 * 1024
        ),
        cost_estimate=pl.CostEstimate(flops=9_000_000_000, bytes_accessed=13_000_000, transcendentals=1_100_000),
    )(video.reshape(N, D), spatial_in.T, spatial_out, temporal_in.T, temporal_out, cotangent.reshape(N, D))
    out, grad_video, grad_in, grad_out = pl.pallas_call(
        hand_over,
        out_shape=results,
        in_specs=[whole] * 4,
        out_specs=(whole,) * 4,
        cost_estimate=pl.CostEstimate(flops=0, bytes_accessed=2_400_000, transcendentals=0),
    )(*held)
    return (out.reshape(video.shape), grad_video.reshape(video.shape), grad_in, grad_out)


def solution(mesh):
    in_specs = (P("dp", "seq", None, None), P(), P(), P(), P(), P("dp", "seq", None, None))
    out_specs = (
        P("dp", "seq", None, None),
        P("dp", "seq", None, None),
        P("seq", "dp"),
        P("seq", "dp"),
    )
    return jax.shard_map(local, mesh=mesh, in_specs=in_specs, out_specs=out_specs, check_vma=False)
```

```python
import jax
import jax.numpy as jnp
from jax import lax
from jax.experimental import pallas as pl
from jax.experimental.pallas import tpu as pltpu
from jax.sharding import PartitionSpec as P

HEADS = 8
HEAD = 72
D = 1152
HD = 576
N = 256
PAD = 640
FACTOR = HEAD ** (-0.5)
F32 = jnp.float32
BF16 = jnp.bfloat16
MESH = pl.DeviceIdType.MESH
CHUNK = 32


def dot(a, b):
    return jnp.dot(a, b, preferred_element_type=F32)


def dot_nt(a, b):
    return lax.dot_general(a, b, (((1,), (1,)), ((), ())), preferred_element_type=F32)


def dot_tn(a, b):
    return lax.dot_general(a, b, (((0,), (0,)), ((), ())), preferred_element_type=F32)


def remote(kind, **ends):
    return pltpu.make_async_remote_copy(**ends)


def drain(kind, some, sem):
    pltpu.make_async_copy(some, some, sem).wait()


def window(head):
    start = head * HEAD
    low = start // 128 * 128
    wide = 128 if start + HEAD <= low + 128 else 256
    return start - low, slice(low, low + wide), wide


def head_mask(offset, wide):
    lane = lax.broadcasted_iota(jnp.int32, (N, wide), 1)
    return (lane >= offset) & (lane < offset + HEAD)


def scratch_shapes():
    slab, thin = (2, 144, 128), (2, 48, 128)
    vm = lambda *shape: pltpu.VMEM(shape, BF16)
    vf = lambda *shape: pltpu.VMEM(shape, F32)
    dma = pltpu.SemaphoreType.DMA
    return dict(
        vid=vm(N, D), cot=vm(N, D), wsi=vm(3 * HD, D), wso=vm(HD, D), wti=vm(3 * HD, D), wto=vm(HD, D),
        ga_send=vm(32, 8, HD), ga_recv=vm(32, 8, HD), h_send=vm(32, 8, D), h_recv=vm(32, 8, D),
        at_send=vm(32, 8, HD), at_recv=vm(32, 8, HD), gh_send=vm(32, 8, D), gh_recv=vm(32, 8, D),
        sh=vm(N, D), sq=vm(N, PAD), sk=vm(N, PAD), sv=vm(N, PAD), sw=vm(HEADS, N, N),
        th=vm(N, D), tq=vm(N, PAD), tk=vm(N, PAD), tv=vm(N, PAD), tw=vm(HEADS, N, N),
        acc=vf(N, PAD), accq=vf(N, PAD), acck=vf(N, PAD), accv=vf(N, PAD),
        small=vm(N, PAD), nat=vm(N, 1792), big=vf(N, D),
        res=vm(N, D), gres=vm(N, D), att=vm(N, HD), s_mean=vf(N, 128), s_inv=vf(N, 128), t_mean=vf(N, 128), t_inv=vf(N, 128),
        turn=vf(D, N), h_t=vm(2, HD, N), att_t=vm(2, HD // 2, N), h_t_pair=vm(HD, N), att_t_pair=vm(HD // 2, N),
        gpad=vm(8, N, 256), cpad=vm(8, N, 256), gpad_pair=vm(8, N, 256), cpad_pair=vm(8, N, 256),
        part_in=vm(2, 4, 4, *slab), part_out=vm(2, 4, 4, *thin),
        one_in=vm(2, 2, 2, *slab), one_out=vm(2, 2, 2, *thin), two_in=vm(2, 2, 4, *slab), two_out=vm(2, 2, 4, *thin),
        mid_in=vm(2, 4, *slab), mid_out=vm(2, 4, *thin),
        last_in=vm(2, 3, *slab), last_out=vm(2, 3, *thin),
        zsum=vf(2, 2, 216, 128), z_send_in=vm(8, 2, 40, 128), z_recv_in=vm(8, 2, 40, 128),
        z_send_out=vm(8, 24, 128), z_recv_out=vm(8, 24, 128),
        load=dma((6,)), a_send=dma((4,)), a_recv=dma((4,)), c_ssem=dma((7,)), c_rsem=dma((7,)),
        one_ssem=dma((2, 2, 2)), one_rsem=dma((2, 2, 2)), two_ssem=dma((2, 2, 2, 2)), two_rsem=dma((2, 2, 2, 2)),
        last_ssem=dma((2, 2, 3)), last_rsem=dma((2, 2, 3)),
        z_ssem=dma((2,)), z_rsem=dma((2,)),
    )


def rows_of(step, size=CHUNK):
    return pl.ds(pl.multiple_of(step * size, size), size)


def slabs_of(step, size=CHUNK // 8):
    return pl.ds(step * size, size)


def mean_of(x):
    return jnp.sum(x, -1, keepdims=True) * (1.0 / D)


def normalize(x):
    center = x - mean_of(x)
    inverse = lax.rsqrt(mean_of(center * center) + 1e-06)
    return center, inverse


def project(src, w, q, k, v):
    x = src[...]
    q[...] = dot_nt(x, w[0:PAD, :]).astype(BF16)
    k[...] = dot_nt(x, w[HD : HD + PAD, :]).astype(BF16)
    v[:, 512:PAD] = jnp.zeros((N, 128), BF16)
    v[:, 0:HD] = dot_nt(x, w[D : 3 * HD, :]).astype(BF16)


def forward_heads(q, k, v, weights, acc, keep):
    for head in range(HEADS):
        offset, cut, wide = window(head)
        mine = head_mask(offset, wide)
        queries = jnp.where(mine, q[:, cut].astype(F32), 0.0).astype(BF16)
        p = jnp.exp(dot_nt(queries, k[:, cut]) * FACTOR)
        if keep is not None:
            p = jnp.where(keep, p, 0.0)
        w = (p * (1.0 / jnp.sum(p, -1, keepdims=True))).astype(BF16)
        weights[head] = w
        out = dot(w, v[:, cut])
        acc[:, cut] = out if head == 0 else jnp.where(mine, out, acc[:, cut])


def backward_heads(q, k, v, weights, grad, accq, acck, accv):
    for head in range(HEADS):
        offset, cut, wide = window(head)
        mine = head_mask(offset, wide)
        g = grad[:, cut]
        w = weights[head]
        e = dot_nt(jnp.where(mine, g.astype(F32), 0.0).astype(BF16), v[:, cut])
        p = w.astype(F32)
        r = (p * (e - jnp.sum(e * p, -1, keepdims=True)) * FACTOR).astype(BF16)
        for acc, out in ((accv, dot_tn(w, g)), (accq, dot(r, k[:, cut])), (acck, dot_tn(r, q[:, cut]))):
            acc[:, cut] = out if head == 0 else jnp.where(mine, out, acc[:, cut])


def join(nat, accq, acck, accv):
    lane = lax.broadcasted_iota(jnp.int32, (N, 128), 1)
    moved = pltpu.roll(acck[...], 64, 1)
    nat[:, 0:512] = accq[:, 0:512].astype(BF16)
    nat[:, 512:640] = jnp.where(lane < 64, accq[:, 512:640], moved[:, 0:128]).astype(BF16)
    nat[:, 640:1152] = moved[:, 128:640].astype(BF16)
    nat[:, 1152:1664] = accv[:, 0:512].astype(BF16)
    nat[:, 1664:1792] = jnp.where(lane < 64, accv[:, 512:640], 0.0).astype(BF16)


def kernel(vid_hbm, wsi_hbm, wso_hbm, wti_hbm, wto_hbm, cot_hbm, o_out, o_gv, o_gi, o_go, names, *refs):
    r = dict(zip(names, refs))
    seq = lax.axis_index("seq")
    dp = lax.axis_index("dp")
    z, y_hi, core = seq // 4, seq // 2 % 2, seq % 2
    x, y_lo = dp // 2, dp % 2
    y = y_hi * 2 + y_lo

    def at_seq(s):
        return {"seq": s, "dp": dp}

    def at_x(to):
        return {"seq": seq, "dp": to * 2 + y_lo}

    def at_y(to):
        return {"seq": z * 4 + to // 2 * 2 + core, "dp": x * 2 + to % 2}

    loads = []
    for i, (src, dst) in enumerate(
        ((cot_hbm, "cot"), (wto_hbm, "wto"), (vid_hbm, "vid"), (wsi_hbm, "wsi"), (wso_hbm, "wso"), (wti_hbm, "wti"))
    ):
        copy = pltpu.make_async_copy(src, r[dst], r["load"].at[i])
        copy.start()
        loads.append(copy)

    barrier = pltpu.get_barrier_semaphore()

    def greet(k, carry):
        pl.semaphore_signal(barrier, inc=1, device_id=at_seq(lax.rem(seq + k, 32)), device_id_type=MESH)
        return carry

    lax.fori_loop(1, 32, greet, 0)
    for step in (1, 2, 3):
        pl.semaphore_signal(barrier, inc=1, device_id=at_x((x + step) % 4), device_id_type=MESH)
    for step in (1, 3):
        pl.semaphore_signal(barrier, inc=1, device_id=at_y((y + step) % 4), device_id_type=MESH)

    def slab_copy(which, send, recv, to):
        return remote(
            "swap",
            src_ref=send.at[to],
            dst_ref=recv.at[seq],
            send_sem=r["a_send"].at[which],
            recv_sem=r["a_recv"].at[which],
            device_id=at_seq(to),
            device_id_type=MESH,
        )

    def send_chunk(which, send, recv, i):
        for j in range(4):
            to = i * 4 + lax.rem(seq + 2 + j, 4)

            @pl.when(to != seq)
            def _():
                slab_copy(which, send, recv, to).start()

    def exchange(which, send, recv):
        def one(i, carry):
            k = 16 + (i + 1) // 2 * (1 - 2 * (i % 2))
            slab_copy(which, send, recv, lax.rem(seq + k, 32)).start()
            return carry

        lax.fori_loop(0, 31, one, 0)
        recv[seq] = send[seq]

    def wait_exchange(which, recv):
        drain("swap", recv.at[pl.ds(0, 31)], r["a_recv"].at[which])

    def wait_sent(which, send):
        drain("swap", send.at[pl.ds(0, 31)], r["a_send"].at[which])

    loads[0].wait()
    loads[1].wait()
    ga = dot_nt(r["cot"][...], r["wto"][...])
    r["ga_send"][...] = ga.reshape(32, 8, HD).astype(BF16)
    pl.semaphore_wait(barrier, 36)
    exchange(0, r["ga_send"], r["ga_recv"])

    loads[2].wait()

    def norm_video(i, carry):
        rows = rows_of(i)
        v = r["vid"][rows, :].astype(F32)
        mean = mean_of(v)
        center = v - mean
        inverse = lax.rsqrt(mean_of(center * center) + 1e-06)
        r["s_mean"][rows, :] = jnp.broadcast_to(mean, (CHUNK, 128))
        r["s_inv"][rows, :] = jnp.broadcast_to(inverse, (CHUNK, 128))
        r["sh"][rows, :] = (center * inverse).astype(BF16)
        return carry

    lax.fori_loop(0, N // CHUNK, norm_video, 0, unroll=2)
    loads[3].wait()
    project(r["sh"], r["wsi"], r["sq"], r["sk"], r["sv"])
    forward_heads(r["sq"], r["sk"], r["sv"], r["sw"], r["acc"], None)
    r["small"][...] = r["acc"][...].astype(BF16)
    loads[4].wait()
    for n in range(0, D, 384):
        r["big"][:, n : n + 384] = dot(r["small"][:, 0:HD], r["wso"][:, n : n + 384])

    def norm_residual(step, carry):
        i = lax.rem(z + 4 + (step + 1) // 2 * (1 - 2 * (step % 2)), 8)
        rows = rows_of(i)
        v = (r["vid"][rows, :].astype(F32) + r["big"][rows, :]).astype(BF16)
        r["res"][rows, :] = v
        v = v.astype(F32)
        mean = mean_of(v)
        center = v - mean
        inverse = lax.rsqrt(mean_of(center * center) + 1e-06)
        r["t_mean"][rows, :] = jnp.broadcast_to(mean, (CHUNK, 128))
        r["t_inv"][rows, :] = jnp.broadcast_to(inverse, (CHUNK, 128))
        r["h_send"][slabs_of(i)] = (center * inverse).reshape(CHUNK // 8, 8, D).astype(BF16)
        send_chunk(1, r["h_send"], r["h_recv"], i)
        return carry

    lax.fori_loop(0, N // CHUNK, norm_residual, 0)
    r["h_recv"][seq] = r["h_send"][seq]

    turns = (2, 1, 3, 0)

    def pair_copy(i):
        if i < 4:
            blocks = pl.ds(2 * ((x + turns[i]) % 4), 2)
            src, dst = r["gpad"].at[blocks], r["gpad_pair"].at[blocks]
        elif i == 4:
            src, dst = r["cpad"], r["cpad_pair"]
        elif i == 5:
            src, dst = r["h_t"].at[1 - core], r["h_t_pair"]
        else:
            src, dst = r["att_t"].at[1 - core], r["att_t_pair"]
        return remote(
            "core",
            src_ref=src, dst_ref=dst, send_sem=r["c_ssem"].at[i], recv_sem=r["c_rsem"].at[i],
            device_id=at_seq(seq + 1 - 2 * core), device_id_type=MESH,
        )

    for b in range(8):
        part = r["cot"][:, 128 * b : 128 * b + 256].astype(F32)
        if b:
            part = pltpu.roll(part, 256 - 16 * b, 1)
        r["cpad"][b] = part.astype(BF16)
    pair_copy(4).start()
    loads[5].wait()

    wait_exchange(0, r["ga_recv"])
    r["small"][:, 512:PAD] = jnp.zeros((N, 128), BF16)
    r["small"][:, 0:HD] = r["ga_recv"][...].astype(F32).reshape(N, HD).astype(BF16)
    wait_exchange(1, r["h_recv"])

    def take_h(i, carry):
        v = r["h_recv"][slabs_of(i)].astype(F32).reshape(CHUNK, D)
        r["th"][rows_of(i), :] = v.astype(BF16)
        return carry

    lax.fori_loop(0, N // CHUNK, take_h, 0)
    project(r["th"], r["wti"], r["tq"], r["tk"], r["tv"])
    place = lax.broadcasted_iota(jnp.int32, (N, N), 0) % 8
    other = lax.broadcasted_iota(jnp.int32, (N, N), 1) % 8
    forward_heads(r["tq"], r["tk"], r["tv"], r["tw"], r["acc"], place == other)
    r["at_send"][...] = r["acc"][:, 0:HD].reshape(32, 8, HD).astype(BF16)
    exchange(2, r["at_send"], r["at_recv"])

    r["turn"][...] = r["th"][...].astype(F32).T
    for ab in range(2):
        for c in range(2):
            for hi in range(2):
                pieces = []
                for zz in range(4 * ab, 4 * ab + 4):
                    first = zz * 144 + hi * 72 + c * 36
                    pieces.append(r["turn"][first : first + 36, :])
                low = ab * 288 + hi * 144
                r["h_t"][c, low : low + 144, :] = jnp.concatenate(pieces, 0).astype(BF16)
    pair_copy(5).start()

    backward_heads(r["tq"], r["tk"], r["tv"], r["tw"], r["small"], r["accq"], r["acck"], r["accv"])
    join(r["nat"], r["accq"], r["acck"], r["accv"])
    for b in range(8):
        low = 216 * b // 128 * 128
        off = 216 * b - low
        part = r["nat"][:, low : low + 384].astype(F32)
        if off:
            part = pltpu.roll(part, 384 - off, 1)
        r["gpad"][b] = part[:, 0:256].astype(BF16)
    for k in range(4):
        pair_copy(k).start()
    for n in range(0, D, 384):
        r["big"][:, n : n + 384] = dot(r["nat"][:, 0 : 3 * HD], r["wti"][:, n : n + 384])

    def give_gh(step, carry):
        i = lax.rem(z + 4 + (step + 1) // 2 * (1 - 2 * (step % 2)), 8)
        r["gh_send"][slabs_of(i)] = r["big"][rows_of(i), :].reshape(CHUNK // 8, 8, D).astype(BF16)
        send_chunk(3, r["gh_send"], r["gh_recv"], i)
        return carry

    lax.fori_loop(0, N // CHUNK, give_gh, 0)
    r["gh_recv"][seq] = r["gh_send"][seq]

    parts = (r["part_in"], r["part_out"])
    one_recv = (r["one_in"], r["one_out"])
    two_recv = (r["two_in"], r["two_out"])
    mid = (r["mid_in"], r["mid_out"])
    last_recv = (r["last_in"], r["last_out"])
    both = ((0, 0), (1, 0), (0, 1), (1, 1))

    def x_first(w, ab):
        return w == 1 or ab == 0

    def places(first, w, ab):
        if x_first(w, ab) == first:
            return x, at_x
        return y, at_y

    def target(w, ab, k):
        me, _ = places(True, w, ab)
        return (me + turns[k]) % 4

    def one_copy(w, ab, way):
        me, where = places(True, w, ab)
        to = (me + (1, 3)[way]) % 4
        return remote(
            "one",
            src_ref=parts[w].at[ab, (me + 2) % 4, pl.ds(2 * way, 2)], dst_ref=one_recv[w].at[ab, way],
            send_sem=r["one_ssem"].at[w, ab, way], recv_sem=r["one_rsem"].at[w, ab, way],
            device_id=where(to), device_id_type=MESH,
        )

    def two_copy(w, ab, way, late):
        me, where = places(True, w, ab)
        to = (me + (1, 3)[way]) % 4
        low = 2 * way if late else 2 - 2 * way
        return remote(
            "two",
            src_ref=parts[w].at[ab, to, pl.ds(low, 2)], dst_ref=two_recv[w].at[ab, way, pl.ds(low, 2)],
            send_sem=r["two_ssem"].at[w, ab, way, late], recv_sem=r["two_rsem"].at[w, ab, way, late],
            device_id=where(to), device_id_type=MESH,
        )

    def last_copy(w, ab, step):
        me, where = places(False, w, ab)
        to = (me + step) % 4
        return remote(
            "last",
            src_ref=mid[w].at[ab, to], dst_ref=last_recv[w].at[ab, step - 1],
            send_sem=r["last_ssem"].at[w, ab, step - 1], recv_sem=r["last_rsem"].at[w, ab, step - 1],
            device_id=where(to), device_id_type=MESH,
        )

    def add_in(dst, dst_at, src, src_at):
        dst[dst_at] = (dst[dst_at].astype(F32) + src[src_at].astype(F32)).astype(BF16)

    lane8 = lax.broadcasted_iota(jnp.int32, (8, 128), 1) // 16

    def store(w, ab, slot, value):
        if w == 0:
            for half in range(2):
                parts[0][slot + (half,)] = value[:, half * 128 : half * 128 + 128].astype(BF16)
            return
        tail = value[:, 128:256]
        packed = tail[0:8, :]
        for g in range(1, 8):
            packed = jnp.where(lane8 == g, pltpu.roll(tail[8 * g : 8 * g + 8, :], 16 * g, 1), packed)
        parts[1][slot + (0,)] = value[0:48, 0:128].astype(BF16)
        rest = [value[48:72, 0:128], packed, tail[64:72, :], jnp.zeros((8, 128), F32)]
        parts[1][slot + (1,)] = jnp.concatenate(rest, 0).astype(BF16)

    def fill(w, ab, at):
        left, right, size = ((r["h_t"], r["gpad"], 144), (r["att_t"], r["cpad"], 72))[w]
        left_pair, right_pair = ((r["h_t_pair"], r["gpad_pair"]), (r["att_t_pair"], r["cpad_pair"]))[w]
        rows = slice(ab * 2 * size, ab * 2 * size + 2 * size)
        for i in range(2 if x_first(w, ab) else 4):
            xx, lo = (at, i) if x_first(w, ab) else (i, at)
            b = 2 * xx + lo
            value = dot(left[core, rows, :], right[b]) + dot(left_pair[rows, :], right_pair[b])
            for hi in range(2):
                yy = hi * 2 + lo
                slot = (ab, xx, yy) if x_first(w, ab) else (ab, yy, xx)
                store(w, ab, slot, value[size * hi : size * hi + size, :])

    def start_ring(w, ab, k):
        if k == 0:
            one_copy(w, ab, 0).start()
            one_copy(w, ab, 1).start()
        elif k < 3:
            two_copy(w, ab, k - 1, 0).start()

    def pass_on(w, ab, way):
        one_copy(w, ab, way).wait_recv()
        me, _ = places(True, w, ab)
        to = (me + (1, 3)[way]) % 4
        for j in range(2):
            add_in(parts[w], (ab, to, 2 * way + j), one_recv[w], (ab, way, j))
        two_copy(w, ab, way, 1).start()

    def second_ring(w, ab):
        for way in range(2):
            for late in range(2):
                two_copy(w, ab, way, late).wait_recv()
        me, _ = places(True, w, ab)
        for j in range(4):
            mid[w][ab, j] = (
                parts[w][ab, me, j].astype(F32)
                + two_recv[w][ab, 0, j].astype(F32)
                + two_recv[w][ab, 1, j].astype(F32)
            ).astype(BF16)
        for step in (2, 1, 3):
            last_copy(w, ab, step).start()

    def ring_sum(w, ab, half):
        me, _ = places(False, w, ab)
        total = mid[w][ab, me, half].astype(F32)
        for i in range(3):
            total = total + last_recv[w][ab, i, half].astype(F32)
        return total

    def ring_wait(w, ab):
        for step in range(1, 4):
            last_copy(w, ab, step).wait_recv()

    pair_copy(5).wait_recv()
    for k in range(4):
        pair_copy(k).wait_recv()
        if k < 3:
            fill(0, 0, target(0, 0, k))
            start_ring(0, 0, k)
    fill(0, 1, y_lo)
    start_ring(0, 1, 0)
    fill(0, 1, 1 - y_lo)
    start_ring(0, 1, 1)
    start_ring(0, 1, 2)
    fill(0, 0, target(0, 0, 3))

    for ab, way in both:
        pass_on(0, ab, way)
    wait_exchange(2, r["at_recv"])
    r["acc"][:, 0:HD] = r["at_recv"][...].astype(F32).reshape(N, HD)
    r["att"][...] = r["acc"][:, 0:HD].astype(BF16)
    r["turn"][0:HD, :] = r["acc"][:, 0:HD].T
    for ab in range(2):
        for c in range(2):
            pieces = []
            for hi in range(2):
                for zz in range(4 * ab, 4 * ab + 4):
                    first = zz * 72 + hi * 36 + c * 18
                    pieces.append(r["turn"][first : first + 18, :])
            r["att_t"][c, ab * 144 : ab * 144 + 144, :] = jnp.concatenate(pieces, 0).astype(BF16)
    pair_copy(6).start()
    pair_copy(4).wait_recv()
    pair_copy(6).wait_recv()
    for k in range(4):
        for ab in range(2):
            fill(1, ab, target(1, ab, k))
            start_ring(1, ab, k)
    for ab, way in both:
        pass_on(1, ab, way)

    for ab in range(2):
        second_ring(0, ab)
    for n in range(0, D, 384):
        o_out[:, n : n + 384] = (
            r["res"][:, n : n + 384].astype(F32) + dot(r["att"][...], r["wto"][:, n : n + 384])
        ).astype(BF16)

    wait_exchange(3, r["gh_recv"])

    def norm_back_residual(i, carry):
        rows = rows_of(i)
        g = r["gh_recv"][slabs_of(i)].astype(F32).reshape(CHUNK, D)
        inverse = r["t_inv"][rows, 0:1]
        n = (r["res"][rows, :].astype(F32) - r["t_mean"][rows, 0:1]) * inverse
        back = inverse * (g - mean_of(g) - n * mean_of(g * n))
        r["gres"][rows, :] = (r["cot"][rows, :].astype(F32) + back).astype(BF16)
        return carry

    lax.fori_loop(0, N // CHUNK, norm_back_residual, 0, unroll=2)
    r["small"][:, 0:HD] = dot_nt(r["gres"][...], r["wso"][...]).astype(BF16)
    for ab in range(2):
        second_ring(1, ab)
    backward_heads(r["sq"], r["sk"], r["sv"], r["sw"], r["small"], r["accq"], r["acck"], r["accv"])
    z_send = (r["z_send_in"], r["z_send_out"])
    z_recv = (r["z_recv_in"], r["z_recv_out"])

    lane6 = lax.broadcasted_iota(jnp.int32, (6, 128), 1) // 16

    def give_z(w):
        for ab in range(2):
            for j in range(4):
                if w == 0:
                    for half in range(2):
                        piece = [r["zsum"][ab, half, 36 * j : 36 * j + 36, :], jnp.zeros((4, 128), F32)]
                        z_send[0][4 * ab + j, half] = jnp.concatenate(piece, 0).astype(BF16)
                else:
                    low = 144 + 18 * j
                    tail = r["zsum"][ab, 1, low : low + 6, :]
                    for g in range(1, 3):
                        more = r["zsum"][ab, 1, low + 6 * g : low + 6 * g + 6, :]
                        tail = jnp.where(lane6 == g, pltpu.roll(more, 16 * g, 1), tail)
                    piece = [r["zsum"][ab, 0, low : low + 18, :], tail]
                    z_send[1][4 * ab + j] = jnp.concatenate(piece, 0).astype(BF16)

        def z_one(k, carry):
            to = lax.rem(z + 4 + (k + 1) // 2 * (1 - 2 * (k % 2)), 8)
            remote(
                "z",
                src_ref=z_send[w].at[to], dst_ref=z_recv[w].at[z],
                send_sem=r["z_ssem"].at[w], recv_sem=r["z_rsem"].at[w],
                device_id=at_seq(to * 4 + y_hi * 2 + core), device_id_type=MESH,
            ).start()
            return carry

        lax.fori_loop(0, 7, z_one, 0)
        z_recv[w][z] = z_send[w][z]

    for ab in range(2):
        ring_wait(0, ab)
        for half in range(2):
            r["zsum"][ab, half, 0:144] = ring_sum(0, ab, half)
    give_z(0)
    join(r["nat"], r["accq"], r["acck"], r["accv"])
    for n in range(0, D, 384):
        r["big"][:, n : n + 384] = dot(r["nat"][:, 0 : 3 * HD], r["wsi"][:, n : n + 384])

    for ab in range(2):
        ring_wait(1, ab)
        first, rest = ring_sum(1, ab, 0), ring_sum(1, ab, 1)
        r["zsum"][ab, 0, 144:192] = first
        r["zsum"][ab, 0, 192:216] = rest[0:24, :]
        for g in range(8):
            tail = rest[24:32, :]
            r["zsum"][ab, 1, 144 + 8 * g : 152 + 8 * g] = pltpu.roll(tail, 128 - 16 * g, 1) if g else tail
        r["zsum"][ab, 1, 208:216] = rest[32:40, :]
    give_z(1)

    def norm_back_video(i, carry):
        rows = rows_of(i)
        g = r["big"][rows, :]
        inverse = r["s_inv"][rows, 0:1]
        n = (r["vid"][rows, :].astype(F32) - r["s_mean"][rows, 0:1]) * inverse
        back = inverse * (g - mean_of(g) - n * mean_of(g * n))
        o_gv[rows, :] = (r["gres"][rows, :].astype(F32) + back).astype(BF16)
        return carry

    lax.fori_loop(0, N // CHUNK, norm_back_video, 0, unroll=2)

    drain("z", z_recv[0].at[pl.ds(0, 7)], r["z_rsem"].at[0])
    for half in range(2):
        total = z_recv[0][0, half].astype(F32)
        for j in range(1, 8):
            total = total + z_recv[0][j, half].astype(F32)
        o_gi[:, half * 128 : (128, 216)[half]] = total[0:36, 0 : (128, 88)[half]]
    drain("z", z_recv[1].at[pl.ds(0, 7)], r["z_rsem"].at[1])
    total = z_recv[1][0].astype(F32)
    for j in range(1, 8):
        total = total + z_recv[1][j].astype(F32)
    o_go[:, 0:128] = total[0:18, :]
    for g in range(3):
        o_go[6 * g : 6 * g + 6, 128:144] = total[18:24, 16 * g : 16 * g + 16]

    for which, name in enumerate(("ga_send", "h_send", "at_send", "gh_send")):
        wait_sent(which, r[name])
    for i in range(7):
        pair_copy(i).wait_send()
    for w in range(2):
        for ab in range(2):
            for way in range(2):
                one_copy(w, ab, way).wait_send()
                for late in range(2):
                    two_copy(w, ab, way, late).wait_send()
            for step in range(1, 4):
                last_copy(w, ab, step).wait_send()
    for w in range(2):
        drain("z", z_send[w].at[pl.ds(0, 7)], r["z_ssem"].at[w])


def hand_over(*refs):
    for source, result in zip(refs[:4], refs[4:]):
        result[...] = source[...]


def local(video, spatial_in, spatial_out, temporal_in, temporal_out, cotangent):
    shapes = scratch_shapes()
    names = tuple(shapes)
    anywhere = pl.BlockSpec(memory_space=pl.ANY)
    whole = pl.BlockSpec(memory_space=pltpu.VMEM)

    def body(*refs):
        kernel(*refs[:10], names, *refs[10:])

    results = (
        jax.ShapeDtypeStruct((N, D), BF16),
        jax.ShapeDtypeStruct((N, D), BF16),
        jax.ShapeDtypeStruct((36, 216), F32),
        jax.ShapeDtypeStruct((18, 144), F32),
    )
    held = pl.pallas_call(
        body,
        out_shape=results,
        in_specs=[anywhere] * 6,
        out_specs=(whole,) * 4,
        scratch_shapes=list(shapes.values()),
        compiler_params=pltpu.CompilerParams(
            collective_id=0, has_side_effects=True, vmem_limit_bytes=60 * 1024 * 1024
        ),
        cost_estimate=pl.CostEstimate(flops=9_000_000_000, bytes_accessed=13_000_000, transcendentals=1_100_000),
    )(video.reshape(N, D), spatial_in.T, spatial_out, temporal_in.T, temporal_out, cotangent.reshape(N, D))
    out, grad_video, grad_in, grad_out = pl.pallas_call(
        hand_over,
        out_shape=results,
        in_specs=[whole] * 4,
        out_specs=(whole,) * 4,
        cost_estimate=pl.CostEstimate(flops=0, bytes_accessed=2_400_000, transcendentals=0),
    )(*held)
    return (out.reshape(video.shape), grad_video.reshape(video.shape), grad_in, grad_out)


def solution(mesh):
    in_specs = (P("dp", "seq", None, None), P(), P(), P(), P(), P("dp", "seq", None, None))
    out_specs = (
        P("dp", "seq", None, None),
        P("dp", "seq", None, None),
        P("seq", "dp"),
        P("seq", "dp"),
    )
    return jax.shard_map(local, mesh=mesh, in_specs=in_specs, out_specs=out_specs, check_vma=False)
```
